32 devices in a mesh: dp: 8 (over y, x, core), mp: 4 (over z).
Axes of the slice: x: 2, y: 2, z: 4, core: 2. Of those that a mesh axis runs over, the one named last changes fastest.
Arguments:
- block_input: bfloat16 [2, 8, 256, 1536], P(None, 'dp', 'mp'), may hold values from -6 to 6
- out_grad: bfloat16 [2, 8, 256, 1536], P(None, 'dp', 'mp'), may hold values from -6 to 6
- doc_lengths: int32 [2, 8, 4], P(None, 'dp'), may hold values from 1 to 224, 256 in all within a row
- attn_gain: bfloat16 [1536], P('dp'), may hold values from 0.5 to 1.5
- qkv_weight: bfloat16 [3, 1536, 1536], P(None, 'dp', 'mp'), may hold values from -0.15625 to 0.15625
- conv_kernel: float32 [16, 6, 11], P('mp'), may hold values from -0.25 to 1.25
- head_mixing: float32 [8, 2, 2], P('mp'), may hold values from -0.5 to 1.5
- group_gain: bfloat16 [1536], P('mp'), may hold values from 0.25 to 1.75
- out_weight: bfloat16 [1536, 1536], P('mp', 'dp'), may hold values from -0.15625 to 0.15625
- mlp_gain: bfloat16 [1536], P('dp'), may hold values from 0.5 to 1.5
- gate_weight: bfloat16 [1536, 4096], P('dp', 'mp'), may hold values from -0.15625 to 0.15625
- up_weight: bfloat16 [1536, 4096], P('dp', 'mp'), may hold values from -0.15625 to 0.15625
- down_weight: bfloat16 [4096, 1536], P('mp', 'dp'), may hold values from -0.09375 to 0.09375
Outputs:
- block_output: bfloat16 [2, 8, 256, 1536], P(None, 'dp', 'mp')
- input_grad: float32 [2, 8, 256, 1536], P(None, 'dp', 'mp')
- attn_gain_grad: float32 [1536], P('dp')
- qkv_grad: float32 [3, 1536, 1536], P(None, 'dp', 'mp')
- kernel_grad: float32 [16, 6, 11], P('mp')
- mixing_grad: float32 [8, 2, 2], P('mp')
- group_gain_grad: float32 [1536], P('mp')
- out_weight_grad: float32 [1536, 1536], P('mp', 'dp')
- mlp_gain_grad: float32 [1536], P('dp')
- gate_grad: float32 [1536, 4096], P('dp', 'mp')
- up_grad: float32 [1536, 4096], P('dp', 'mp')
- down_grad: float32 [4096, 1536], P('mp', 'dp')
The draws below stay inside these ranges and needn't reach their ends.
Inputs may be any that keep to these rules, and one draw needn't show every extreme that they name: `doc_lengths`: each group's 4 lengths sum to 256; the longest is 224.
All inputs are finite; a program needn't handle non-finite values.
Results may differ from the reference program's by a relative error of at most 0.023.
Values may be sent and summed in bfloat16 or wider, within the bound.
No kernel may reach another device: no remote copies, remote signals or barrier semaphores. Data moves between devices by JAX's collectives and lax.ppermute only.
A program may use at most 192 MiB of HBM per device.

```python
import math
import jax
import jax.numpy as jnp
import numpy as np
from jax import lax

H = 16
HD = 96
FF = 4096
LEN = 256
MICRO = 2
NDOC = 4
CQ = 6
CK = 11
D = 1536
GROUPS = 8
LONGEST = 224


def draw_conv_kernel(key, part):
    key = jax.random.fold_in(key, 11)
    noise = jax.random.uniform(key, (H, CQ, CK), jnp.float32, -0.25, 0.25)
    first_query = lax.broadcasted_iota(jnp.int32, (H, CQ, CK), 1) == 0
    middle_key = lax.broadcasted_iota(jnp.int32, (H, CQ, CK), 2) == CK // 2
    return noise + (first_query & middle_key).astype(jnp.float32)


def draw_head_mixing(key, part):
    key = jax.random.fold_in(key, 23)
    noise = jax.random.uniform(key, (H // 2, 2, 2), jnp.float32, -0.5, 0.5)
    rows_index = lax.broadcasted_iota(jnp.int32, (H // 2, 2, 2), 1)
    cols_index = lax.broadcasted_iota(jnp.int32, (H // 2, 2, 2), 2)
    return noise + (rows_index == cols_index).astype(jnp.float32)


def levels(stream_key, dims, shards, low, top_value):
    level, own = 1.0, jax.random.fold_in(stream_key, 6)
    for dim, parts in shards:
        steps = jnp.exp(jax.random.uniform(jax.random.fold_in(own, dim), (parts,), jnp.float32, low / len(shards), top_value / len(shards)))
        level = level * jnp.repeat(steps, dims[dim] // parts).reshape([-1 if axis == dim else 1 for axis in range(len(dims))])
    return level


def profile(count, total, most, lean):
    weights = [(1 << 20) // math.isqrt(grade ** lean) + 1 for grade in range(2, count + 1)]
    spare, counts = total - most - (count - 1), [1] * (count - 1)
    while spare > 0:
        movable = [i for i in range(count - 1) if counts[i] < most]
        whole, left = sum([weights[i] for i in movable]), spare
        for i in movable:
            more = min(most - counts[i], max(1, left * weights[i] // whole), spare)
            counts[i] = counts[i] + more
            spare = spare - more
    return np.array([most] + counts)


def ragged_sizes(stream_key, number_of, total, limit, lean):
    if number_of == 2:
        one = jax.random.randint(stream_key, (), max(1, total - limit), min(limit, total - 1) + 1)
        return jnp.stack([one, total - one])
    sizes = jnp.asarray(profile(number_of, total, limit, lean), jnp.int32)
    couples = (number_of - 1) // 2
    source_of, sink = sizes[1:1 + 2 * couples:2], sizes[2:2 + 2 * couples:2]
    slack = jnp.minimum(source_of - 1, limit - sink)
    moved = jax.random.randint(jax.random.fold_in(stream_key, 1), (couples,), 0, 1 << 20) % (slack + 1)
    sizes = sizes.at[1:1 + 2 * couples:2].set(source_of - moved).at[2:2 + 2 * couples:2].set(sink + moved)
    return sizes[jax.random.permutation(jax.random.fold_in(stream_key, 2), number_of)]


def bell_draw(own_key, dims, width, limit, pieces=(), kind=jnp.bfloat16):
    level = levels(own_key, dims, pieces, -0.22, 0.18) if pieces else 1.0
    values = jax.random.normal(own_key, dims, jnp.float32) * width * level
    return jnp.minimum(jnp.maximum(values, -limit), limit).astype(kind)


def setup_inputs(seed: int = 0) -> dict:
    key_list = jax.random.split(jax.random.key(seed), 14)
    return {
        "block_input": bell_draw(key_list[0], (MICRO, GROUPS, LEN, D), 1.0, 6.0, ((1, 8), (2, 4))),
        "out_grad": bell_draw(key_list[1], (MICRO, GROUPS, LEN, D), 1.0, 6.0, ((1, 8), (2, 4))),
        "doc_lengths": jax.vmap(lambda own: ragged_sizes(own, NDOC, LEN, LONGEST, 1))(jax.random.split(key_list[2], MICRO * GROUPS)).reshape((MICRO, GROUPS, NDOC)).astype(jnp.int32),
        "attn_gain": jnp.clip(1.0 + 0.1 * jax.random.normal(key_list[3], (D,), jnp.float32), 0.5, 1.5).astype(jnp.bfloat16),
        "qkv_weight": bell_draw(key_list[4], (3, D, D), D ** -0.5, 0.15625, ((1, 8), (2, 4))),
        "conv_kernel": draw_conv_kernel(jax.random.fold_in(key_list[13], 71), 0),
        "head_mixing": draw_head_mixing(jax.random.fold_in(key_list[13], 71), 0),
        "group_gain": jnp.clip(1.0 + 0.15 * jax.random.normal(key_list[7], (D,), jnp.float32), 0.25, 1.75).astype(jnp.bfloat16),
        "out_weight": bell_draw(key_list[8], (D, D), D ** -0.5, 0.15625, ((0, 4), (1, 8))),
        "mlp_gain": jnp.clip(1.0 + 0.1 * jax.random.normal(key_list[9], (D,), jnp.float32), 0.5, 1.5).astype(jnp.bfloat16),
        "gate_weight": bell_draw(key_list[10], (D, FF), D ** -0.5, 0.15625, ((0, 8), (1, 4))),
        "up_weight": bell_draw(key_list[11], (D, FF), D ** -0.5, 0.15625, ((0, 8), (1, 4))),
        "down_weight": bell_draw(key_list[12], (FF, D), FF ** -0.5, 0.09375, ((0, 4), (1, 8))),
    }


@jax.custom_vjp
def low(v):
    return lax.optimization_barrier(v.astype(jnp.bfloat16)).astype(jnp.float32)

@jax.custom_vjp
def low_back(v):
    return v

def low_keep(v):
    return (low(v), None)

def low_pass(kept, grad):
    return (grad,)

def back_keep(v):
    return (v, None)

def back_low(kept, grad):
    return (low(grad),)
low.defvjp(low_keep, low_pass)
low_back.defvjp(back_keep, back_low)
EPS = 1e-05

def segment_ids(lengths, length):
    ends = jnp.cumsum(lengths.astype(jnp.int32)).astype(jnp.int32)
    places = jnp.arange(length, dtype=jnp.int32)
    return lax.optimization_barrier(jnp.sum((places[:, None] >= ends[None, :]).astype(jnp.int32), axis=1)).astype(jnp.int32)

def allowed(segment):
    places = jnp.arange(segment.shape[0], dtype=jnp.int32)
    return (places[None, :] <= places[:, None]) & (segment[None, :] == segment[:, None])

def key_query_conv(zeroed, kernel, segment):
    length = zeroed.shape[1]
    center = CK // 2
    padded = jnp.pad(zeroed, ((0, 0), (CQ - 1, 0), (center, CK - 1 - center)))
    seg_pad = jnp.pad(segment, (CQ - 1, 0), constant_values=-1)
    summed = jnp.zeros_like(zeroed)
    for query_shift in range(CQ):
        earlier_rows = padded[:, CQ - 1 - query_shift:CQ - 1 - query_shift + length, :]
        same_doc = (seg_pad[CQ - 1 - query_shift:CQ - 1 - query_shift + length] == segment).astype(zeroed.dtype)
        partial_sum = jnp.zeros_like(zeroed)
        for key_shift in range(CK):
            partial_sum = partial_sum + kernel[:, query_shift, key_shift][:, None, None] * earlier_rows[:, :, CK - 1 - key_shift:CK - 1 - key_shift + length]
        summed = summed + same_doc[None, :, None] * partial_sum
    return summed

def rms_scale(values, gain):
    return values * lax.rsqrt(lax.optimization_barrier(jnp.mean(values * values, axis=-1, keepdims=True)) + EPS) * gain

def matmul(left, right):
    return jnp.dot(left, right, precision=lax.Precision.HIGHEST, preferred_element_type=jnp.float32)

def layer(params, tokens_in, segment):
    attn_gain, qkv_weight, conv_kernel, head_mixing, group_gain, out_weight, mlp_gain, gate_weight, up_weight, down_weight = params
    length = tokens_in.shape[0]
    normed_in = low(rms_scale(tokens_in, attn_gain))
    query = low_back(low(matmul(normed_in, qkv_weight[0])))
    keys = low_back(low(matmul(normed_in, qkv_weight[1])))
    values = low_back(low(matmul(normed_in, qkv_weight[2])))

    def split_heads(flat):
        return flat.reshape(length, H, HD).transpose(1, 0, 2)
    scores = jnp.einsum('hid,hjd->hij', split_heads(query), split_heads(keys), precision=lax.Precision.HIGHEST) / math.sqrt(HD)
    scores = low_back(scores)
    mask = allowed(segment)
    zeroed = jnp.where(mask[None], scores, 0.0)
    logits = key_query_conv(zeroed, conv_kernel, segment)
    masked = jnp.where(mask[None], logits, -jnp.inf)
    top = lax.optimization_barrier(jnp.max(masked, axis=-1, keepdims=True))
    expo = jnp.exp(masked - top)
    probs = expo / lax.optimization_barrier(jnp.sum(expo, axis=-1, keepdims=True))
    paired = probs.reshape(H // 2, 2, length, length)
    mixed = lax.optimization_barrier(jnp.sum(head_mixing[:, :, :, None, None] * paired[:, None, :, :, :], axis=2))
    mixed = low(mixed.reshape(H, length, length))
    heads_out = low_back(jnp.einsum('hij,hjd->hid', mixed, split_heads(values), precision=lax.Precision.HIGHEST))
    centered = heads_out - lax.optimization_barrier(jnp.mean(heads_out, axis=-1, keepdims=True))
    normed_heads = centered * lax.rsqrt(lax.optimization_barrier(jnp.mean(centered * centered, axis=-1, keepdims=True)) + EPS)
    grouped = low(normed_heads.transpose(1, 0, 2).reshape(length, D) * group_gain)
    attended = low_back(matmul(grouped, out_weight))
    hidden_in = tokens_in + attended
    normed_mid = low(rms_scale(hidden_in, mlp_gain))
    gate = low_back(matmul(normed_mid, gate_weight))
    upward = low_back(matmul(normed_mid, up_weight))
    hidden = low(jax.nn.silu(gate) * upward)
    return hidden_in + matmul(hidden, down_weight)

def reference(block_input, out_grad, doc_lengths, attn_gain, qkv_weight, conv_kernel, head_mixing, group_gain, out_weight, mlp_gain, gate_weight, up_weight, down_weight):
    params = tuple((array.astype(jnp.float32) for array in (attn_gain, qkv_weight, conv_kernel, head_mixing, group_gain, out_weight, mlp_gain, gate_weight, up_weight, down_weight)))
    flat_in = block_input.reshape(MICRO * GROUPS, LEN, D).astype(jnp.float32)
    flat_grad = out_grad.reshape(MICRO * GROUPS, LEN, D).astype(jnp.float32)
    flat_lengths = doc_lengths.reshape(MICRO * GROUPS, NDOC).astype(jnp.int32)
    zero_grads = tuple((jnp.zeros_like(array) for array in params))

    def one_group(carry, inputs):
        tokens_in, grad_out, lengths = inputs
        segment = segment_ids(lengths, LEN)
        output, pullback = jax.vjp(lambda weights, acts: layer(weights, acts, segment), params, tokens_in)
        weight_grads, input_grad = pullback(grad_out)
        carry = tuple((first + second for first, second in zip(carry, weight_grads)))
        return (carry, (output.astype(jnp.bfloat16), input_grad))
    grads, (outputs, input_grads) = lax.scan(one_group, zero_grads, (flat_in, flat_grad, flat_lengths))
    block_output = outputs.reshape(MICRO, GROUPS, LEN, D)
    input_grad = input_grads.reshape(MICRO, GROUPS, LEN, D)
    return (block_output, input_grad, grads[0], grads[1], grads[2], grads[3], grads[4], grads[5], grads[6], grads[7], grads[8], grads[9])
```

```python
import functools
import math

import jax
import jax.numpy as jnp
from jax import lax
from jax.experimental import pallas as pl
from jax.experimental.pallas import tpu as pltpu
from jax.sharding import PartitionSpec as P

CQ = 6
CK = 11
CENTER = CK // 2
EPS = 1e-05
F32 = jnp.float32
BF16 = jnp.bfloat16
VMEM_LIMIT = 58 * 1024 * 1024

NN = (((1,), (0,)), ((), ()))
NT = (((1,), (1,)), ((), ()))
TN = (((0,), (0,)), ((), ()))


def mm(left, right, dims=NN):
    return lax.dot_general(left, right, dims, preferred_element_type=F32)


def spec_vmem():
    return pl.BlockSpec(memory_space=pltpu.VMEM)


def spec_smem():
    return pl.BlockSpec(memory_space=pltpu.SMEM)


def call(body, outs, ins, scratch=(), smem=0, flops=0, name=None):
    nbytes = sum(math.prod(a.shape) * a.dtype.itemsize for a in list(ins) + list(outs))
    return pl.pallas_call(
        body,
        out_shape=outs,
        in_specs=[spec_smem()] * smem + [spec_vmem()] * (len(ins) - smem),
        out_specs=[spec_vmem()] * len(outs),
        scratch_shapes=list(scratch),
        compiler_params=pltpu.CompilerParams(vmem_limit_bytes=VMEM_LIMIT),
        cost_estimate=pl.CostEstimate(flops=flops, bytes_accessed=nbytes, transcendentals=0),
        name=name,
    )(*ins)


def sds(shape, dtype):
    return jax.ShapeDtypeStruct(shape, dtype)


def segment_ids(lengths, length):
    ends = jnp.cumsum(lengths)
    places = jnp.arange(length, dtype=jnp.int32)
    return jnp.sum((places[:, None] >= ends[None, :]).astype(jnp.int32), axis=1)


def place(me, step, parts, rows):
    return pl.multiple_of(lax.rem(me - step + parts, parts) * rows, rows)


def masks(seg_col, seg_row, length):
    same = seg_col == seg_row
    row = lax.broadcasted_iota(jnp.int32, (length, length), 0)
    col = lax.broadcasted_iota(jnp.int32, (length, length), 1)
    return same, same & (col <= row)


def shift_rows(values, shift, same):
    if shift == 0:
        return values.astype(BF16)
    length = values.shape[0]
    return jnp.where(same, pltpu.roll(values, shift % length, 0), 0.0).astype(BF16)


def head_norm(heads_out):
    centered = heads_out - jnp.mean(heads_out, axis=-1, keepdims=True)
    inv_std = lax.rsqrt(jnp.mean(centered * centered, axis=-1, keepdims=True) + EPS)
    return centered * inv_std, inv_std


def attn_fwd_body(cfg, me_ref, mix_ref, *refs):
    parts, rows, heads, size = cfg
    x_refs = refs[:parts]
    w_ref, band_ref, segc_ref, segr_ref, ggain_ref = refs[parts : parts + 5]
    outs = refs[parts + 5 :]
    att_refs = outs[:parts]
    normed_ref, qkv_ref, z_ref, p_ref, ho_ref, grouped_ref, gains_ref, att_scr = outs[parts:]
    length = parts * rows
    width = heads * size
    me = me_ref[0]
    gains = w_ref[:, 4 * width :].astype(F32).T
    gains_ref[...] = gains[:8]
    gain = gains[0:1]
    for step in range(parts):
        x = x_refs[step][...].astype(F32)
        r1 = lax.rsqrt(jnp.mean(x * x, axis=-1, keepdims=True) + EPS)
        normed_ref[pl.ds(place(me, step, parts, rows), rows), :] = (x * r1 * gain).astype(BF16)
    qkv_ref[...] = mm(normed_ref[...], w_ref[:, : 3 * width]).astype(BF16)
    same, allow = masks(segc_ref[...], segr_ref[...], length)
    scale = 1.0 / math.sqrt(size)
    for pair in range(heads // 2):
        probs = []
        for b in range(2):
            h = 2 * pair + b
            q = qkv_ref[:, h * size : (h + 1) * size]
            k = qkv_ref[:, width + h * size : width + (h + 1) * size]
            z = jnp.where(allow, mm(q, k, NT) * scale, 0.0)
            z_ref[h] = z.astype(BF16)
            acc = jnp.zeros((length, length), F32)
            for a in range(CQ):
                acc = acc + mm(shift_rows(z, a, same), band_ref[h * CQ + a])
            logits = jnp.where(allow, acc, -jnp.inf)
            e = jnp.exp(logits - jnp.max(logits, axis=-1, keepdims=True))
            p = e * (1.0 / jnp.sum(e, axis=-1, keepdims=True))
            p_ref[h] = p
            probs.append(p)
        for a in range(2):
            h = 2 * pair + a
            mixed = (
                mix_ref[4 * pair + 2 * a] * probs[0] + mix_ref[4 * pair + 2 * a + 1] * probs[1]
            ).astype(BF16)
            v = qkv_ref[:, 2 * width + h * size : 2 * width + (h + 1) * size]
            ho = mm(mixed, v)
            ho_ref[h] = ho
            normed, _ = head_norm(ho)
            grouped_ref[:, h * size : (h + 1) * size] = (
                normed * ggain_ref[:, h * size : (h + 1) * size]
            ).astype(BF16)
    att_scr[...] = mm(grouped_ref[...], w_ref[:, 3 * width : 4 * width], NT)
    for step in range(parts):
        att_refs[step][...] = att_scr[pl.ds(place(me, step, parts, rows), rows), :].astype(BF16)


def attn_fwd(me, mix, xs, w1, band, segc, segr, ggain, heads, size):
    parts = len(xs)
    rows, d = xs[0].shape
    length, width = parts * rows, heads * size
    outs = (
        [sds((rows, d), BF16)] * parts
        + [
            sds((length, d), BF16),
            sds((length, 3 * width), BF16),
            sds((heads, length, length), BF16),
            sds((heads, length, length), F32),
            sds((heads, length, size), F32),
            sds((length, width), BF16),
            sds((8, d), F32),
        ]
    )
    res = call(
        functools.partial(attn_fwd_body, (parts, rows, heads, size)),
        outs,
        [me, mix, *xs, w1, band, segc, segr, ggain],
        scratch=[pltpu.VMEM((length, d), F32)],
        smem=2,
        flops=2 * length * d * width * 4 + 2 * heads * (CQ + 2) * length**3,
        name="attn_fwd",
    )
    return res[:parts], res[parts:]


def tail_rms(values, gain):
    r = lax.rsqrt(jnp.mean(values * values, axis=-1, keepdims=True) + EPS)
    return values * r, r


def rms_back(grad, normal, r, gain):
    u = grad * gain
    return r * (u - normal * jnp.mean(u * normal, axis=-1, keepdims=True))


def total(refs):
    acc = refs[0][...].astype(F32)
    for ref in refs[1:]:
        acc = acc + ref[...].astype(F32)
    return acc


def mid_body(parts, *refs):
    x_ref, gains_ref = refs[:2]
    hid_ref, mid_ref = refs[2 + parts :]
    hidden_in = x_ref[...].astype(F32) + total(refs[2 : 2 + parts])
    hid_ref[...] = hidden_in
    normal, _ = tail_rms(hidden_in, None)
    mid_ref[...] = (normal * gains_ref[1:2]).astype(BF16)


def mid_step(x, gains, pieces):
    return call(
        functools.partial(mid_body, len(pieces)),
        [sds(x.shape, F32), sds(x.shape, BF16)],
        [x, gains, *pieces],
        name="mid_step",
    )


def mid_back_body(parts, *refs):
    hid_ref, dy_ref, gains_ref = refs[:3]
    ghid_ref, ga_ref, gain_ref = refs[3 + parts :]
    gain = gains_ref[1:2]
    normal, r = tail_rms(hid_ref[...], None)
    grad = total(refs[3 : 3 + parts])
    gain_ref[...] = jnp.sum(grad * normal, axis=0, keepdims=True)
    ghid = dy_ref[...].astype(F32) + rms_back(grad, normal, r, gain)
    ghid_ref[...] = ghid
    ga_ref[...] = ghid.astype(BF16)


def mid_back(hid, dy, gains, pieces):
    return call(
        functools.partial(mid_back_body, len(pieces)),
        [sds(hid.shape, F32), sds(hid.shape, BF16), sds((1, hid.shape[1]), F32)],
        [hid, dy, gains, *pieces],
        name="mid_back",
    )


def last_body(parts, *refs):
    x_ref, ghid_ref, gains_ref = refs[:3]
    out_ref = refs[3 + parts]
    normal, r = tail_rms(x_ref[...].astype(F32), None)
    grad = total(refs[3 : 3 + parts])
    out_ref[...] = ghid_ref[...] + rms_back(grad, normal, r, gains_ref[0:1])


def last_step(x, ghid, gains, pieces):
    return call(
        functools.partial(last_body, len(pieces)),
        [sds(x.shape, F32)],
        [x, ghid, gains, *pieces],
        name="last_step",
    )[0]


def ffn_body(parts, rows, *refs):
    m_refs, dy_refs = refs[:parts], refs[parts : 2 * parts]
    wg_ref, wu_ref, wd_ref = refs[2 * parts : 2 * parts + 3]
    rest = refs[2 * parts + 3 :]
    o_refs, g_refs = rest[:parts], rest[parts : 2 * parts]
    mid_ref, dya_ref, hid_ref, gg_ref, gu_ref, out_acc, gmid_acc = rest[2 * parts :]
    j = pl.program_id(0)

    @pl.when(j == 0)
    def _():
        for step in range(parts):
            mid_ref[step * rows : (step + 1) * rows, :] = m_refs[step][...]
            dya_ref[step * rows : (step + 1) * rows, :] = dy_refs[step][...]
        out_acc[...] = jnp.zeros_like(out_acc)
        gmid_acc[...] = jnp.zeros_like(gmid_acc)

    mid = mid_ref[...]
    gate = mm(mid, wg_ref[...])
    up = mm(mid, wu_ref[...])
    gh = mm(dya_ref[...], wd_ref[...])
    sig = jax.nn.sigmoid(gate)
    swish = gate * sig
    hidden = (swish * up).astype(BF16)
    hid_ref[...] = hidden
    gg = (gh * up * sig * (1.0 + gate * (1.0 - sig))).astype(BF16)
    gu = (gh * swish).astype(BF16)
    gg_ref[...] = gg
    gu_ref[...] = gu
    gmid_acc[...] += mm(gg, wg_ref[...], NT) + mm(gu, wu_ref[...], NT)
    out_acc[...] += mm(hidden, wd_ref[...], NT)

    @pl.when(j == pl.num_programs(0) - 1)
    def _():
        for step in range(parts):
            o_refs[step][...] = out_acc[step * rows : (step + 1) * rows, :].astype(BF16)
            g_refs[step][...] = gmid_acc[step * rows : (step + 1) * rows, :].astype(BF16)


def ffn(ms, dys, w2):
    parts = len(ms)
    rows, d = ms[0].shape
    length = parts * rows
    ff = w2.shape[1] // 3
    cols = min(256, ff)
    steps = ff // cols
    whole = lambda shape: pl.BlockSpec(shape, lambda j: (0, 0))
    weight = lambda c: pl.BlockSpec((d, cols), lambda j, c=c: (0, c * steps + j))
    chunk = pl.BlockSpec((length, cols), lambda j: (0, j))
    outs = (
        [sds((rows, d), BF16)] * (2 * parts)
        + [sds((length, d), BF16)] * 2
        + [sds((length, ff), BF16)] * 3
    )
    res = pl.pallas_call(
        functools.partial(ffn_body, parts, rows),
        grid=(steps,),
        in_specs=[whole((rows, d))] * (2 * parts) + [weight(0), weight(1), weight(2)],
        out_specs=[whole((rows, d))] * (2 * parts) + [whole((length, d))] * 2 + [chunk] * 3,
        out_shape=outs,
        scratch_shapes=[pltpu.VMEM((length, d), F32)] * 2,
        compiler_params=pltpu.CompilerParams(vmem_limit_bytes=VMEM_LIMIT),
        cost_estimate=pl.CostEstimate(
            flops=2 * length * d * ff * 6, bytes_accessed=6 * d * ff, transcendentals=0
        ),
        name="ffn",
    )(*ms, *dys, w2, w2, w2)
    return res[:parts], res[parts : 2 * parts], res[2 * parts :]


def band_sum(values, length):
    lane = lax.broadcasted_iota(jnp.int32, (8, 128), 1)
    lane = jnp.where(lane >= 64, lane - 128, lane)
    acc = jnp.zeros((8, 128), F32)
    tiles = length // 128
    for s in range(length // 8):
        back = (128 - 8 * s % 128) % 128
        low, high = 8 * s - CENTER, 8 * s + 7 + CENTER
        first, last = max(low, 0) // 128, min(high, length - 1) // 128
        for tile in range(first, last + 1):
            piece = values[8 * s : 8 * s + 8, tile * 128 : (tile + 1) * 128]
            if back:
                piece = pltpu.roll(piece, back, 1)
            start, stop = tile * 128 - 8 * s, tile * 128 + 128 - 8 * s
            if low < tile * 128 or high >= tile * 128 + 128:
                piece = jnp.where((lane >= start) & (lane < stop), piece, 0.0)
            acc = acc + piece
    return acc


def attn_bwd_body(cfg, me_ref, mix_ref, *refs):
    parts, rows, heads, size = cfg
    ga_refs = refs[:parts]
    (w_ref, band_ref, segc_ref, segr_ref, ggain_ref, gains_ref, normed_ref, qkv_ref, z_ref,
     p_ref, ho_ref) = refs[parts : parts + 11]
    outs = refs[parts + 11 :]
    gi_refs = outs[:parts]
    (gaa_ref, gproj_ref, again_ref, ggrad_ref, kern_ref, mixg_ref, gin_scr, diag_scr) = outs[parts:]
    length = parts * rows
    width = heads * size
    me = me_ref[0]
    for step in range(parts):
        gaa_ref[pl.ds(place(me, step, parts, rows), rows), :] = ga_refs[step][...]
    gin_scr[:, :width] = mm(gaa_ref[...], w_ref[:, 3 * width : 4 * width])
    same, allow = masks(segc_ref[...], segr_ref[...], length)
    scale = 1.0 / math.sqrt(size)
    for pair in range(heads // 2):
        gmix = []
        for a in range(2):
            h = 2 * pair + a
            lanes = slice(h * size, (h + 1) * size)
            gg = gin_scr[:, lanes]
            normed, inv_std = head_norm(ho_ref[h])
            ggrad_ref[:, lanes] = jnp.sum(gg * normed, axis=0, keepdims=True)
            u = gg * ggain_ref[:, lanes]
            gh = inv_std * (
                u
                - jnp.mean(u, axis=-1, keepdims=True)
                - normed * jnp.mean(u * normed, axis=-1, keepdims=True)
            )
            gh = gh.astype(BF16)
            v = qkv_ref[:, 2 * width + h * size : 2 * width + (h + 1) * size]
            gmix.append(mm(gh, v, NT))
            mixed = (
                mix_ref[4 * pair + 2 * a] * p_ref[2 * pair]
                + mix_ref[4 * pair + 2 * a + 1] * p_ref[2 * pair + 1]
            ).astype(BF16)
            gproj_ref[:, 2 * width + h * size : 2 * width + (h + 1) * size] = mm(
                mixed, gh, TN
            ).astype(BF16)
        for b in range(2):
            h = 2 * pair + b
            p = p_ref[h]
            for a in range(2):
                mixg_ref[4 * pair + 2 * a + b : 4 * pair + 2 * a + b + 1, :] = jnp.sum(
                    gmix[a] * p, axis=0, keepdims=True
                )
            gp = mix_ref[4 * pair + b] * gmix[0] + mix_ref[4 * pair + 2 + b] * gmix[1]
            gl = p * (gp - jnp.sum(gp * p, axis=-1, keepdims=True))
            glt = gl.T.astype(BF16)
            z = z_ref[h].astype(F32)
            gz = jnp.zeros((length, length), F32)
            for a in range(CQ):
                gz = gz + mm(shift_rows(gl, -a, same), band_ref[h * CQ + a], NT)
                diag_scr[h * CQ + a] = band_sum(mm(glt, shift_rows(z, a, same)), length)
            gs = jnp.where(allow, gz, 0.0).astype(BF16)
            q = qkv_ref[:, h * size : (h + 1) * size]
            k = qkv_ref[:, width + h * size : width + (h + 1) * size]
            gproj_ref[:, h * size : (h + 1) * size] = (mm(gs, k) * scale).astype(BF16)
            gproj_ref[:, width + h * size : width + (h + 1) * size] = (
                mm(gs, q, TN) * scale
            ).astype(BF16)
    taps = diag_scr[:, 0, :]
    for r in range(1, 8):
        taps = taps + pltpu.roll(diag_scr[:, r, :], 128 - r, 1)
    kern_ref[...] = taps
    gin_scr[...] = mm(gproj_ref[...], w_ref[:, : 3 * width], NT)
    again_ref[...] = (
        jnp.sum(gin_scr[...] * normed_ref[...].astype(F32), axis=0, keepdims=True) / gains_ref[0:1]
    )
    for step in range(parts):
        gi_refs[step][...] = gin_scr[pl.ds(place(me, step, parts, rows), rows), :].astype(BF16)


def attn_bwd(me, mix, gas, w1, band, segc, segr, ggain, gains, saved, heads, size):
    parts = len(gas)
    rows, d = gas[0].shape
    length, width = parts * rows, heads * size
    outs = (
        [sds((rows, d), BF16)] * parts
        + [
            sds((length, d), BF16),
            sds((length, 3 * width), BF16),
            sds((1, d), F32),
            sds((1, width), F32),
            sds((heads * CQ, 128), F32),
            sds((2 * heads, length), F32),
        ]
    )
    res = call(
        functools.partial(attn_bwd_body, (parts, rows, heads, size)),
        outs,
        [me, mix, *gas, w1, band, segc, segr, ggain, gains, *saved],
        scratch=[pltpu.VMEM((length, d), F32), pltpu.VMEM((heads * CQ, 8, 128), F32)],
        smem=2,
        flops=2 * length * d * width * 4 + 2 * heads * (2 * CQ + 4) * length**3,
        name="attn_bwd",
    )
    return res[:parts], res[parts:]


def gather_mp(part, size):
    return [part] + [
        lax.ppermute(part, "mp", [(i, (i + step) % size) for i in range(size)])
        for step in range(1, size)
    ]


def scatter_mp(pieces, size):
    return [pieces[0]] + [
        lax.ppermute(pieces[step], "mp", [(i, (i - step) % size) for i in range(size)])
        for step in range(1, size)
    ]


def sum_all(values, axis, size):
    bit = 1
    while bit < size:
        values = values + lax.ppermute(values, axis, [(i, i ^ bit) for i in range(size)])
        bit *= 2
    return values


def shards(
    block_input,
    out_grad,
    doc_lengths,
    attn_gain,
    qkv_weight,
    conv_kernel,
    head_mixing,
    group_gain,
    out_weight,
    mlp_gain,
    gate_weight,
    up_weight,
    down_weight,
):
    batches = block_input.shape[0]
    rows = block_input.shape[2]
    mp, dp = lax.axis_size("mp"), lax.axis_size("dp")
    length = rows * mp
    heads = conv_kernel.shape[0]
    width = qkv_weight.shape[2]
    size = width // heads
    local_d = attn_gain.shape[0]
    me = lax.axis_index("mp").astype(jnp.int32).reshape(1)
    mix = head_mixing.reshape(-1)
    ggain = group_gain.astype(F32)[None]

    gains_cols = jnp.pad(jnp.stack([attn_gain, mlp_gain], axis=1), ((0, 0), (0, 126)))
    pack1 = jnp.concatenate(
        [qkv_weight[0], qkv_weight[1], qkv_weight[2], out_weight.T, gains_cols], axis=1
    )
    pack2 = jnp.concatenate([gate_weight, up_weight, down_weight.T], axis=1)
    w1 = lax.all_gather(pack1, "dp", axis=0, tiled=True)
    w2 = lax.all_gather(pack2, "dp", axis=0, tiled=True)

    offset = (
        jnp.arange(length, dtype=jnp.int32)[None, :]
        - jnp.arange(length, dtype=jnp.int32)[:, None]
        + CENTER
    )
    band = jnp.zeros((heads * CQ, length, length), F32)
    taps = conv_kernel.reshape(heads * CQ, CK)
    for b in range(CK):
        band = jnp.where(offset[None] == b, taps[:, b][:, None, None], band)
    band = band.astype(BF16)

    outputs, input_grads, kept = [], [], []
    head_total = None
    for batch in range(batches):
        segment = segment_ids(doc_lengths[batch, 0], length)
        segc, segr = segment[:, None], segment[None, :]
        x, dy = block_input[batch, 0], out_grad[batch, 0]
        xs = gather_mp(x, mp)
        dys = gather_mp(dy, mp)
        pieces, saved = attn_fwd(me, mix, xs, w1, band, segc, segr, ggain, heads, size)
        normed, qkv, z, probs, ho, grouped, gains = saved
        hid, mid = mid_step(x, gains, scatter_mp(pieces, mp))
        mids = gather_mp(mid, mp)
        o_pieces, g_pieces, (mid_all, dy_all, hidden, gg, gu) = ffn(mids, dys, w2)
        ghid, ga, mlp_part = mid_back(hid, dy, gains, scatter_mp(g_pieces, mp))
        out = hid
        for piece in scatter_mp(o_pieces, mp):
            out = out + piece.astype(F32)
        outputs.append(out.astype(BF16))
        gas = gather_mp(ga, mp)
        gi_pieces, (ga_all, gproj, again, ggrad, kern, mixg) = attn_bwd(
            me, mix, gas, w1, band, segc, segr, ggain, gains, [normed, qkv, z, probs, ho], heads, size
        )
        input_grads.append(last_step(x, ghid, gains, scatter_mp(gi_pieces, mp)))
        small = (again, mlp_part, ggrad, kern, jnp.sum(mixg, axis=1))
        head_total = small if head_total is None else jax.tree.map(jnp.add, head_total, small)
        kept.append((mid_all, dy_all, hidden, gg, gu, normed, gproj, grouped, ga_all))

    mid_all, dy_all, hidden, gg, gu, normed, gproj, grouped, ga_all = (
        jnp.concatenate(group, axis=0) for group in zip(*kept)
    )
    grads2 = jnp.concatenate(
        [mm(mid_all, gg, TN), mm(mid_all, gu, TN), mm(dy_all, hidden, TN)], axis=1
    ).astype(BF16)
    share2 = lax.psum_scatter(grads2, "dp", scatter_dimension=0, tiled=True).astype(F32)
    grads1 = jnp.concatenate([mm(normed, gproj, TN), mm(ga_all, grouped, TN)], axis=1).astype(BF16)
    share1 = lax.psum_scatter(grads1, "dp", scatter_dimension=0, tiled=True).astype(F32)

    again, mlp_part, ggrad, kern, mixg = head_total
    d = again.shape[1]
    flat = jnp.concatenate([again[0], mlp_part[0], ggrad[0], kern.reshape(-1), mixg])
    count = flat.shape[0]
    flat = jnp.pad(flat, (0, -count % 128)).reshape(-1, 128)
    flat = sum_all(flat, "dp", dp).reshape(-1)
    gain_grads = sum_all(flat[: 2 * d].reshape(-1, 128), "mp", mp).reshape(2, dp, local_d)
    gain_grads = lax.dynamic_index_in_dim(gain_grads, lax.axis_index("dp"), 1, keepdims=False)
    ggrad = flat[2 * d : 2 * d + width]
    kern = flat[2 * d + width : 2 * d + width + heads * CQ * 128].reshape(heads, CQ, 128)
    kernel_grad = jnp.roll(kern, CK - 1 - CENTER, axis=2)[:, :, :CK][:, :, ::-1]
    mixing_grad = flat[2 * d + width + heads * CQ * 128 : count].reshape(heads // 2, 2, 2)
    ff = gate_weight.shape[1]
    return (
        jnp.stack(outputs)[:, None],
        jnp.stack(input_grads)[:, None],
        gain_grads[0],
        jnp.stack([share1[:, c * width : (c + 1) * width] for c in range(3)]),
        kernel_grad,
        mixing_grad,
        ggrad,
        share1[:, 3 * width :].T,
        gain_grads[1],
        share2[:, :ff],
        share2[:, ff : 2 * ff],
        share2[:, 2 * ff :].T,
    )


def solution(mesh):
    return jax.shard_map(
        shards,
        mesh=mesh,
        in_specs=(
            P(None, "dp", "mp", None),
            P(None, "dp", "mp", None),
            P(None, "dp", None),
            P("dp"),
            P(None, "dp", "mp"),
            P("mp", None, None),
            P("mp", None, None),
            P("mp"),
            P("mp", "dp"),
            P("dp"),
            P("dp", "mp"),
            P("dp", "mp"),
            P("mp", "dp"),
        ),
        out_specs=(
            P(None, "dp", "mp", None),
            P(None, "dp", "mp", None),
            P("dp"),
            P(None, "dp", "mp"),
            P("mp", None, None),
            P("mp", None, None),
            P("mp"),
            P("mp", "dp"),
            P("dp"),
            P("dp", "mp"),
            P("dp", "mp"),
            P("mp", "dp"),
        ),
        check_vma=False,
    )
```

```python
import functools
import math

import jax
import jax.numpy as jnp
from jax import lax
from jax.experimental import pallas as pl
from jax.experimental.pallas import tpu as pltpu
from jax.sharding import PartitionSpec as P

CQ = 6
CK = 11
CENTER = CK // 2
EPS = 1e-05
F32 = jnp.float32
BF16 = jnp.bfloat16
VMEM_LIMIT = 58 * 1024 * 1024

NN = (((1,), (0,)), ((), ()))
NT = (((1,), (1,)), ((), ()))
TN = (((0,), (0,)), ((), ()))


def mm(left, right, dims=NN):
    return lax.dot_general(left, right, dims, preferred_element_type=F32)


def spec_vmem():
    return pl.BlockSpec(memory_space=pltpu.VMEM)


def spec_smem():
    return pl.BlockSpec(memory_space=pltpu.SMEM)


def call(body, outs, ins, scratch=(), smem=0, flops=0, name=None):
    nbytes = sum(math.prod(a.shape) * a.dtype.itemsize for a in list(ins) + list(outs))
    return pl.pallas_call(
        body,
        out_shape=outs,
        in_specs=[spec_smem()] * smem + [spec_vmem()] * (len(ins) - smem),
        out_specs=[spec_vmem()] * len(outs),
        scratch_shapes=list(scratch),
        compiler_params=pltpu.CompilerParams(vmem_limit_bytes=VMEM_LIMIT),
        cost_estimate=pl.CostEstimate(flops=flops, bytes_accessed=nbytes, transcendentals=0),
        name=name,
    )(*ins)


def sds(shape, dtype):
    return jax.ShapeDtypeStruct(shape, dtype)


def segment_ids(lengths, length):
    ends = jnp.cumsum(lengths)
    places = jnp.arange(length, dtype=jnp.int32)
    return jnp.sum((places[:, None] >= ends[None, :]).astype(jnp.int32), axis=1)


def place(me, step, parts, rows):
    return pl.multiple_of(lax.rem(me - step + parts, parts) * rows, rows)


def masks(seg_col, seg_row, length):
    same = seg_col == seg_row
    row = lax.broadcasted_iota(jnp.int32, (length, length), 0)
    col = lax.broadcasted_iota(jnp.int32, (length, length), 1)
    return same, same & (col <= row)


def shift_rows(values, shift, same):
    if shift == 0:
        return values.astype(BF16)
    length = values.shape[0]
    return jnp.where(same, pltpu.roll(values, shift % length, 0), 0.0).astype(BF16)


def head_norm(heads_out):
    centered = heads_out - jnp.mean(heads_out, axis=-1, keepdims=True)
    inv_std = lax.rsqrt(jnp.mean(centered * centered, axis=-1, keepdims=True) + EPS)
    return centered * inv_std, inv_std


def attn_fwd_body(cfg, me_ref, mix_ref, *refs):
    parts, rows, heads, size, batch = cfg
    x_refs = refs[:parts]
    w_ref, band_ref, segc_ref, segr_ref, ggain_ref = refs[parts : parts + 5]
    outs = refs[parts + 5 :]
    att_refs = outs[:parts]
    normed_ref, qkv_ref, z_ref, p_ref, ho_ref, grouped_ref, gains_ref, att_scr = outs[parts:]
    length = parts * rows
    width = heads * size
    me = me_ref[0]
    gains = w_ref[:, 4 * width :].astype(F32).T
    gains_ref[...] = gains[:8]
    gain = gains[0:1]
    for step in range(parts):
        x = x_refs[step][batch].astype(F32)
        r1 = lax.rsqrt(jnp.mean(x * x, axis=-1, keepdims=True) + EPS)
        normed_ref[pl.ds(place(me, step, parts, rows), rows), :] = (x * r1 * gain).astype(BF16)
    qkv_ref[...] = mm(normed_ref[...], w_ref[:, : 3 * width]).astype(BF16)
    same, allow = masks(segc_ref[...], segr_ref[...], length)
    scale = 1.0 / math.sqrt(size)
    for pair in range(heads // 2):
        probs = []
        for b in range(2):
            h = 2 * pair + b
            q = qkv_ref[:, h * size : (h + 1) * size]
            k = qkv_ref[:, width + h * size : width + (h + 1) * size]
            z = jnp.where(allow, mm(q, k, NT) * scale, 0.0)
            z_ref[h] = z.astype(BF16)
            acc = jnp.zeros((length, length), F32)
            for a in range(CQ):
                acc = acc + mm(shift_rows(z, a, same), band_ref[h * CQ + a])
            logits = jnp.where(allow, acc, -jnp.inf)
            e = jnp.exp(logits - jnp.max(logits, axis=-1, keepdims=True))
            p = e * (1.0 / jnp.sum(e, axis=-1, keepdims=True))
            p_ref[h] = p
            probs.append(p)
        for a in range(2):
            h = 2 * pair + a
            mixed = (
                mix_ref[4 * pair + 2 * a] * probs[0] + mix_ref[4 * pair + 2 * a + 1] * probs[1]
            ).astype(BF16)
            v = qkv_ref[:, 2 * width + h * size : 2 * width + (h + 1) * size]
            ho = mm(mixed, v)
            ho_ref[h] = ho
            normed, _ = head_norm(ho)
            grouped_ref[:, h * size : (h + 1) * size] = (
                normed * ggain_ref[:, h * size : (h + 1) * size]
            ).astype(BF16)
    att_scr[...] = mm(grouped_ref[...], w_ref[:, 3 * width : 4 * width], NT)
    for step in range(parts):
        att_refs[step][...] = att_scr[pl.ds(place(me, step, parts, rows), rows), :].astype(BF16)


def attn_fwd(me, mix, xs, w1, band, segc, segr, ggain, heads, size, batch):
    parts = len(xs)
    _, rows, d = xs[0].shape
    length, width = parts * rows, heads * size
    outs = (
        [sds((rows, d), BF16)] * parts
        + [
            sds((length, d), BF16),
            sds((length, 3 * width), BF16),
            sds((heads, length, length), BF16),
            sds((heads, length, length), F32),
            sds((heads, length, size), F32),
            sds((length, width), BF16),
            sds((8, d), F32),
        ]
    )
    res = call(
        functools.partial(attn_fwd_body, (parts, rows, heads, size, batch)),
        outs,
        [me, mix, *xs, w1, band, segc, segr, ggain],
        scratch=[pltpu.VMEM((length, d), F32)],
        smem=2,
        flops=2 * length * d * width * 4 + 2 * heads * (CQ + 2) * length**3,
        name="attn_fwd",
    )
    return res[:parts], res[parts:]


def tail_rms(values, gain):
    r = lax.rsqrt(jnp.mean(values * values, axis=-1, keepdims=True) + EPS)
    return values * r, r


def rms_back(grad, normal, r, gain):
    u = grad * gain
    return r * (u - normal * jnp.mean(u * normal, axis=-1, keepdims=True))


def total(refs):
    acc = refs[0][...].astype(F32)
    for ref in refs[1:]:
        acc = acc + ref[...].astype(F32)
    return acc


def mid_body(parts, *refs):
    x_ref, gains_ref = refs[:2]
    hid_ref, mid_ref = refs[2 + parts :]
    hidden_in = x_ref[...].astype(F32) + total(refs[2 : 2 + parts])
    hid_ref[...] = hidden_in
    normal, _ = tail_rms(hidden_in, None)
    mid_ref[...] = (normal * gains_ref[1:2]).astype(BF16)


def mid_step(x, gains, pieces):
    return call(
        functools.partial(mid_body, len(pieces)),
        [sds(x.shape, F32), sds(x.shape, BF16)],
        [x, gains, *pieces],
        name="mid_step",
    )


def mid_back_body(parts, *refs):
    hid_ref, dy_ref, gains_ref = refs[:3]
    ghid_ref, ga_ref, gain_ref = refs[3 + parts :]
    gain = gains_ref[1:2]
    normal, r = tail_rms(hid_ref[...], None)
    grad = total(refs[3 : 3 + parts])
    gain_ref[...] = jnp.sum(grad * normal, axis=0, keepdims=True)
    ghid = dy_ref[...].astype(F32) + rms_back(grad, normal, r, gain)
    ghid_ref[...] = ghid
    ga_ref[...] = ghid.astype(BF16)


def mid_back(hid, dy, gains, pieces):
    return call(
        functools.partial(mid_back_body, len(pieces)),
        [sds(hid.shape, F32), sds(hid.shape, BF16), sds((1, hid.shape[1]), F32)],
        [hid, dy, gains, *pieces],
        name="mid_back",
    )


def last_body(parts, *refs):
    x_ref, ghid_ref, gains_ref = refs[:3]
    out_ref = refs[3 + parts]
    normal, r = tail_rms(x_ref[...].astype(F32), None)
    grad = total(refs[3 : 3 + parts])
    out_ref[...] = ghid_ref[...] + rms_back(grad, normal, r, gains_ref[0:1])


def last_step(x, ghid, gains, pieces):
    return call(
        functools.partial(last_body, len(pieces)),
        [sds(x.shape, F32)],
        [x, ghid, gains, *pieces],
        name="last_step",
    )[0]


def ffn_body(parts, rows, batch, me_ref, *refs):
    m_refs, dy_refs = refs[:parts], refs[parts : 2 * parts]
    wg_ref, wu_ref, wd_ref = refs[2 * parts : 2 * parts + 3]
    rest = refs[2 * parts + 3 :]
    g_refs = rest[:parts]
    o_ref, mid_ref, dy_ref, right_ref, out_acc, gmid_acc = rest[parts:]
    j = pl.program_id(0)
    me = me_ref[0]

    @pl.when(j == 0)
    def _():
        for step in range(parts):
            spot = pl.ds(place(me, step, parts, rows), rows)
            mid_ref[spot, :] = m_refs[step][...]
            dy_ref[spot, :] = dy_refs[step][batch]
        out_acc[...] = jnp.zeros_like(out_acc)
        gmid_acc[...] = jnp.zeros_like(gmid_acc)

    mid = mid_ref[...]
    gate = mm(mid, wg_ref[...])
    up = mm(mid, wu_ref[...])
    gh = mm(dy_ref[...], wd_ref[...])
    sig = jax.nn.sigmoid(gate)
    swish = gate * sig
    hidden = (swish * up).astype(BF16)
    gg = (gh * up * sig * (1.0 + gate * (1.0 - sig))).astype(BF16)
    gu = (gh * swish).astype(BF16)
    right_ref[0] = gg
    right_ref[1] = gu
    right_ref[2] = hidden
    gmid_acc[...] += mm(gg, wg_ref[...], NT) + mm(gu, wu_ref[...], NT)
    out_acc[...] += mm(hidden, wd_ref[...], NT)

    @pl.when(j == pl.num_programs(0) - 1)
    def _():
        for step in range(parts):
            spot = pl.ds(place(me, step, parts, rows), rows)
            g_refs[step][...] = gmid_acc[spot, :].astype(BF16)
        o_ref[...] = out_acc[...].astype(BF16)


def ffn(me, ms, dys, w2, batch):
    parts = len(ms)
    rows, d = ms[0].shape
    length = parts * rows
    ff = w2.shape[1] // 3
    cols = min(256, ff)
    steps = ff // cols
    whole = lambda shape: pl.BlockSpec(shape, lambda j: (0, 0))
    weight = lambda c: pl.BlockSpec((d, cols), lambda j, c=c: (0, c * steps + j))
    res = pl.pallas_call(
        functools.partial(ffn_body, parts, rows, batch),
        grid=(steps,),
        in_specs=[spec_smem()]
        + [whole((rows, d))] * parts
        + [pl.BlockSpec(dys[0].shape, lambda j: (0, 0, 0))] * parts
        + [weight(0), weight(1), weight(2)],
        out_specs=[whole((rows, d))] * parts
        + [whole((length, d))] * 3
        + [pl.BlockSpec((3, length, cols), lambda j: (0, 0, j))],
        out_shape=[sds((rows, d), BF16)] * parts
        + [sds((length, d), BF16)] * 3
        + [sds((3, length, ff), BF16)],
        scratch_shapes=[pltpu.VMEM((length, d), F32)] * 2,
        compiler_params=pltpu.CompilerParams(vmem_limit_bytes=VMEM_LIMIT),
        cost_estimate=pl.CostEstimate(
            flops=2 * length * d * ff * 6, bytes_accessed=6 * d * ff, transcendentals=0
        ),
        name="ffn",
    )(me, *ms, *dys, w2, w2, w2)
    return res[:parts], res[parts], res[parts + 1 :]


def turn(left, sources):
    length = sources[0].shape[0]
    for n, source in enumerate(sources):
        left[:, n * length : (n + 1) * length] = source[...].T


def stack(right, sources):
    length = sources[0].shape[0]
    for n, source in enumerate(sources):
        right[n * length : (n + 1) * length, :] = source


def ffn_grads_body(count, *refs):
    mids, dys, rights = refs[:count], refs[count : 2 * count], refs[2 * count : 3 * count]
    out_ref, left, right = refs[3 * count :]
    kind, j = pl.program_id(0), pl.program_id(1)
    pl.when((kind == 0) & (j == 0))(lambda: turn(left, mids))
    pl.when((kind == 2) & (j == 0))(lambda: turn(left, dys))
    stack(right, [ref[0] for ref in rights])
    out_ref[...] = mm(left[...], right[...]).astype(BF16)


def ffn_grads(mids, dys, rights):
    count = len(mids)
    length, d = mids[0].shape
    ff = rights[0].shape[2]
    cols = min(512, ff)
    steps = ff // cols
    whole = pl.BlockSpec((length, d), lambda k, j: (0, 0))
    return pl.pallas_call(
        functools.partial(ffn_grads_body, count),
        grid=(3, steps),
        in_specs=[whole] * (2 * count)
        + [pl.BlockSpec((1, length, cols), lambda k, j: (k, 0, j))] * count,
        out_specs=pl.BlockSpec((d, cols), lambda k, j: (0, k * steps + j)),
        out_shape=sds((d, 3 * ff), BF16),
        scratch_shapes=[
            pltpu.VMEM((d, count * length), BF16),
            pltpu.VMEM((count * length, cols), BF16),
        ],
        compiler_params=pltpu.CompilerParams(vmem_limit_bytes=VMEM_LIMIT),
        cost_estimate=pl.CostEstimate(
            flops=6 * count * length * d * ff, bytes_accessed=6 * d * ff, transcendentals=0
        ),
        name="ffn_grads",
    )(*mids, *dys, *rights)


def attn_grads_body(count, *refs):
    ins, gas = refs[:count], refs[count : 2 * count]
    projs, groups = refs[2 * count : 3 * count], refs[3 * count : 4 * count]
    out_ref, left, right = refs[4 * count :]
    j = pl.program_id(0)
    last = pl.num_programs(0) - 1

    @pl.when(j == 0)
    def _():
        turn(left, ins)

    @pl.when(j < last)
    def _():
        stack(right, [ref[...] for ref in projs])

    @pl.when(j == last)
    def _():
        turn(left, gas)
        stack(right, [ref[...] for ref in groups])

    out_ref[...] = mm(left[...], right[...]).astype(BF16)


def attn_grads(ins, gas, projs, groups):
    count = len(ins)
    length, d = ins[0].shape
    width = groups[0].shape[1]
    whole = pl.BlockSpec((length, d), lambda j: (0, 0))
    return pl.pallas_call(
        functools.partial(attn_grads_body, count),
        grid=(4,),
        in_specs=[whole] * (2 * count)
        + [pl.BlockSpec((length, width), lambda j: (0, jnp.minimum(j, 2)))] * count
        + [pl.BlockSpec((length, width), lambda j: (0, 0))] * count,
        out_specs=pl.BlockSpec((d, width), lambda j: (0, j)),
        out_shape=sds((d, 4 * width), BF16),
        scratch_shapes=[
            pltpu.VMEM((d, count * length), BF16),
            pltpu.VMEM((count * length, width), BF16),
        ],
        compiler_params=pltpu.CompilerParams(vmem_limit_bytes=VMEM_LIMIT),
        cost_estimate=pl.CostEstimate(
            flops=8 * count * length * d * width, bytes_accessed=8 * d * width, transcendentals=0
        ),
        name="attn_grads",
    )(*ins, *gas, *projs, *groups)


def band_sum(values, length):
    lane = lax.broadcasted_iota(jnp.int32, (8, 128), 1)
    lane = jnp.where(lane >= 64, lane - 128, lane)
    acc = jnp.zeros((8, 128), F32)
    tiles = length // 128
    for s in range(length // 8):
        back = (128 - 8 * s % 128) % 128
        low, high = 8 * s - CENTER, 8 * s + 7 + CENTER
        first, last = max(low, 0) // 128, min(high, length - 1) // 128
        for tile in range(first, last + 1):
            piece = values[8 * s : 8 * s + 8, tile * 128 : (tile + 1) * 128]
            if back:
                piece = pltpu.roll(piece, back, 1)
            start, stop = tile * 128 - 8 * s, tile * 128 + 128 - 8 * s
            if low < tile * 128 or high >= tile * 128 + 128:
                piece = jnp.where((lane >= start) & (lane < stop), piece, 0.0)
            acc = acc + piece
    return acc


def attn_bwd_body(cfg, me_ref, mix_ref, *refs):
    parts, rows, heads, size = cfg
    ga_refs = refs[:parts]
    (w_ref, band_ref, segc_ref, segr_ref, ggain_ref, gains_ref, normed_ref, qkv_ref, z_ref,
     p_ref, ho_ref) = refs[parts : parts + 11]
    outs = refs[parts + 11 :]
    gi_refs = outs[:parts]
    (gaa_ref, gproj_ref, again_ref, ggrad_ref, kern_ref, mixg_ref, gin_scr, diag_scr) = outs[parts:]
    length = parts * rows
    width = heads * size
    me = me_ref[0]
    for step in range(parts):
        gaa_ref[pl.ds(place(me, step, parts, rows), rows), :] = ga_refs[step][...]
    gin_scr[:, :width] = mm(gaa_ref[...], w_ref[:, 3 * width : 4 * width])
    same, allow = masks(segc_ref[...], segr_ref[...], length)
    scale = 1.0 / math.sqrt(size)
    for pair in range(heads // 2):
        gmix = []
        for a in range(2):
            h = 2 * pair + a
            lanes = slice(h * size, (h + 1) * size)
            gg = gin_scr[:, lanes]
            normed, inv_std = head_norm(ho_ref[h])
            ggrad_ref[:, lanes] = jnp.sum(gg * normed, axis=0, keepdims=True)
            u = gg * ggain_ref[:, lanes]
            gh = inv_std * (
                u
                - jnp.mean(u, axis=-1, keepdims=True)
                - normed * jnp.mean(u * normed, axis=-1, keepdims=True)
            )
            gh = gh.astype(BF16)
            v = qkv_ref[:, 2 * width + h * size : 2 * width + (h + 1) * size]
            gmix.append(mm(gh, v, NT))
            mixed = (
                mix_ref[4 * pair + 2 * a] * p_ref[2 * pair]
                + mix_ref[4 * pair + 2 * a + 1] * p_ref[2 * pair + 1]
            ).astype(BF16)
            gproj_ref[:, 2 * width + h * size : 2 * width + (h + 1) * size] = mm(
                mixed, gh, TN
            ).astype(BF16)
        for b in range(2):
            h = 2 * pair + b
            p = p_ref[h]
            for a in range(2):
                mixg_ref[4 * pair + 2 * a + b : 4 * pair + 2 * a + b + 1, :] = jnp.sum(
                    gmix[a] * p, axis=0, keepdims=True
                )
            gp = mix_ref[4 * pair + b] * gmix[0] + mix_ref[4 * pair + 2 + b] * gmix[1]
            gl = p * (gp - jnp.sum(gp * p, axis=-1, keepdims=True))
            glt = gl.T.astype(BF16)
            z = z_ref[h].astype(F32)
            gz = jnp.zeros((length, length), F32)
            for a in range(CQ):
                gz = gz + mm(shift_rows(gl, -a, same), band_ref[h * CQ + a], NT)
                diag_scr[h * CQ + a] = band_sum(mm(glt, shift_rows(z, a, same)), length)
            gs = jnp.where(allow, gz, 0.0).astype(BF16)
            q = qkv_ref[:, h * size : (h + 1) * size]
            k = qkv_ref[:, width + h * size : width + (h + 1) * size]
            gproj_ref[:, h * size : (h + 1) * size] = (mm(gs, k) * scale).astype(BF16)
            gproj_ref[:, width + h * size : width + (h + 1) * size] = (
                mm(gs, q, TN) * scale
            ).astype(BF16)
    taps = diag_scr[:, 0, :]
    for r in range(1, 8):
        taps = taps + pltpu.roll(diag_scr[:, r, :], 128 - r, 1)
    kern_ref[...] = taps
    gin_scr[...] = mm(gproj_ref[...], w_ref[:, : 3 * width], NT)
    again_ref[...] = (
        jnp.sum(gin_scr[...] * normed_ref[...].astype(F32), axis=0, keepdims=True) / gains_ref[0:1]
    )
    for step in range(parts):
        gi_refs[step][...] = gin_scr[pl.ds(place(me, step, parts, rows), rows), :].astype(BF16)


def attn_bwd(me, mix, gas, w1, band, segc, segr, ggain, gains, saved, heads, size):
    parts = len(gas)
    rows, d = gas[0].shape
    length, width = parts * rows, heads * size
    outs = (
        [sds((rows, d), BF16)] * parts
        + [
            sds((length, d), BF16),
            sds((length, 3 * width), BF16),
            sds((1, d), F32),
            sds((1, width), F32),
            sds((heads * CQ, 128), F32),
            sds((2 * heads, length), F32),
        ]
    )
    res = call(
        functools.partial(attn_bwd_body, (parts, rows, heads, size)),
        outs,
        [me, mix, *gas, w1, band, segc, segr, ggain, gains, *saved],
        scratch=[pltpu.VMEM((length, d), F32), pltpu.VMEM((heads * CQ, 8, 128), F32)],
        smem=2,
        flops=2 * length * d * width * 4 + 2 * heads * (2 * CQ + 4) * length**3,
        name="attn_bwd",
    )
    return res[:parts], res[parts:]


def shift_mp(part, step, size):
    return lax.ppermute(part, "mp", [(i, (i + step) % size) for i in range(size)])


def gather_mp(part, size):
    if size != 4:
        return [part] + [shift_mp(part, step, size) for step in range(1, size)]
    back, ahead = shift_mp(part, 1, size), shift_mp(part, -1, size)
    return [part, back, shift_mp(back, 1, size), ahead]


def scatter_mp(pieces, size):
    if size != 4:
        return [pieces[0]] + [shift_mp(pieces[step], -step, size) for step in range(1, size)]
    far = shift_mp(pieces[2], -1, size)
    ahead = shift_mp(pieces[3], 1, size)
    near = (pieces[1].astype(F32) + far.astype(F32)).astype(BF16)
    return [pieces[0], ahead, shift_mp(near, -1, size)]


def take(values, index, axis):
    return lax.dynamic_index_in_dim(values, index, axis, keepdims=False)


def scatter_dp(whole, extra, size):
    rows, cols = whole.shape[0] // size, whole.shape[1]
    if size != 8:
        whole = lax.psum_scatter(whole, "dp", scatter_dimension=0, tiled=True).astype(F32)
        return whole, lax.psum(extra, "dp")
    me = lax.axis_index("dp")
    core, chip = me % 2, me // 2
    pieces = whole.reshape(size // 2, 2, rows, cols)
    keep, give = take(pieces, core, 1), take(pieces, 1 - core, 1)
    pairs = [(i, i ^ 1) for i in range(size)]
    keep = (keep.astype(F32) + lax.ppermute(give, "dp", pairs).astype(F32)).astype(BF16)
    extra = extra + lax.ppermute(extra, "dp", pairs)
    count = extra.shape[0]
    high = extra.astype(BF16)
    low = (extra - high.astype(F32)).astype(BF16)
    tail = jnp.concatenate([high, low])
    tail = jnp.pad(tail, (0, -tail.shape[0] % (16 * cols))).reshape(-1, cols)
    total = take(keep, chip, 0).astype(F32)
    for step in (3, 1, 2):
        send = jnp.concatenate([take(keep, chip ^ step, 0), tail])
        got = lax.ppermute(send, "dp", [(i, i ^ (2 * step)) for i in range(size)]).astype(F32)
        total = total + got[:rows]
        flat = got[rows:].reshape(-1)
        extra = extra + (flat[:count] + flat[count : 2 * count])
    return total, extra


def shards(
    block_input,
    out_grad,
    doc_lengths,
    attn_gain,
    qkv_weight,
    conv_kernel,
    head_mixing,
    group_gain,
    out_weight,
    mlp_gain,
    gate_weight,
    up_weight,
    down_weight,
):
    batches = block_input.shape[0]
    rows = block_input.shape[2]
    mp, dp = lax.axis_size("mp"), lax.axis_size("dp")
    length = rows * mp
    heads = conv_kernel.shape[0]
    width = qkv_weight.shape[2]
    size = width // heads
    local_d = attn_gain.shape[0]
    me = lax.axis_index("mp").astype(jnp.int32).reshape(1)
    mix = head_mixing.reshape(-1)
    ggain = group_gain.astype(F32)[None]

    gains_cols = jnp.pad(jnp.stack([attn_gain, mlp_gain], axis=1), ((0, 0), (0, 126)))
    pack1 = jnp.concatenate(
        [qkv_weight[0], qkv_weight[1], qkv_weight[2], out_weight.T, gains_cols], axis=1
    )
    pack2 = jnp.concatenate([gate_weight, up_weight, down_weight.T], axis=1)
    w1 = lax.all_gather(pack1, "dp", axis=0, tiled=True)
    w2 = lax.all_gather(pack2, "dp", axis=0, tiled=True)

    offset = (
        jnp.arange(length, dtype=jnp.int32)[None, :]
        - jnp.arange(length, dtype=jnp.int32)[:, None]
        + CENTER
    )
    band = jnp.zeros((heads * CQ, length, length), F32)
    taps = conv_kernel.reshape(heads * CQ, CK)
    for b in range(CK):
        band = jnp.where(offset[None] == b, taps[:, b][:, None, None], band)
    band = band.astype(BF16)

    xs = gather_mp(block_input[:, 0], mp)
    dy_rows, _ = lax.optimization_barrier((out_grad[:, 0], xs))
    dys = gather_mp(dy_rows, mp)
    segs, front = [], []
    for batch in range(batches):
        segment = segment_ids(doc_lengths[batch, 0], length)
        segs.append((segment[:, None], segment[None, :]))
        front.append(attn_fwd(me, mix, xs, w1, band, *segs[batch], ggain, heads, size, batch))
    mids = []
    for batch in range(batches):
        pieces, saved = front[batch]
        x, _ = lax.optimization_barrier((block_input[batch, 0], dys))
        mids.append(mid_step(x, saved[-1], scatter_mp(pieces, mp)))
    middle = []
    for batch in range(batches):
        parts = gather_mp(mids[batch][1], mp)
        parts, _ = lax.optimization_barrier((parts, mids[-1]))
        middle.append((mids[batch][0], *ffn(me, parts, dys, w2, batch)))
    grads2 = ffn_grads([m[3][0] for m in middle], [m[3][1] for m in middle], [m[3][2] for m in middle])
    share2 = lax.psum_scatter(grads2, "dp", scatter_dimension=0, tiled=True)

    turned = []
    for batch in range(batches):
        hid, g_pieces, _, _ = middle[batch]
        got, _ = lax.optimization_barrier((scatter_mp(g_pieces, mp), grads2))
        turned.append(mid_back(hid, out_grad[batch, 0], front[batch][1][-1], got))
    back, kept, head_total = [], [], None
    for batch in range(batches):
        normed, qkv, z, probs, ho, grouped, gains = front[batch][1]
        ghid, ga, mlp_part = turned[batch]
        gas, _ = lax.optimization_barrier((gather_mp(ga, mp), turned[-1]))
        gi_pieces, (ga_all, gproj, again, ggrad, kern, mixg) = attn_bwd(
            me, mix, gas, w1, band, *segs[batch], ggain, gains, [normed, qkv, z, probs, ho], heads, size
        )
        back.append((ghid, gi_pieces))
        small = (again, mlp_part, ggrad, kern, jnp.sum(mixg, axis=1))
        head_total = small if head_total is None else jax.tree.map(jnp.add, head_total, small)
        kept.append((normed, ga_all, gproj, grouped))
    input_grads = []
    for batch in range(batches):
        ghid, gi_pieces = back[batch]
        gains = front[batch][1][-1]
        input_grads.append(last_step(block_input[batch, 0], ghid, gains, scatter_mp(gi_pieces, mp)))
    o_parts, _ = lax.optimization_barrier((jnp.stack([m[2] for m in middle]), back[0][1][0]))
    mlp_out = lax.psum_scatter(o_parts, "mp", scatter_dimension=1, tiled=True)
    outputs = (jnp.stack([m[0] for m in middle]) + mlp_out.astype(F32)).astype(BF16)

    again, mlp_part, ggrad, kern, mixg = head_total
    d = again.shape[1]
    kern = jnp.roll(kern, CK - 1 - CENTER, axis=1)[:, :CK][:, ::-1]
    extra = jnp.concatenate([again[0], mlp_part[0], ggrad[0], kern.reshape(-1), mixg])
    grads1 = attn_grads(*(list(group) for group in zip(*kept)))
    share1, extra = scatter_dp(grads1, extra, dp)
    share2 = share2.astype(F32)
    gain_grads = extra[: 2 * d].reshape(2, dp, local_d)
    gain_grads = take(gain_grads, lax.axis_index("dp"), 1)
    gain_grads = functools.reduce(jnp.add, gather_mp(gain_grads, mp))
    ggrad, kern, mixg = jnp.split(extra[2 * d :], [width, width + heads * CQ * CK])
    kernel_grad = kern.reshape(heads, CQ, CK)
    mixing_grad = mixg.reshape(heads // 2, 2, 2)
    ff = gate_weight.shape[1]
    return (
        outputs[:, None],
        jnp.stack(input_grads)[:, None],
        gain_grads[0],
        jnp.stack([share1[:, c * width : (c + 1) * width] for c in range(3)]),
        kernel_grad,
        mixing_grad,
        ggrad,
        share1[:, 3 * width :].T,
        gain_grads[1],
        share2[:, :ff],
        share2[:, ff : 2 * ff],
        share2[:, 2 * ff :].T,
    )


def solution(mesh):
    return jax.shard_map(
        shards,
        mesh=mesh,
        in_specs=(
            P(None, "dp", "mp", None),
            P(None, "dp", "mp", None),
            P(None, "dp", None),
            P("dp"),
            P(None, "dp", "mp"),
            P("mp", None, None),
            P("mp", None, None),
            P("mp"),
            P("mp", "dp"),
            P("dp"),
            P("dp", "mp"),
            P("dp", "mp"),
            P("mp", "dp"),
        ),
        out_specs=(
            P(None, "dp", "mp", None),
            P(None, "dp", "mp", None),
            P("dp"),
            P(None, "dp", "mp"),
            P("mp", None, None),
            P("mp", None, None),
            P("mp"),
            P("mp", "dp"),
            P("dp"),
            P("dp", "mp"),
            P("dp", "mp"),
            P("mp", "dp"),
        ),
        check_vma=False,
    )
```

```python
import functools
import math

import jax
import jax.numpy as jnp
from jax import lax
from jax.experimental import pallas as pl
from jax.experimental.pallas import tpu as pltpu
from jax.sharding import PartitionSpec as P

CQ = 6
CK = 11
CENTER = CK // 2
EPS = 1e-05
F32 = jnp.float32
BF16 = jnp.bfloat16
VMEM_LIMIT = 58 * 1024 * 1024

NN = (((1,), (0,)), ((), ()))
NT = (((1,), (1,)), ((), ()))
TN = (((0,), (0,)), ((), ()))


def mm(left, right, dims=NN):
    return lax.dot_general(left, right, dims, preferred_element_type=F32)


def spec_vmem():
    return pl.BlockSpec(memory_space=pltpu.VMEM)


def spec_smem():
    return pl.BlockSpec(memory_space=pltpu.SMEM)


def call(body, outs, ins, scratch=(), smem=0, flops=0, name=None):
    nbytes = sum(math.prod(a.shape) * a.dtype.itemsize for a in list(ins) + list(outs))
    return pl.pallas_call(
        body,
        out_shape=outs,
        in_specs=[spec_smem()] * smem + [spec_vmem()] * (len(ins) - smem),
        out_specs=[spec_vmem()] * len(outs),
        scratch_shapes=list(scratch),
        compiler_params=pltpu.CompilerParams(vmem_limit_bytes=VMEM_LIMIT),
        cost_estimate=pl.CostEstimate(flops=flops, bytes_accessed=nbytes, transcendentals=0),
        name=name,
    )(*ins)


def sds(shape, dtype):
    return jax.ShapeDtypeStruct(shape, dtype)


def segment_ids(lengths, length):
    ends = jnp.cumsum(lengths)
    places = jnp.arange(length, dtype=jnp.int32)
    return jnp.sum((places[:, None] >= ends[None, :]).astype(jnp.int32), axis=1)


def place(me, step, parts, rows):
    return pl.multiple_of(lax.rem(me - step + parts, parts) * rows, rows)


def masks(seg_col, seg_row, length):
    same = seg_col == seg_row
    row = lax.broadcasted_iota(jnp.int32, (length, length), 0)
    col = lax.broadcasted_iota(jnp.int32, (length, length), 1)
    return same, same & (col <= row)


def shift_rows(values, shift, same):
    if shift == 0:
        return values.astype(BF16)
    length = values.shape[0]
    return jnp.where(same, pltpu.roll(values, shift % length, 0), 0.0).astype(BF16)


def head_norm(heads_out):
    centered = heads_out - jnp.mean(heads_out, axis=-1, keepdims=True)
    inv_std = lax.rsqrt(jnp.mean(centered * centered, axis=-1, keepdims=True) + EPS)
    return centered * inv_std, inv_std


def attn_fwd_body(cfg, me_ref, mix_ref, *refs):
    parts, rows, heads, size, batch = cfg
    x_refs = refs[:parts]
    w_ref, band_ref, segc_ref, segr_ref, ggain_ref = refs[parts : parts + 5]
    outs = refs[parts + 5 :]
    att_refs = outs[:parts]
    normed_ref, qkv_ref, z_ref, p_ref, ho_ref, grouped_ref, gains_ref, att_scr = outs[parts:]
    length = parts * rows
    width = heads * size
    me = me_ref[0]
    gains = w_ref[:, 4 * width :].astype(F32).T
    gains_ref[...] = gains[:8]
    gain = gains[0:1]
    for step in range(parts):
        x = x_refs[step][batch].astype(F32)
        r1 = lax.rsqrt(jnp.mean(x * x, axis=-1, keepdims=True) + EPS)
        normed_ref[pl.ds(place(me, step, parts, rows), rows), :] = (x * r1 * gain).astype(BF16)
    qkv_ref[...] = mm(normed_ref[...], w_ref[:, : 3 * width]).astype(BF16)
    same, allow = masks(segc_ref[...], segr_ref[...], length)
    scale = 1.0 / math.sqrt(size)
    for pair in range(heads // 2):
        probs = []
        for b in range(2):
            h = 2 * pair + b
            q = qkv_ref[:, h * size : (h + 1) * size]
            k = qkv_ref[:, width + h * size : width + (h + 1) * size]
            z = jnp.where(allow, mm(q, k, NT) * scale, 0.0)
            z_ref[h] = z.astype(BF16)
            acc = jnp.zeros((length, length), F32)
            for a in range(CQ):
                acc = acc + mm(shift_rows(z, a, same), band_ref[h * CQ + a])
            logits = jnp.where(allow, acc, -jnp.inf)
            e = jnp.exp(logits - jnp.max(logits, axis=-1, keepdims=True))
            p = e * (1.0 / jnp.sum(e, axis=-1, keepdims=True))
            p_ref[h] = p
            probs.append(p)
        for a in range(2):
            h = 2 * pair + a
            mixed = (
                mix_ref[4 * pair + 2 * a] * probs[0] + mix_ref[4 * pair + 2 * a + 1] * probs[1]
            ).astype(BF16)
            v = qkv_ref[:, 2 * width + h * size : 2 * width + (h + 1) * size]
            ho = mm(mixed, v)
            ho_ref[h] = ho
            normed, _ = head_norm(ho)
            grouped_ref[:, h * size : (h + 1) * size] = (
                normed * ggain_ref[:, h * size : (h + 1) * size]
            ).astype(BF16)
    att_scr[...] = mm(grouped_ref[...], w_ref[:, 3 * width : 4 * width], NT)
    for step in range(parts):
        att_refs[step][...] = att_scr[pl.ds(place(me, step, parts, rows), rows), :].astype(BF16)


def attn_fwd(me, mix, xs, w1, band, segc, segr, ggain, heads, size, batch):
    parts = len(xs)
    _, rows, d = xs[0].shape
    length, width = parts * rows, heads * size
    outs = (
        [sds((rows, d), BF16)] * parts
        + [
            sds((length, d), BF16),
            sds((length, 3 * width), BF16),
            sds((heads, length, length), BF16),
            sds((heads, length, length), F32),
            sds((heads, length, size), F32),
            sds((length, width), BF16),
            sds((8, d), F32),
        ]
    )
    res = call(
        functools.partial(attn_fwd_body, (parts, rows, heads, size, batch)),
        outs,
        [me, mix, *xs, w1, band, segc, segr, ggain],
        scratch=[pltpu.VMEM((length, d), F32)],
        smem=2,
        flops=2 * length * d * width * 4 + 2 * heads * (CQ + 2) * length**3,
        name="attn_fwd",
    )
    return res[:parts], res[parts:]


def tail_rms(values, gain):
    r = lax.rsqrt(jnp.mean(values * values, axis=-1, keepdims=True) + EPS)
    return values * r, r


def rms_back(grad, normal, r, gain):
    u = grad * gain
    return r * (u - normal * jnp.mean(u * normal, axis=-1, keepdims=True))


def total(refs):
    acc = refs[0][...].astype(F32)
    for ref in refs[1:]:
        acc = acc + ref[...].astype(F32)
    return acc


def mid_body(parts, *refs):
    x_ref, gains_ref = refs[:2]
    hid_ref, mid_ref = refs[2 + parts :]
    hidden_in = x_ref[...].astype(F32) + total(refs[2 : 2 + parts])
    hid_ref[...] = hidden_in
    normal, _ = tail_rms(hidden_in, None)
    mid_ref[...] = (normal * gains_ref[1:2]).astype(BF16)


def mid_step(x, gains, pieces):
    return call(
        functools.partial(mid_body, len(pieces)),
        [sds(x.shape, F32), sds(x.shape, BF16)],
        [x, gains, *pieces],
        name="mid_step",
    )


def mid_back_body(parts, *refs):
    hid_ref, dy_ref, gains_ref = refs[:3]
    ghid_ref, ga_ref, gain_ref = refs[3 + parts :]
    gain = gains_ref[1:2]
    normal, r = tail_rms(hid_ref[...], None)
    grad = total(refs[3 : 3 + parts])
    gain_ref[...] = jnp.sum(grad * normal, axis=0, keepdims=True)
    ghid = dy_ref[...].astype(F32) + rms_back(grad, normal, r, gain)
    ghid_ref[...] = ghid
    ga_ref[...] = ghid.astype(BF16)


def mid_back(hid, dy, gains, pieces):
    return call(
        functools.partial(mid_back_body, len(pieces)),
        [sds(hid.shape, F32), sds(hid.shape, BF16), sds((1, hid.shape[1]), F32)],
        [hid, dy, gains, *pieces],
        name="mid_back",
    )


def last_body(parts, *refs):
    x_ref, ghid_ref, gains_ref = refs[:3]
    out_ref = refs[3 + parts]
    normal, r = tail_rms(x_ref[...].astype(F32), None)
    grad = total(refs[3 : 3 + parts])
    out_ref[...] = ghid_ref[...] + rms_back(grad, normal, r, gains_ref[0:1])


def last_step(x, ghid, gains, pieces):
    return call(
        functools.partial(last_body, len(pieces)),
        [sds(x.shape, F32)],
        [x, ghid, gains, *pieces],
        name="last_step",
    )[0]


def ffn_body(parts, rows, batch, me_ref, *refs):
    m_refs, dy_refs = refs[:parts], refs[parts : 2 * parts]
    wg_ref, wu_ref, wd_ref = refs[2 * parts : 2 * parts + 3]
    rest = refs[2 * parts + 3 :]
    g_refs = rest[:parts]
    o_ref, mid_ref, dy_ref, right_ref, out_acc, gmid_acc = rest[parts:]
    j = pl.program_id(0)
    me = me_ref[0]

    @pl.when(j == 0)
    def _():
        for step in range(parts):
            spot = pl.ds(place(me, step, parts, rows), rows)
            mid_ref[spot, :] = m_refs[step][...]
            dy_ref[spot, :] = dy_refs[step][batch]
        out_acc[...] = jnp.zeros_like(out_acc)
        gmid_acc[...] = jnp.zeros_like(gmid_acc)

    mid = mid_ref[...]
    gate = mm(mid, wg_ref[...])
    up = mm(mid, wu_ref[...])
    gh = mm(dy_ref[...], wd_ref[...])
    sig = jax.nn.sigmoid(gate)
    swish = gate * sig
    hidden = (swish * up).astype(BF16)
    gg = (gh * up * sig * (1.0 + gate * (1.0 - sig))).astype(BF16)
    gu = (gh * swish).astype(BF16)
    right_ref[0] = gg
    right_ref[1] = gu
    right_ref[2] = hidden
    gmid_acc[...] += mm(gg, wg_ref[...], NT) + mm(gu, wu_ref[...], NT)
    out_acc[...] += mm(hidden, wd_ref[...], NT)

    @pl.when(j == pl.num_programs(0) - 1)
    def _():
        for step in range(parts):
            spot = pl.ds(place(me, step, parts, rows), rows)
            g_refs[step][...] = gmid_acc[spot, :].astype(BF16)
        o_ref[...] = out_acc[...].astype(BF16)


def ffn(me, ms, dys, w2, batch):
    parts = len(ms)
    rows, d = ms[0].shape
    length = parts * rows
    ff = w2.shape[1] // 3
    cols = min(256, ff)
    steps = ff // cols
    whole = lambda shape: pl.BlockSpec(shape, lambda j: (0, 0))
    weight = lambda c: pl.BlockSpec((d, cols), lambda j, c=c: (0, c * steps + j))
    res = pl.pallas_call(
        functools.partial(ffn_body, parts, rows, batch),
        grid=(steps,),
        in_specs=[spec_smem()]
        + [whole((rows, d))] * parts
        + [pl.BlockSpec(dys[0].shape, lambda j: (0, 0, 0))] * parts
        + [weight(0), weight(1), weight(2)],
        out_specs=[whole((rows, d))] * parts
        + [whole((length, d))] * 3
        + [pl.BlockSpec((3, length, cols), lambda j: (0, 0, j))],
        out_shape=[sds((rows, d), BF16)] * parts
        + [sds((length, d), BF16)] * 3
        + [sds((3, length, ff), BF16)],
        scratch_shapes=[pltpu.VMEM((length, d), F32)] * 2,
        compiler_params=pltpu.CompilerParams(vmem_limit_bytes=VMEM_LIMIT),
        cost_estimate=pl.CostEstimate(
            flops=2 * length * d * ff * 6, bytes_accessed=6 * d * ff, transcendentals=0
        ),
        name="ffn",
    )(me, *ms, *dys, w2, w2, w2)
    return res[:parts], res[parts], res[parts + 1 :]


def turn(left, sources):
    length = sources[0].shape[0]
    for n, source in enumerate(sources):
        left[:, n * length : (n + 1) * length] = source[...].T


def stack(right, sources):
    length = sources[0].shape[0]
    for n, source in enumerate(sources):
        right[n * length : (n + 1) * length, :] = source


def ffn_grads_body(count, *refs):
    mids, dys, rights = refs[:count], refs[count : 2 * count], refs[2 * count : 3 * count]
    out_ref, left, right = refs[3 * count :]
    kind, j = pl.program_id(0), pl.program_id(1)
    pl.when((kind == 0) & (j == 0))(lambda: turn(left, mids))
    pl.when((kind == 2) & (j == 0))(lambda: turn(left, dys))
    stack(right, [ref[0] for ref in rights])
    out_ref[...] = mm(left[...], right[...]).astype(BF16)


def ffn_grads(mids, dys, rights):
    count = len(mids)
    length, d = mids[0].shape
    ff = rights[0].shape[2]
    cols = min(512, ff)
    steps = ff // cols
    whole = pl.BlockSpec((length, d), lambda k, j: (0, 0))
    return pl.pallas_call(
        functools.partial(ffn_grads_body, count),
        grid=(3, steps),
        in_specs=[whole] * (2 * count)
        + [pl.BlockSpec((1, length, cols), lambda k, j: (k, 0, j))] * count,
        out_specs=pl.BlockSpec((d, cols), lambda k, j: (0, k * steps + j)),
        out_shape=sds((d, 3 * ff), BF16),
        scratch_shapes=[
            pltpu.VMEM((d, count * length), BF16),
            pltpu.VMEM((count * length, cols), BF16),
        ],
        compiler_params=pltpu.CompilerParams(vmem_limit_bytes=VMEM_LIMIT),
        cost_estimate=pl.CostEstimate(
            flops=6 * count * length * d * ff, bytes_accessed=6 * d * ff, transcendentals=0
        ),
        name="ffn_grads",
    )(*mids, *dys, *rights)


def attn_grads_body(count, *refs):
    ins, gas = refs[:count], refs[count : 2 * count]
    projs, groups = refs[2 * count : 3 * count], refs[3 * count : 4 * count]
    out_ref, left, right = refs[4 * count :]
    j = pl.program_id(0)
    last = pl.num_programs(0) - 1

    @pl.when(j == 0)
    def _():
        turn(left, ins)

    @pl.when(j < last)
    def _():
        stack(right, [ref[...] for ref in projs])

    @pl.when(j == last)
    def _():
        turn(left, gas)
        stack(right, [ref[...] for ref in groups])

    out_ref[...] = mm(left[...], right[...]).astype(BF16)


def attn_grads(ins, gas, projs, groups):
    count = len(ins)
    length, d = ins[0].shape
    width = groups[0].shape[1]
    whole = pl.BlockSpec((length, d), lambda j: (0, 0))
    return pl.pallas_call(
        functools.partial(attn_grads_body, count),
        grid=(4,),
        in_specs=[whole] * (2 * count)
        + [pl.BlockSpec((length, width), lambda j: (0, jnp.minimum(j, 2)))] * count
        + [pl.BlockSpec((length, width), lambda j: (0, 0))] * count,
        out_specs=pl.BlockSpec((d, width), lambda j: (0, j)),
        out_shape=sds((d, 4 * width), BF16),
        scratch_shapes=[
            pltpu.VMEM((d, count * length), BF16),
            pltpu.VMEM((count * length, width), BF16),
        ],
        compiler_params=pltpu.CompilerParams(vmem_limit_bytes=VMEM_LIMIT),
        cost_estimate=pl.CostEstimate(
            flops=8 * count * length * d * width, bytes_accessed=8 * d * width, transcendentals=0
        ),
        name="attn_grads",
    )(*ins, *gas, *projs, *groups)


def band_sum(values, length):
    lane = lax.broadcasted_iota(jnp.int32, (8, 128), 1)
    lane = jnp.where(lane >= 64, lane - 128, lane)
    acc = jnp.zeros((8, 128), F32)
    tiles = length // 128
    for s in range(length // 8):
        back = (128 - 8 * s % 128) % 128
        low, high = 8 * s - CENTER, 8 * s + 7 + CENTER
        first, last = max(low, 0) // 128, min(high, length - 1) // 128
        for tile in range(first, last + 1):
            piece = values[8 * s : 8 * s + 8, tile * 128 : (tile + 1) * 128]
            if back:
                piece = pltpu.roll(piece, back, 1)
            start, stop = tile * 128 - 8 * s, tile * 128 + 128 - 8 * s
            if low < tile * 128 or high >= tile * 128 + 128:
                piece = jnp.where((lane >= start) & (lane < stop), piece, 0.0)
            acc = acc + piece
    return acc


def attn_bwd_body(cfg, me_ref, mix_ref, *refs):
    parts, rows, heads, size = cfg
    ga_refs = refs[:parts]
    (w_ref, band_ref, segc_ref, segr_ref, ggain_ref, gains_ref, normed_ref, qkv_ref, z_ref,
     p_ref, ho_ref) = refs[parts : parts + 11]
    outs = refs[parts + 11 :]
    gi_refs = outs[:parts]
    (gaa_ref, gproj_ref, again_ref, ggrad_ref, kern_ref, mixg_ref, gin_scr, diag_scr) = outs[parts:]
    length = parts * rows
    width = heads * size
    me = me_ref[0]
    for step in range(parts):
        gaa_ref[pl.ds(place(me, step, parts, rows), rows), :] = ga_refs[step][...]
    gin_scr[:, :width] = mm(gaa_ref[...], w_ref[:, 3 * width : 4 * width])
    same, allow = masks(segc_ref[...], segr_ref[...], length)
    scale = 1.0 / math.sqrt(size)
    for pair in range(heads // 2):
        gmix = []
        for a in range(2):
            h = 2 * pair + a
            lanes = slice(h * size, (h + 1) * size)
            gg = gin_scr[:, lanes]
            normed, inv_std = head_norm(ho_ref[h])
            ggrad_ref[:, lanes] = jnp.sum(gg * normed, axis=0, keepdims=True)
            u = gg * ggain_ref[:, lanes]
            gh = inv_std * (
                u
                - jnp.mean(u, axis=-1, keepdims=True)
                - normed * jnp.mean(u * normed, axis=-1, keepdims=True)
            )
            gh = gh.astype(BF16)
            v = qkv_ref[:, 2 * width + h * size : 2 * width + (h + 1) * size]
            gmix.append(mm(gh, v, NT))
            mixed = (
                mix_ref[4 * pair + 2 * a] * p_ref[2 * pair]
                + mix_ref[4 * pair + 2 * a + 1] * p_ref[2 * pair + 1]
            ).astype(BF16)
            gproj_ref[:, 2 * width + h * size : 2 * width + (h + 1) * size] = mm(
                mixed, gh, TN
            ).astype(BF16)
        for b in range(2):
            h = 2 * pair + b
            p = p_ref[h]
            for a in range(2):
                mixg_ref[4 * pair + 2 * a + b : 4 * pair + 2 * a + b + 1, :] = jnp.sum(
                    gmix[a] * p, axis=0, keepdims=True
                )
            gp = mix_ref[4 * pair + b] * gmix[0] + mix_ref[4 * pair + 2 + b] * gmix[1]
            gl = p * (gp - jnp.sum(gp * p, axis=-1, keepdims=True))
            glt = gl.T.astype(BF16)
            z = z_ref[h].astype(F32)
            gz = jnp.zeros((length, length), F32)
            for a in range(CQ):
                gz = gz + mm(shift_rows(gl, -a, same), band_ref[h * CQ + a], NT)
                diag_scr[h * CQ + a] = band_sum(mm(glt, shift_rows(z, a, same)), length)
            gs = jnp.where(allow, gz, 0.0).astype(BF16)
            q = qkv_ref[:, h * size : (h + 1) * size]
            k = qkv_ref[:, width + h * size : width + (h + 1) * size]
            gproj_ref[:, h * size : (h + 1) * size] = (mm(gs, k) * scale).astype(BF16)
            gproj_ref[:, width + h * size : width + (h + 1) * size] = (
                mm(gs, q, TN) * scale
            ).astype(BF16)
    taps = diag_scr[:, 0, :]
    for r in range(1, 8):
        taps = taps + pltpu.roll(diag_scr[:, r, :], 128 - r, 1)
    kern_ref[...] = taps
    gin_scr[...] = mm(gproj_ref[...], w_ref[:, : 3 * width], NT)
    again_ref[...] = (
        jnp.sum(gin_scr[...] * normed_ref[...].astype(F32), axis=0, keepdims=True) / gains_ref[0:1]
    )
    for step in range(parts):
        gi_refs[step][...] = gin_scr[pl.ds(place(me, step, parts, rows), rows), :].astype(BF16)


def attn_bwd(me, mix, gas, w1, band, segc, segr, ggain, gains, saved, heads, size):
    parts = len(gas)
    rows, d = gas[0].shape
    length, width = parts * rows, heads * size
    outs = (
        [sds((rows, d), BF16)] * parts
        + [
            sds((length, d), BF16),
            sds((length, 3 * width), BF16),
            sds((1, d), F32),
            sds((1, width), F32),
            sds((heads * CQ, 128), F32),
            sds((2 * heads, length), F32),
        ]
    )
    res = call(
        functools.partial(attn_bwd_body, (parts, rows, heads, size)),
        outs,
        [me, mix, *gas, w1, band, segc, segr, ggain, gains, *saved],
        scratch=[pltpu.VMEM((length, d), F32), pltpu.VMEM((heads * CQ, 8, 128), F32)],
        smem=2,
        flops=2 * length * d * width * 4 + 2 * heads * (2 * CQ + 4) * length**3,
        name="attn_bwd",
    )
    return res[:parts], res[parts:]


def shift_mp(part, step, size):
    return lax.ppermute(part, "mp", [(i, (i + step) % size) for i in range(size)])


def gather_mp(part, size):
    if size != 4:
        return [part] + [shift_mp(part, step, size) for step in range(1, size)]
    back, ahead = shift_mp(part, 1, size), shift_mp(part, -1, size)
    return [part, back, shift_mp(back, 1, size), ahead]


def scatter_first(pieces, size):
    if size != 4:
        return [pieces[0]] + [shift_mp(pieces[step], -step, size) for step in range(1, size)], None
    far = shift_mp(pieces[2], -1, size)
    ahead = shift_mp(pieces[3], 1, size)
    return [pieces[0], ahead], (pieces[1].astype(F32) + far.astype(F32)).astype(BF16)


def scatter_second(first, size):
    here, near = first
    return here if near is None else here + [shift_mp(near, -1, size)]


def scatter_mp(pieces, size):
    return scatter_second(scatter_first(pieces, size), size)


def take(values, index, axis):
    return lax.dynamic_index_in_dim(values, index, axis, keepdims=False)


def scatter_dp(whole, extra, size):
    rows, cols = whole.shape[0] // size, whole.shape[1]
    if size != 8:
        whole = lax.psum_scatter(whole, "dp", scatter_dimension=0, tiled=True).astype(F32)
        return whole, lax.psum(extra, "dp"), whole
    me = lax.axis_index("dp")
    core, chip = me % 2, me // 2
    pieces = whole.reshape(size // 2, 2, rows, cols)
    keep, give = take(pieces, core, 1), take(pieces, 1 - core, 1)
    pairs = [(i, i ^ 1) for i in range(size)]
    keep = (keep.astype(F32) + lax.ppermute(give, "dp", pairs).astype(F32)).astype(BF16)
    extra = extra + lax.ppermute(extra, "dp", pairs)
    count = extra.shape[0]
    high = extra.astype(BF16)
    low = (extra - high.astype(F32)).astype(BF16)
    tail = jnp.concatenate([high, low])
    tail = jnp.pad(tail, (0, -tail.shape[0] % (16 * cols))).reshape(-1, cols)
    total = take(keep, chip, 0).astype(F32)
    for step in (3, 1, 2):
        send = jnp.concatenate([take(keep, chip ^ step, 0), tail])
        got = lax.ppermute(send, "dp", [(i, i ^ (2 * step)) for i in range(size)]).astype(F32)
        total = total + got[:rows]
        flat = got[rows:].reshape(-1)
        extra = extra + (flat[:count] + flat[count : 2 * count])
    return total, extra, keep


def shards(
    block_input,
    out_grad,
    doc_lengths,
    attn_gain,
    qkv_weight,
    conv_kernel,
    head_mixing,
    group_gain,
    out_weight,
    mlp_gain,
    gate_weight,
    up_weight,
    down_weight,
):
    batches = block_input.shape[0]
    rows = block_input.shape[2]
    mp, dp = lax.axis_size("mp"), lax.axis_size("dp")
    length = rows * mp
    heads = conv_kernel.shape[0]
    width = qkv_weight.shape[2]
    size = width // heads
    local_d = attn_gain.shape[0]
    me = lax.axis_index("mp").astype(jnp.int32).reshape(1)
    mix = head_mixing.reshape(-1)
    ggain = group_gain.astype(F32)[None]

    gains_cols = jnp.pad(jnp.stack([attn_gain, mlp_gain], axis=1), ((0, 0), (0, 126)))
    pack1 = jnp.concatenate(
        [qkv_weight[0], qkv_weight[1], qkv_weight[2], out_weight.T, gains_cols], axis=1
    )
    pack2 = jnp.concatenate([gate_weight, up_weight, down_weight.T], axis=1)
    w1 = lax.all_gather(pack1, "dp", axis=0, tiled=True)
    w2 = lax.all_gather(pack2, "dp", axis=0, tiled=True)

    offset = (
        jnp.arange(length, dtype=jnp.int32)[None, :]
        - jnp.arange(length, dtype=jnp.int32)[:, None]
        + CENTER
    )
    band = jnp.zeros((heads * CQ, length, length), F32)
    taps = conv_kernel.reshape(heads * CQ, CK)
    for b in range(CK):
        band = jnp.where(offset[None] == b, taps[:, b][:, None, None], band)
    band = band.astype(BF16)

    barrier = lambda value, *others: lax.optimization_barrier((value, others))[0]
    xs = gather_mp(block_input[:, 0], mp)
    dys = gather_mp(barrier(out_grad[:, 0], xs), mp)
    segs, front = [], []
    for batch in range(batches):
        segment = segment_ids(doc_lengths[batch, 0], length)
        segs.append((segment[:, None], segment[None, :]))
        front.append(attn_fwd(me, mix, xs, w1, band, *segs[batch], ggain, heads, size, batch))
    mids = []
    for batch in range(batches):
        pieces, saved = front[batch]
        x = barrier(block_input[batch, 0], dys)
        mids.append(mid_step(x, saved[-1], scatter_mp(pieces, mp)))
    middle = []
    for batch in range(batches):
        parts = gather_mp(mids[batch][1], mp)
        parts = barrier(parts, mids[-1])
        middle.append((mids[batch][0], *ffn(me, parts, dys, w2, batch)))

    firsts = [scatter_first(m[1], mp) for m in middle]
    rights = barrier([m[3][2] for m in middle], firsts[0])
    grads2 = ffn_grads([m[3][0] for m in middle], [m[3][1] for m in middle], rights)
    share2 = lax.psum_scatter(grads2, "dp", scatter_dimension=0, tiled=True)
    turned = []
    for batch in range(batches):
        got = barrier(scatter_second(firsts[batch], mp), grads2)
        turned.append(mid_back(middle[batch][0], out_grad[batch, 0], front[batch][1][-1], got))
    gass = [gather_mp(turned[n][1], mp) for n in range(batches)]
    back, kept, head_total = [], [], None
    for batch in range(batches):
        normed, qkv, z, probs, ho, grouped, gains = front[batch][1]
        ghid, ga, mlp_part = turned[batch]
        gas = barrier(gass[batch], turned[-1], grads2)
        gi_pieces, (ga_all, gproj, again, ggrad, kern, mixg) = attn_bwd(
            me, mix, gas, w1, band, *segs[batch], ggain, gains, [normed, qkv, z, probs, ho], heads, size
        )
        back.append((ghid, scatter_first(gi_pieces, mp)))
        small = (again, mlp_part, ggrad, kern, jnp.sum(mixg, axis=1))
        head_total = small if head_total is None else jax.tree.map(jnp.add, head_total, small)
        kept.append((normed, ga_all, gproj, grouped))

    o_parts = barrier(jnp.stack([m[2] for m in middle]), share2)
    mlp_out = lax.psum_scatter(o_parts, "mp", scatter_dimension=1, tiled=True)
    kept = barrier(kept, share2, back[0][1])
    again, mlp_part, ggrad, kern, mixg = head_total
    d = again.shape[1]
    kern = jnp.roll(kern, CK - 1 - CENTER, axis=1)[:, :CK][:, ::-1]
    gain_grads = jnp.concatenate([again, mlp_part]).reshape(-1, 128)
    gain_grads = functools.reduce(
        jnp.add, [gain_grads] + [shift_mp(gain_grads, step, mp) for step in range(1, mp)]
    )
    extra = jnp.concatenate([gain_grads.reshape(-1), ggrad[0], kern.reshape(-1), mixg])
    grads1 = attn_grads(*(list(group) for group in zip(*kept)))
    share1, extra, keep = scatter_dp(grads1, extra, dp)
    input_grads = []
    for batch in range(batches):
        ghid, first = back[batch]
        got = barrier(scatter_second(first, mp), keep)
        input_grads.append(last_step(block_input[batch, 0], ghid, front[batch][1][-1], got))
    outputs = (jnp.stack([m[0] for m in middle]) + mlp_out.astype(F32)).astype(BF16)
    share2 = share2.astype(F32)
    gain_grads = extra[: 2 * d].reshape(2, dp, local_d)
    gain_grads = take(gain_grads, lax.axis_index("dp"), 1)
    ggrad, kern, mixg = jnp.split(extra[2 * d :], [width, width + heads * CQ * CK])
    kernel_grad = kern.reshape(heads, CQ, CK)
    mixing_grad = mixg.reshape(heads // 2, 2, 2)
    ff = gate_weight.shape[1]
    return (
        outputs[:, None],
        jnp.stack(input_grads)[:, None],
        gain_grads[0],
        jnp.stack([share1[:, c * width : (c + 1) * width] for c in range(3)]),
        kernel_grad,
        mixing_grad,
        ggrad,
        share1[:, 3 * width :].T,
        gain_grads[1],
        share2[:, :ff],
        share2[:, ff : 2 * ff],
        share2[:, 2 * ff :].T,
    )


def solution(mesh):
    return jax.shard_map(
        shards,
        mesh=mesh,
        in_specs=(
            P(None, "dp", "mp", None),
            P(None, "dp", "mp", None),
            P(None, "dp", None),
            P("dp"),
            P(None, "dp", "mp"),
            P("mp", None, None),
            P("mp", None, None),
            P("mp"),
            P("mp", "dp"),
            P("dp"),
            P("dp", "mp"),
            P("dp", "mp"),
            P("mp", "dp"),
        ),
        out_specs=(
            P(None, "dp", "mp", None),
            P(None, "dp", "mp", None),
            P("dp"),
            P(None, "dp", "mp"),
            P("mp", None, None),
            P("mp", None, None),
            P("mp"),
            P("mp", "dp"),
            P("dp"),
            P("dp", "mp"),
            P("dp", "mp"),
            P("mp", "dp"),
        ),
        check_vma=False,
    )
```

```python
import functools
import math

import jax
import jax.numpy as jnp
from jax import lax
from jax.experimental import pallas as pl
from jax.experimental.pallas import tpu as pltpu
from jax.sharding import PartitionSpec as P

CQ = 6
CK = 11
CENTER = CK // 2
EPS = 1e-05
F32 = jnp.float32
BF16 = jnp.bfloat16
VMEM_LIMIT = 58 * 1024 * 1024

NN = (((1,), (0,)), ((), ()))
NT = (((1,), (1,)), ((), ()))
TN = (((0,), (0,)), ((), ()))


def mm(left, right, dims=NN):
    return lax.dot_general(left, right, dims, preferred_element_type=F32)


def spec_vmem():
    return pl.BlockSpec(memory_space=pltpu.VMEM)


def spec_smem():
    return pl.BlockSpec(memory_space=pltpu.SMEM)


def spec_any():
    return pl.BlockSpec(memory_space=pl.ANY)


def begin(sems, *pairs):
    copies = [pltpu.make_async_copy(src, dst, sems.at[n]) for n, (src, dst) in enumerate(pairs)]
    for copy in copies:
        copy.start()
    return copies


def call(body, outs, ins, scratch=(), smem=0, flops=0, name=None, far_in=(), far_out=()):
    nbytes = sum(math.prod(a.shape) * a.dtype.itemsize for a in list(ins) + list(outs))
    return pl.pallas_call(
        body,
        out_shape=outs,
        in_specs=[
            spec_smem() if n < smem else spec_any() if n in far_in else spec_vmem()
            for n in range(len(ins))
        ],
        out_specs=[spec_any() if n in far_out else spec_vmem() for n in range(len(outs))],
        scratch_shapes=list(scratch),
        compiler_params=pltpu.CompilerParams(vmem_limit_bytes=VMEM_LIMIT),
        cost_estimate=pl.CostEstimate(flops=flops, bytes_accessed=nbytes, transcendentals=0),
        name=name,
    )(*ins)


def sds(shape, dtype):
    return jax.ShapeDtypeStruct(shape, dtype)


def pack_attn_body(qkv_ref, out_ref, gains_ref, pack_ref):
    width = qkv_ref.shape[2]
    for c in range(3):
        pack_ref[:, c * width : (c + 1) * width] = qkv_ref[c]
    pack_ref[:, 3 * width : 4 * width] = out_ref[...]
    rows = qkv_ref.shape[1]
    at = lax.broadcasted_iota(jnp.int32, (128, rows), 0)
    first, second = gains_ref[0:1].astype(F32), gains_ref[1:2].astype(F32)
    gains = jnp.where(at == 0, first, jnp.where(at == 1, second, 0.0))
    pack_ref[:, 4 * width :] = gains.T.astype(BF16)


def pack_attn(qkv, out, first, second):
    _, rows, width = qkv.shape
    if rows % 16:
        gains = jnp.pad(jnp.stack([first, second], axis=1), ((0, 0), (0, 126)))
        return jnp.concatenate([qkv[0], qkv[1], qkv[2], out.T, gains], axis=1)
    return call(
        pack_attn_body,
        [sds((rows, 4 * width + 128), BF16)],
        [qkv, out.T, jnp.stack([first, second])],
        name="pack_attn",
    )[0]


def segment_ids(lengths, length):
    ends = jnp.cumsum(lengths)
    places = jnp.arange(length, dtype=jnp.int32)
    return jnp.sum((places[:, None] >= ends[None, :]).astype(jnp.int32), axis=1)


def place(me, step, parts, rows):
    return pl.multiple_of(lax.rem(me - step + parts, parts) * rows, rows)


def masks(seg_col, seg_row, length):
    same = seg_col == seg_row
    row = lax.broadcasted_iota(jnp.int32, (length, length), 0)
    col = lax.broadcasted_iota(jnp.int32, (length, length), 1)
    return same, same & (col <= row)


def shift_rows(values, shift, same):
    if shift == 0:
        return values.astype(BF16)
    length = values.shape[0]
    return jnp.where(same, pltpu.roll(values, shift % length, 0), 0.0).astype(BF16)


def head_norm(heads_out):
    centered = heads_out - jnp.mean(heads_out, axis=-1, keepdims=True)
    inv_std = lax.rsqrt(jnp.mean(centered * centered, axis=-1, keepdims=True) + EPS)
    return centered * inv_std, inv_std


def attn_fwd_body(cfg, me_ref, mix_ref, *refs):
    parts, rows, heads, size, batch = cfg
    x_refs = refs[:parts]
    w_ref, band_ref, segc_ref, segr_ref, ggain_ref = refs[parts : parts + 5]
    outs = refs[parts + 5 :]
    att_refs = outs[:parts]
    normed_ref, qkv_ref, z_ref, p_ref, ho_ref, grouped_ref, gains_ref, att_scr = outs[parts:]
    length = parts * rows
    width = heads * size
    me = me_ref[0]
    gains = w_ref[:, 4 * width :].astype(F32).T
    gains_ref[...] = gains[:8]
    gain = gains[0:1]
    for step in range(parts):
        x = x_refs[step][batch].astype(F32)
        r1 = lax.rsqrt(jnp.mean(x * x, axis=-1, keepdims=True) + EPS)
        normed_ref[pl.ds(place(me, step, parts, rows), rows), :] = (x * r1 * gain).astype(BF16)
    qkv_ref[...] = mm(normed_ref[...], w_ref[:, : 3 * width]).astype(BF16)
    same, allow = masks(segc_ref[...], segr_ref[...], length)
    scale = 1.0 / math.sqrt(size)
    for pair in range(heads // 2):
        probs = []
        for b in range(2):
            h = 2 * pair + b
            q = qkv_ref[:, h * size : (h + 1) * size]
            k = qkv_ref[:, width + h * size : width + (h + 1) * size]
            z = jnp.where(allow, mm(q, k, NT) * scale, 0.0)
            z_ref[h] = z.astype(BF16)
            acc = jnp.zeros((length, length), F32)
            for a in range(CQ):
                acc = acc + mm(shift_rows(z, a, same), band_ref[h * CQ + a])
            logits = jnp.where(allow, acc, -jnp.inf)
            e = jnp.exp(logits - jnp.max(logits, axis=-1, keepdims=True))
            p = e * (1.0 / jnp.sum(e, axis=-1, keepdims=True))
            p_ref[h] = p
            probs.append(p)
        for a in range(2):
            h = 2 * pair + a
            mixed = (
                mix_ref[4 * pair + 2 * a] * probs[0] + mix_ref[4 * pair + 2 * a + 1] * probs[1]
            ).astype(BF16)
            v = qkv_ref[:, 2 * width + h * size : 2 * width + (h + 1) * size]
            ho = mm(mixed, v)
            ho_ref[h] = ho
            normed, _ = head_norm(ho)
            grouped_ref[:, h * size : (h + 1) * size] = (
                normed * ggain_ref[:, h * size : (h + 1) * size]
            ).astype(BF16)
    att_scr[...] = mm(grouped_ref[...], w_ref[:, 3 * width : 4 * width], NT)
    for step in range(parts):
        att_refs[step][...] = att_scr[pl.ds(place(me, step, parts, rows), rows), :].astype(BF16)


def attn_fwd(me, mix, xs, w1, band, segc, segr, ggain, heads, size, batch):
    parts = len(xs)
    _, rows, d = xs[0].shape
    length, width = parts * rows, heads * size
    outs = (
        [sds((rows, d), BF16)] * parts
        + [
            sds((length, d), BF16),
            sds((length, 3 * width), BF16),
            sds((heads, length, length), BF16),
            sds((heads, length, length), F32),
            sds((heads, length, size), F32),
            sds((length, width), BF16),
            sds((8, d), F32),
        ]
    )
    res = call(
        functools.partial(attn_fwd_body, (parts, rows, heads, size, batch)),
        outs,
        [me, mix, *xs, w1, band, segc, segr, ggain],
        scratch=[pltpu.VMEM((length, d), F32)],
        smem=2,
        flops=2 * length * d * width * 4 + 2 * heads * (CQ + 2) * length**3,
        name="attn_fwd",
    )
    return res[:parts], res[parts:]


def tail_rms(values, gain):
    r = lax.rsqrt(jnp.mean(values * values, axis=-1, keepdims=True) + EPS)
    return values * r, r


def rms_back(grad, normal, r, gain):
    u = grad * gain
    return r * (u - normal * jnp.mean(u * normal, axis=-1, keepdims=True))


def total(refs):
    acc = refs[0][...].astype(F32)
    for ref in refs[1:]:
        acc = acc + ref[...].astype(F32)
    return acc


def mid_body(parts, *refs):
    x_ref, gains_ref = refs[:2]
    hid_ref, mid_ref = refs[2 + parts :]
    hidden_in = x_ref[...].astype(F32) + total(refs[2 : 2 + parts])
    hid_ref[...] = hidden_in
    normal, _ = tail_rms(hidden_in, None)
    mid_ref[...] = (normal * gains_ref[1:2]).astype(BF16)


def mid_step(x, gains, pieces):
    return call(
        functools.partial(mid_body, len(pieces)),
        [sds(x.shape, F32), sds(x.shape, BF16)],
        [x, gains, *pieces],
        name="mid_step",
    )


def mid_back_body(parts, *refs):
    hid_ref, dy_ref, gains_ref = refs[:3]
    ghid_ref, ga_ref, gain_ref = refs[3 + parts :]
    gain = gains_ref[1:2]
    normal, r = tail_rms(hid_ref[...], None)
    grad = total(refs[3 : 3 + parts])
    gain_ref[...] = jnp.sum(grad * normal, axis=0, keepdims=True)
    ghid = dy_ref[...].astype(F32) + rms_back(grad, normal, r, gain)
    ghid_ref[...] = ghid
    ga_ref[...] = ghid.astype(BF16)


def mid_back(hid, dy, gains, pieces):
    return call(
        functools.partial(mid_back_body, len(pieces)),
        [sds(hid.shape, F32), sds(hid.shape, BF16), sds((1, hid.shape[1]), F32)],
        [hid, dy, gains, *pieces],
        name="mid_back",
    )


def last_body(parts, *refs):
    x_ref, ghid_ref, gains_ref = refs[:3]
    out_ref = refs[3 + parts]
    normal, r = tail_rms(x_ref[...].astype(F32), None)
    grad = total(refs[3 : 3 + parts])
    out_ref[...] = ghid_ref[...] + rms_back(grad, normal, r, gains_ref[0:1])


def last_step(x, ghid, gains, pieces):
    return call(
        functools.partial(last_body, len(pieces)),
        [sds(x.shape, F32)],
        [x, ghid, gains, *pieces],
        name="last_step",
    )[0]


def ffn_body(parts, rows, batch, me_ref, *refs):
    m_refs, dy_hbm = refs[:parts], refs[parts : 2 * parts]
    w_hbm = refs[2 * parts]
    rest = refs[2 * parts + 1 :]
    g_refs = rest[:parts]
    o_ref, mid_ref, dy_ref, right_ref, gmid, wg_ref, wu_ref, wd_ref, sems = rest[parts:]
    me = me_ref[0]
    ff = wg_ref.shape[1]
    spots = [pl.ds(place(me, step, parts, rows), rows) for step in range(parts)]
    copies = begin(
        sems,
        (w_hbm.at[:, pl.ds(0, ff)], wg_ref),
        (w_hbm.at[:, pl.ds(ff, ff)], wu_ref),
        *[(dy_hbm[step].at[batch], dy_ref.at[spots[step]]) for step in range(parts)],
        (w_hbm.at[:, pl.ds(2 * ff, ff)], wd_ref),
    )
    for step in range(parts):
        mid_ref[spots[step], :] = m_refs[step][...]
    mid = mid_ref[...]
    cols = min(512, ff)
    copies[0].wait()
    gates = [mm(mid, wg_ref[:, c : c + cols]) for c in range(0, ff, cols)]
    copies[1].wait()
    ups = [mm(mid, wu_ref[:, c : c + cols]) for c in range(0, ff, cols)]
    for copy in copies[2:]:
        copy.wait()
    for n, (gate, up) in enumerate(zip(gates, ups)):
        at = slice(n * cols, (n + 1) * cols)
        gh = mm(dy_ref[...], wd_ref[:, at])
        sig = jax.nn.sigmoid(gate)
        swish = gate * sig
        right_ref[0, :, at] = (gh * up * sig * (1.0 + gate * (1.0 - sig))).astype(BF16)
        right_ref[1, :, at] = (gh * swish).astype(BF16)
        right_ref[2, :, at] = (swish * up).astype(BF16)
    gmid[...] = mm(right_ref[0], wg_ref[...], NT) + mm(right_ref[1], wu_ref[...], NT)
    o_ref[...] = mm(right_ref[2], wd_ref[...], NT).astype(BF16)
    for step in range(parts):
        g_refs[step][...] = gmid[spots[step], :].astype(BF16)


def ffn(me, ms, dys, w2, batch):
    parts = len(ms)
    rows, d = ms[0].shape
    length = parts * rows
    ff = w2.shape[1] // 3
    res = call(
        functools.partial(ffn_body, parts, rows, batch),
        [sds((rows, d), BF16)] * parts + [sds((length, d), BF16)] * 3 + [sds((3, length, ff), BF16)],
        [me, *ms, *dys, w2],
        scratch=[pltpu.VMEM((length, d), F32)]
        + [pltpu.VMEM((d, ff), BF16)] * 3
        + [pltpu.SemaphoreType.DMA((3 + parts,))],
        smem=1,
        far_in=range(1 + parts, 2 + 2 * parts),
        flops=2 * length * d * ff * 6,
        name="ffn",
    )
    return res[:parts], res[parts], res[parts + 1 :]


def turn(left, sources):
    length = sources[0].shape[0]
    for n, source in enumerate(sources):
        left[:, n * length : (n + 1) * length] = source[...].T


def stack(right, sources):
    length = sources[0].shape[0]
    for n, source in enumerate(sources):
        right[n * length : (n + 1) * length, :] = source


def ffn_grads_body(count, *refs):
    mids, dys, rights = refs[:count], refs[count : 2 * count], refs[2 * count : 3 * count]
    out_ref, left, right = refs[3 * count :]
    kind, j = pl.program_id(0), pl.program_id(1)
    pl.when((kind == 0) & (j == 0))(lambda: turn(left, mids))
    pl.when((kind == 2) & (j == 0))(lambda: turn(left, dys))
    stack(right, [ref[0] for ref in rights])
    out_ref[...] = mm(left[...], right[...]).astype(BF16)


def ffn_grads(mids, dys, rights):
    count = len(mids)
    length, d = mids[0].shape
    ff = rights[0].shape[2]
    cols = min(512, ff)
    steps = ff // cols
    whole = pl.BlockSpec((length, d), lambda k, j: (0, 0))
    return pl.pallas_call(
        functools.partial(ffn_grads_body, count),
        grid=(3, steps),
        in_specs=[whole] * (2 * count)
        + [pl.BlockSpec((1, length, cols), lambda k, j: (k, 0, j))] * count,
        out_specs=pl.BlockSpec((d, cols), lambda k, j: (0, k * steps + j)),
        out_shape=sds((d, 3 * ff), BF16),
        scratch_shapes=[
            pltpu.VMEM((d, count * length), BF16),
            pltpu.VMEM((count * length, cols), BF16),
        ],
        compiler_params=pltpu.CompilerParams(vmem_limit_bytes=VMEM_LIMIT),
        cost_estimate=pl.CostEstimate(
            flops=6 * count * length * d * ff, bytes_accessed=6 * d * ff, transcendentals=0
        ),
        name="ffn_grads",
    )(*mids, *dys, *rights)


def attn_grads_body(count, *refs):
    ins, gas = refs[:count], refs[count : 2 * count]
    projs, groups = refs[2 * count : 3 * count], refs[3 * count : 4 * count]
    out_ref, left, right = refs[4 * count :]
    j = pl.program_id(0)
    last = pl.num_programs(0) - 1

    @pl.when(j == 0)
    def _():
        turn(left, ins)

    @pl.when(j < last)
    def _():
        stack(right, [ref[...] for ref in projs])

    @pl.when(j == last)
    def _():
        turn(left, gas)
        stack(right, [ref[...] for ref in groups])

    out_ref[...] = mm(left[...], right[...]).astype(BF16)


def attn_grads(ins, gas, projs, groups):
    count = len(ins)
    length, d = ins[0].shape
    width = groups[0].shape[1]
    whole = pl.BlockSpec((length, d), lambda j: (0, 0))
    return pl.pallas_call(
        functools.partial(attn_grads_body, count),
        grid=(4,),
        in_specs=[whole] * (2 * count)
        + [pl.BlockSpec((length, width), lambda j: (0, jnp.minimum(j, 2)))] * count
        + [pl.BlockSpec((length, width), lambda j: (0, 0))] * count,
        out_specs=pl.BlockSpec((d, width), lambda j: (0, j)),
        out_shape=sds((d, 4 * width), BF16),
        scratch_shapes=[
            pltpu.VMEM((d, count * length), BF16),
            pltpu.VMEM((count * length, width), BF16),
        ],
        compiler_params=pltpu.CompilerParams(vmem_limit_bytes=VMEM_LIMIT),
        cost_estimate=pl.CostEstimate(
            flops=8 * count * length * d * width, bytes_accessed=8 * d * width, transcendentals=0
        ),
        name="attn_grads",
    )(*ins, *gas, *projs, *groups)


def band_sum(values, length):
    lane = lax.broadcasted_iota(jnp.int32, (8, 128), 1)
    lane = jnp.where(lane >= 64, lane - 128, lane)
    acc = jnp.zeros((8, 128), F32)
    tiles = length // 128
    for s in range(length // 8):
        back = (128 - 8 * s % 128) % 128
        low, high = 8 * s - CENTER, 8 * s + 7 + CENTER
        first, last = max(low, 0) // 128, min(high, length - 1) // 128
        for tile in range(first, last + 1):
            piece = values[8 * s : 8 * s + 8, tile * 128 : (tile + 1) * 128]
            if back:
                piece = pltpu.roll(piece, back, 1)
            start, stop = tile * 128 - 8 * s, tile * 128 + 128 - 8 * s
            if low < tile * 128 or high >= tile * 128 + 128:
                piece = jnp.where((lane >= start) & (lane < stop), piece, 0.0)
            acc = acc + piece
    return acc


def attn_bwd_body(cfg, me_ref, mix_ref, *refs):
    parts, rows, heads, size = cfg
    ga_refs = refs[:parts]
    (w_hbm, band_hbm, segc_ref, segr_ref, ggain_ref, gains_ref, normed_hbm, qkv_hbm, z_hbm,
     p_hbm, ho_hbm) = refs[parts : parts + 11]
    outs = refs[parts + 11 :]
    gi_refs = outs[:parts]
    (gaa_ref, gproj_ref, again_ref, ggrad_ref, kern_ref, mixg_ref, gin_scr, diag_scr,
     wo_ref, wq_ref, band_ref, normed_ref, qkv_ref, z_ref, p_ref, ho_ref, sems) = outs[parts:]
    length = parts * rows
    width = heads * size
    me = me_ref[0]
    copies = begin(
        sems,
        (w_hbm.at[:, pl.ds(3 * width, width)], wo_ref),
        (ho_hbm, ho_ref),
        (qkv_hbm, qkv_ref),
        (p_hbm, p_ref),
        (z_hbm, z_ref),
        *[(band_hbm.at[pl.ds(h * CQ, CQ)], band_ref.at[pl.ds(h * CQ, CQ)]) for h in range(heads)],
        (w_hbm.at[:, pl.ds(0, 3 * width)], wq_ref),
        (normed_hbm, normed_ref),
    )
    for step in range(parts):
        gaa_ref[pl.ds(place(me, step, parts, rows), rows), :] = ga_refs[step][...]
    copies[0].wait()
    gin_scr[:, :width] = mm(gaa_ref[...], wo_ref[...])
    for copy in copies[1:5]:
        copy.wait()
    same, allow = masks(segc_ref[...], segr_ref[...], length)
    scale = 1.0 / math.sqrt(size)
    for pair in range(heads // 2):
        gmix = []
        for a in range(2):
            h = 2 * pair + a
            lanes = slice(h * size, (h + 1) * size)
            gg = gin_scr[:, lanes]
            normed, inv_std = head_norm(ho_ref[h])
            ggrad_ref[:, lanes] = jnp.sum(gg * normed, axis=0, keepdims=True)
            u = gg * ggain_ref[:, lanes]
            gh = inv_std * (
                u
                - jnp.mean(u, axis=-1, keepdims=True)
                - normed * jnp.mean(u * normed, axis=-1, keepdims=True)
            )
            gh = gh.astype(BF16)
            v = qkv_ref[:, 2 * width + h * size : 2 * width + (h + 1) * size]
            gmix.append(mm(gh, v, NT))
            mixed = (
                mix_ref[4 * pair + 2 * a] * p_ref[2 * pair]
                + mix_ref[4 * pair + 2 * a + 1] * p_ref[2 * pair + 1]
            ).astype(BF16)
            gproj_ref[:, 2 * width + h * size : 2 * width + (h + 1) * size] = mm(
                mixed, gh, TN
            ).astype(BF16)
        for b in range(2):
            h = 2 * pair + b
            p = p_ref[h]
            for a in range(2):
                mixg_ref[4 * pair + 2 * a + b : 4 * pair + 2 * a + b + 1, :] = jnp.sum(
                    gmix[a] * p, axis=0, keepdims=True
                )
            gp = mix_ref[4 * pair + b] * gmix[0] + mix_ref[4 * pair + 2 + b] * gmix[1]
            gl = p * (gp - jnp.sum(gp * p, axis=-1, keepdims=True))
            glt = gl.T.astype(BF16)
            z = z_ref[h].astype(F32)
            copies[5 + h].wait()
            gz = jnp.zeros((length, length), F32)
            for a in range(CQ):
                gz = gz + mm(shift_rows(gl, -a, same), band_ref[h * CQ + a], NT)
                diag_scr[h * CQ + a] = band_sum(mm(glt, shift_rows(z, a, same)), length)
            gs = jnp.where(allow, gz, 0.0).astype(BF16)
            q = qkv_ref[:, h * size : (h + 1) * size]
            k = qkv_ref[:, width + h * size : width + (h + 1) * size]
            gproj_ref[:, h * size : (h + 1) * size] = (mm(gs, k) * scale).astype(BF16)
            gproj_ref[:, width + h * size : width + (h + 1) * size] = (
                mm(gs, q, TN) * scale
            ).astype(BF16)
    taps = diag_scr[:, 0, :]
    for r in range(1, 8):
        taps = taps + pltpu.roll(diag_scr[:, r, :], 128 - r, 1)
    kern_ref[...] = taps
    copies[-2].wait()
    gin_scr[...] = mm(gproj_ref[...], wq_ref[...], NT)
    copies[-1].wait()
    again_ref[...] = (
        jnp.sum(gin_scr[...] * normed_ref[...].astype(F32), axis=0, keepdims=True) / gains_ref[0:1]
    )
    for step in range(parts):
        gi_refs[step][...] = gin_scr[pl.ds(place(me, step, parts, rows), rows), :].astype(BF16)


def attn_bwd(me, mix, gas, w1, band, segc, segr, ggain, gains, saved, heads, size):
    parts = len(gas)
    rows, d = gas[0].shape
    length, width = parts * rows, heads * size
    outs = (
        [sds((rows, d), BF16)] * parts
        + [
            sds((length, d), BF16),
            sds((length, 3 * width), BF16),
            sds((1, d), F32),
            sds((1, width), F32),
            sds((heads * CQ, 128), F32),
            sds((2 * heads, length), F32),
        ]
    )
    res = call(
        functools.partial(attn_bwd_body, (parts, rows, heads, size)),
        outs,
        [me, mix, *gas, w1, band, segc, segr, ggain, gains, *saved],
        scratch=[
            pltpu.VMEM((length, d), F32),
            pltpu.VMEM((heads * CQ, 8, 128), F32),
            pltpu.VMEM((d, width), BF16),
            pltpu.VMEM((d, 3 * width), BF16),
            pltpu.VMEM((heads * CQ, length, length), BF16),
            pltpu.VMEM((length, d), BF16),
            pltpu.VMEM((length, 3 * width), BF16),
            pltpu.VMEM((heads, length, length), BF16),
            pltpu.VMEM((heads, length, length), F32),
            pltpu.VMEM((heads, length, size), F32),
            pltpu.SemaphoreType.DMA((7 + heads,)),
        ],
        smem=2,
        far_in=[parts + 2, parts + 3, *range(parts + 8, parts + 13)],
        flops=2 * length * d * width * 4 + 2 * heads * (2 * CQ + 4) * length**3,
        name="attn_bwd",
    )
    return res[:parts], res[parts:]


def shift_mp(part, step, size):
    return lax.ppermute(part, "mp", [(i, (i + step) % size) for i in range(size)])


def gather_mp(part, size):
    if size != 4:
        return [part] + [shift_mp(part, step, size) for step in range(1, size)]
    back, ahead = shift_mp(part, 1, size), shift_mp(part, -1, size)
    return [part, back, shift_mp(back, 1, size), ahead]


def scatter_first(pieces, size):
    if size != 4:
        return [pieces[0]] + [shift_mp(pieces[step], -step, size) for step in range(1, size)], None
    far = shift_mp(pieces[2], -1, size)
    ahead = shift_mp(pieces[3], 1, size)
    return [pieces[0], ahead], (pieces[1].astype(F32) + far.astype(F32)).astype(BF16)


def scatter_second(first, size):
    here, near = first
    return here if near is None else here + [shift_mp(near, -1, size)]


def scatter_mp(pieces, size):
    return scatter_second(scatter_first(pieces, size), size)


def take(values, index, axis):
    return lax.dynamic_index_in_dim(values, index, axis, keepdims=False)


def scatter_dp(whole, extra, size):
    rows, cols = whole.shape[0] // size, whole.shape[1]
    if size != 8:
        whole = lax.psum_scatter(whole, "dp", scatter_dimension=0, tiled=True).astype(F32)
        return whole, lax.psum(extra, "dp"), whole
    me = lax.axis_index("dp")
    core, chip = me % 2, me // 2
    pieces = whole.reshape(size // 2, 2, rows, cols)
    keep, give = take(pieces, core, 1), take(pieces, 1 - core, 1)
    pairs = [(i, i ^ 1) for i in range(size)]
    keep = (keep.astype(F32) + lax.ppermute(give, "dp", pairs).astype(F32)).astype(BF16)
    extra = extra + lax.ppermute(extra, "dp", pairs)
    count = extra.shape[0]
    high = extra.astype(BF16)
    low = (extra - high.astype(F32)).astype(BF16)
    tail = jnp.concatenate([high, low])
    tail = jnp.pad(tail, (0, -tail.shape[0] % (16 * cols))).reshape(-1, cols)
    total = take(keep, chip, 0).astype(F32)
    for step in (3, 1, 2):
        send = jnp.concatenate([take(keep, chip ^ step, 0), tail])
        got = lax.ppermute(send, "dp", [(i, i ^ (2 * step)) for i in range(size)]).astype(F32)
        total = total + got[:rows]
        flat = got[rows:].reshape(-1)
        extra = extra + (flat[:count] + flat[count : 2 * count])
    return total, extra, keep


def shards(
    block_input,
    out_grad,
    doc_lengths,
    attn_gain,
    qkv_weight,
    conv_kernel,
    head_mixing,
    group_gain,
    out_weight,
    mlp_gain,
    gate_weight,
    up_weight,
    down_weight,
):
    batches = block_input.shape[0]
    rows = block_input.shape[2]
    mp, dp = lax.axis_size("mp"), lax.axis_size("dp")
    length = rows * mp
    heads = conv_kernel.shape[0]
    width = qkv_weight.shape[2]
    size = width // heads
    local_d = attn_gain.shape[0]
    me = lax.axis_index("mp").astype(jnp.int32).reshape(1)
    mix = head_mixing.reshape(-1)
    ggain = group_gain.astype(F32)[None]

    pack1 = pack_attn(qkv_weight, out_weight, attn_gain, mlp_gain)
    pack2 = jnp.concatenate([gate_weight, up_weight, down_weight.T], axis=1)
    w1 = lax.all_gather(pack1, "dp", axis=0, tiled=True)
    w2 = lax.all_gather(pack2, "dp", axis=0, tiled=True)

    offset = (
        jnp.arange(length, dtype=jnp.int32)[None, :]
        - jnp.arange(length, dtype=jnp.int32)[:, None]
        + CENTER
    )
    band = jnp.zeros((heads * CQ, length, length), F32)
    taps = conv_kernel.reshape(heads * CQ, CK)
    for b in range(CK):
        band = jnp.where(offset[None] == b, taps[:, b][:, None, None], band)
    band = band.astype(BF16)

    barrier = lambda value, *others: lax.optimization_barrier((value, others))[0]
    xs = gather_mp(block_input[:, 0], mp)
    dys = gather_mp(barrier(out_grad[:, 0], xs), mp)
    segs, front = [], []
    for batch in range(batches):
        segment = segment_ids(doc_lengths[batch, 0], length)
        segs.append((segment[:, None], segment[None, :]))
        front.append(attn_fwd(me, mix, xs, w1, band, *segs[batch], ggain, heads, size, batch))
    mids = []
    for batch in range(batches):
        pieces, saved = front[batch]
        x = barrier(block_input[batch, 0], dys)
        mids.append(mid_step(x, saved[-1], scatter_mp(pieces, mp)))
    middle = []
    for batch in range(batches):
        parts = gather_mp(mids[batch][1], mp)
        parts = barrier(parts, mids[-1])
        middle.append((mids[batch][0], *ffn(me, parts, dys, w2, batch)))

    firsts = [scatter_first(m[1], mp) for m in middle]
    rights = barrier([m[3][2] for m in middle], firsts[0])
    grads2 = ffn_grads([m[3][0] for m in middle], [m[3][1] for m in middle], rights)
    share2 = lax.psum_scatter(grads2, "dp", scatter_dimension=0, tiled=True)
    turned = []
    for batch in range(batches):
        got = barrier(scatter_second(firsts[batch], mp), grads2)
        turned.append(mid_back(middle[batch][0], out_grad[batch, 0], front[batch][1][-1], got))
    gass = [gather_mp(turned[n][1], mp) for n in range(batches)]
    back, kept, head_total = [], [], None
    for batch in range(batches):
        normed, qkv, z, probs, ho, grouped, gains = front[batch][1]
        ghid, ga, mlp_part = turned[batch]
        gas = barrier(gass[batch], turned[-1], grads2)
        gi_pieces, (ga_all, gproj, again, ggrad, kern, mixg) = attn_bwd(
            me, mix, gas, w1, band, *segs[batch], ggain, gains, [normed, qkv, z, probs, ho], heads, size
        )
        back.append((ghid, scatter_first(gi_pieces, mp)))
        small = (again, mlp_part, ggrad, kern, jnp.sum(mixg, axis=1))
        head_total = small if head_total is None else jax.tree.map(jnp.add, head_total, small)
        kept.append((normed, ga_all, gproj, grouped))

    o_parts = barrier(jnp.stack([m[2] for m in middle]), share2)
    mlp_out = lax.psum_scatter(o_parts, "mp", scatter_dimension=1, tiled=True)
    kept = barrier(kept, share2, back[0][1])
    again, mlp_part, ggrad, kern, mixg = head_total
    d = again.shape[1]
    kern = jnp.roll(kern, CK - 1 - CENTER, axis=1)[:, :CK][:, ::-1]
    gain_grads = jnp.concatenate([again, mlp_part]).reshape(-1, 128)
    gain_grads = functools.reduce(
        jnp.add, [gain_grads] + [shift_mp(gain_grads, step, mp) for step in range(1, mp)]
    )
    extra = jnp.concatenate([gain_grads.reshape(-1), ggrad[0], kern.reshape(-1), mixg])
    grads1 = attn_grads(*(list(group) for group in zip(*kept)))
    share1, extra, keep = scatter_dp(grads1, extra, dp)
    input_grads = []
    for batch in range(batches):
        ghid, first = back[batch]
        got = barrier(scatter_second(first, mp), keep)
        input_grads.append(last_step(block_input[batch, 0], ghid, front[batch][1][-1], got))
    outputs = (jnp.stack([m[0] for m in middle]) + mlp_out.astype(F32)).astype(BF16)
    share2 = share2.astype(F32)
    gain_grads = extra[: 2 * d].reshape(2, dp, local_d)
    gain_grads = take(gain_grads, lax.axis_index("dp"), 1)
    ggrad, kern, mixg = jnp.split(extra[2 * d :], [width, width + heads * CQ * CK])
    kernel_grad = kern.reshape(heads, CQ, CK)
    mixing_grad = mixg.reshape(heads // 2, 2, 2)
    ff = gate_weight.shape[1]
    return (
        outputs[:, None],
        jnp.stack(input_grads)[:, None],
        gain_grads[0],
        jnp.stack([share1[:, c * width : (c + 1) * width] for c in range(3)]),
        kernel_grad,
        mixing_grad,
        ggrad,
        share1[:, 3 * width :].T,
        gain_grads[1],
        share2[:, :ff],
        share2[:, ff : 2 * ff],
        share2[:, 2 * ff :].T,
    )


def solution(mesh):
    return jax.shard_map(
        shards,
        mesh=mesh,
        in_specs=(
            P(None, "dp", "mp", None),
            P(None, "dp", "mp", None),
            P(None, "dp", None),
            P("dp"),
            P(None, "dp", "mp"),
            P("mp", None, None),
            P("mp", None, None),
            P("mp"),
            P("mp", "dp"),
            P("dp"),
            P("dp", "mp"),
            P("dp", "mp"),
            P("mp", "dp"),
        ),
        out_specs=(
            P(None, "dp", "mp", None),
            P(None, "dp", "mp", None),
            P("dp"),
            P(None, "dp", "mp"),
            P("mp", None, None),
            P("mp", None, None),
            P("mp"),
            P("mp", "dp"),
            P("dp"),
            P("dp", "mp"),
            P("dp", "mp"),
            P("mp", "dp"),
        ),
        check_vma=False,
    )
```

```python
import functools
import math

import jax
import jax.numpy as jnp
from jax import lax
from jax.experimental import pallas as pl
from jax.experimental.pallas import tpu as pltpu
from jax.sharding import PartitionSpec as P

CQ = 6
CK = 11
CENTER = CK // 2
EPS = 1e-05
F32 = jnp.float32
BF16 = jnp.bfloat16
VMEM_LIMIT = 58 * 1024 * 1024

NN = (((1,), (0,)), ((), ()))
NT = (((1,), (1,)), ((), ()))
TN = (((0,), (0,)), ((), ()))


def mm(left, right, dims=NN):
    return lax.dot_general(left, right, dims, preferred_element_type=F32)


def spec_vmem():
    return pl.BlockSpec(memory_space=pltpu.VMEM)


def spec_smem():
    return pl.BlockSpec(memory_space=pltpu.SMEM)


def spec_any():
    return pl.BlockSpec(memory_space=pl.ANY)


def begin(sems, *pairs):
    copies = [pltpu.make_async_copy(src, dst, sems.at[n]) for n, (src, dst) in enumerate(pairs)]
    for copy in copies:
        copy.start()
    return copies


def call(body, outs, ins, scratch=(), smem=0, flops=0, name=None, far_in=(), far_out=()):
    nbytes = sum(math.prod(a.shape) * a.dtype.itemsize for a in list(ins) + list(outs))
    return pl.pallas_call(
        body,
        out_shape=outs,
        in_specs=[
            spec_smem() if n < smem else spec_any() if n in far_in else spec_vmem()
            for n in range(len(ins))
        ],
        out_specs=[spec_any() if n in far_out else spec_vmem() for n in range(len(outs))],
        scratch_shapes=list(scratch),
        compiler_params=pltpu.CompilerParams(vmem_limit_bytes=VMEM_LIMIT),
        cost_estimate=pl.CostEstimate(flops=flops, bytes_accessed=nbytes, transcendentals=0),
        name=name,
    )(*ins)


def sds(shape, dtype):
    return jax.ShapeDtypeStruct(shape, dtype)


def pack_attn_body(qkv_ref, out_ref, gains_ref, pack_ref):
    width = qkv_ref.shape[2]
    for c in range(3):
        pack_ref[:, c * width : (c + 1) * width] = qkv_ref[c]
    pack_ref[:, 3 * width : 4 * width] = out_ref[...]
    rows = qkv_ref.shape[1]
    at = lax.broadcasted_iota(jnp.int32, (128, rows), 0)
    first, second = gains_ref[0:1].astype(F32), gains_ref[1:2].astype(F32)
    gains = jnp.where(at == 0, first, jnp.where(at == 1, second, 0.0))
    pack_ref[:, 4 * width :] = gains.T.astype(BF16)


def pack_attn(qkv, out, first, second):
    _, rows, width = qkv.shape
    if rows % 16:
        gains = jnp.pad(jnp.stack([first, second], axis=1), ((0, 0), (0, 126)))
        return jnp.concatenate([qkv[0], qkv[1], qkv[2], out.T, gains], axis=1)
    return call(
        pack_attn_body,
        [sds((rows, 4 * width + 128), BF16)],
        [qkv, out.T, jnp.stack([first, second])],
        name="pack_attn",
    )[0]


def segment_ids(lengths, length):
    ends = jnp.cumsum(lengths)
    places = jnp.arange(length, dtype=jnp.int32)
    return jnp.sum((places[:, None] >= ends[None, :]).astype(jnp.int32), axis=1)


def place(me, step, parts, rows):
    return pl.multiple_of(lax.rem(me - step + parts, parts) * rows, rows)


def masks(seg_col, seg_row, length):
    same = seg_col == seg_row
    row = lax.broadcasted_iota(jnp.int32, (length, length), 0)
    col = lax.broadcasted_iota(jnp.int32, (length, length), 1)
    return same, same & (col <= row)


def shift_rows(values, shift, same):
    if shift == 0:
        return values.astype(BF16)
    length = values.shape[0]
    return jnp.where(same, pltpu.roll(values, shift % length, 0), 0.0).astype(BF16)


def head_norm(heads_out):
    centered = heads_out - jnp.mean(heads_out, axis=-1, keepdims=True)
    inv_std = lax.rsqrt(jnp.mean(centered * centered, axis=-1, keepdims=True) + EPS)
    return centered * inv_std, inv_std


def attn_fwd_body(cfg, me_ref, mix_ref, *refs):
    parts, rows, heads, size, batch = cfg
    x_refs = refs[:parts]
    w_ref, band_ref, segc_ref, segr_ref, ggain_ref = refs[parts : parts + 5]
    outs = refs[parts + 5 :]
    att_refs = outs[:parts]
    normed_ref, qkv_ref, z_ref, p_ref, ho_ref, grouped_ref, gains_ref, att_scr = outs[parts:]
    length = parts * rows
    width = heads * size
    me = me_ref[0]
    gains = w_ref[:, 4 * width :].astype(F32).T
    gains_ref[...] = gains[:8]
    gain = gains[0:1]
    for step in range(parts):
        x = x_refs[step][batch].astype(F32)
        r1 = lax.rsqrt(jnp.mean(x * x, axis=-1, keepdims=True) + EPS)
        normed_ref[pl.ds(place(me, step, parts, rows), rows), :] = (x * r1 * gain).astype(BF16)
    qkv_ref[...] = mm(normed_ref[...], w_ref[:, : 3 * width]).astype(BF16)
    same, allow = masks(segc_ref[...], segr_ref[...], length)
    scale = 1.0 / math.sqrt(size)
    for pair in range(heads // 2):
        probs = []
        for b in range(2):
            h = 2 * pair + b
            q = qkv_ref[:, h * size : (h + 1) * size]
            k = qkv_ref[:, width + h * size : width + (h + 1) * size]
            z = jnp.where(allow, mm(q, k, NT) * scale, 0.0)
            z_ref[h] = z.astype(BF16)
            acc = jnp.zeros((length, length), F32)
            for a in range(CQ):
                acc = acc + mm(shift_rows(z, a, same), band_ref[h * CQ + a])
            logits = jnp.where(allow, acc, -jnp.inf)
            e = jnp.exp(logits - jnp.max(logits, axis=-1, keepdims=True))
            p = e * (1.0 / jnp.sum(e, axis=-1, keepdims=True))
            p_ref[h] = p
            probs.append(p)
        for a in range(2):
            h = 2 * pair + a
            mixed = (
                mix_ref[4 * pair + 2 * a] * probs[0] + mix_ref[4 * pair + 2 * a + 1] * probs[1]
            ).astype(BF16)
            v = qkv_ref[:, 2 * width + h * size : 2 * width + (h + 1) * size]
            ho = mm(mixed, v)
            ho_ref[h] = ho
            normed, _ = head_norm(ho)
            grouped_ref[:, h * size : (h + 1) * size] = (
                normed * ggain_ref[:, h * size : (h + 1) * size]
            ).astype(BF16)
    att_scr[...] = mm(grouped_ref[...], w_ref[:, 3 * width : 4 * width], NT)
    for step in range(parts):
        att_refs[step][...] = att_scr[pl.ds(place(me, step, parts, rows), rows), :].astype(BF16)


def attn_fwd(me, mix, xs, w1, band, segc, segr, ggain, heads, size, batch):
    parts = len(xs)
    _, rows, d = xs[0].shape
    length, width = parts * rows, heads * size
    outs = (
        [sds((rows, d), BF16)] * parts
        + [
            sds((length, d), BF16),
            sds((length, 3 * width), BF16),
            sds((heads, length, length), BF16),
            sds((heads, length, length), F32),
            sds((heads, length, size), F32),
            sds((length, width), BF16),
            sds((8, d), F32),
        ]
    )
    res = call(
        functools.partial(attn_fwd_body, (parts, rows, heads, size, batch)),
        outs,
        [me, mix, *xs, w1, band, segc, segr, ggain],
        scratch=[pltpu.VMEM((length, d), F32)],
        smem=2,
        flops=2 * length * d * width * 4 + 2 * heads * (CQ + 2) * length**3,
        name="attn_fwd",
    )
    return res[:parts], res[parts:]


def tail_rms(values, gain):
    r = lax.rsqrt(jnp.mean(values * values, axis=-1, keepdims=True) + EPS)
    return values * r, r


def rms_back(grad, normal, r, gain):
    u = grad * gain
    return r * (u - normal * jnp.mean(u * normal, axis=-1, keepdims=True))


def total(refs):
    acc = refs[0][...].astype(F32)
    for ref in refs[1:]:
        acc = acc + ref[...].astype(F32)
    return acc


def mid_body(parts, *refs):
    x_ref, gains_ref = refs[:2]
    hid_ref, mid_ref = refs[2 + parts :]
    hidden_in = x_ref[...].astype(F32) + total(refs[2 : 2 + parts])
    hid_ref[...] = hidden_in
    normal, _ = tail_rms(hidden_in, None)
    mid_ref[...] = (normal * gains_ref[1:2]).astype(BF16)


def mid_step(x, gains, pieces):
    return call(
        functools.partial(mid_body, len(pieces)),
        [sds(x.shape, F32), sds(x.shape, BF16)],
        [x, gains, *pieces],
        name="mid_step",
    )


def mid_back_body(parts, *refs):
    hid_ref, dy_ref, gains_ref = refs[:3]
    ghid_ref, ga_ref, gain_ref = refs[3 + parts :]
    gain = gains_ref[1:2]
    normal, r = tail_rms(hid_ref[...], None)
    grad = total(refs[3 : 3 + parts])
    gain_ref[...] = jnp.sum(grad * normal, axis=0, keepdims=True)
    ghid = dy_ref[...].astype(F32) + rms_back(grad, normal, r, gain)
    ghid_ref[...] = ghid
    ga_ref[...] = ghid.astype(BF16)


def mid_back(hid, dy, gains, pieces):
    return call(
        functools.partial(mid_back_body, len(pieces)),
        [sds(hid.shape, F32), sds(hid.shape, BF16), sds((1, hid.shape[1]), F32)],
        [hid, dy, gains, *pieces],
        name="mid_back",
    )


def last_body(parts, *refs):
    x_ref, ghid_ref, gains_ref = refs[:3]
    out_ref = refs[3 + parts]
    normal, r = tail_rms(x_ref[...].astype(F32), None)
    grad = total(refs[3 : 3 + parts])
    out_ref[...] = ghid_ref[...] + rms_back(grad, normal, r, gains_ref[0:1])


def last_step(x, ghid, gains, pieces):
    return call(
        functools.partial(last_body, len(pieces)),
        [sds(x.shape, F32)],
        [x, ghid, gains, *pieces],
        name="last_step",
    )[0]


def ffn_body(parts, rows, batch, me_ref, *refs):
    m_refs, dy_hbm = refs[:parts], refs[parts : 2 * parts]
    w_hbm = refs[2 * parts]
    rest = refs[2 * parts + 1 :]
    g_refs = rest[:parts]
    o_ref, mid_ref, dy_ref, right_ref, gmid, wg_ref, wu_ref, wd_ref, sems = rest[parts:]
    me = me_ref[0]
    ff = wg_ref.shape[1]
    spots = [pl.ds(place(me, step, parts, rows), rows) for step in range(parts)]
    copies = begin(
        sems,
        (w_hbm.at[:, pl.ds(0, ff)], wg_ref),
        (w_hbm.at[:, pl.ds(ff, ff)], wu_ref),
        *[(dy_hbm[step].at[batch], dy_ref.at[spots[step]]) for step in range(parts)],
        (w_hbm.at[:, pl.ds(2 * ff, ff)], wd_ref),
    )
    for step in range(parts):
        mid_ref[spots[step], :] = m_refs[step][...]
    mid = mid_ref[...]
    cols = min(512, ff)
    copies[0].wait()
    gates = [mm(mid, wg_ref[:, c : c + cols]) for c in range(0, ff, cols)]
    copies[1].wait()
    ups = [mm(mid, wu_ref[:, c : c + cols]) for c in range(0, ff, cols)]
    for copy in copies[2:]:
        copy.wait()
    for n, (gate, up) in enumerate(zip(gates, ups)):
        at = slice(n * cols, (n + 1) * cols)
        gh = mm(dy_ref[...], wd_ref[:, at])
        sig = jax.nn.sigmoid(gate)
        swish = gate * sig
        right_ref[0, :, at] = (gh * up * sig * (1.0 + gate * (1.0 - sig))).astype(BF16)
        right_ref[1, :, at] = (gh * swish).astype(BF16)
        right_ref[2, :, at] = (swish * up).astype(BF16)
    gmid[...] = mm(right_ref[0], wg_ref[...], NT) + mm(right_ref[1], wu_ref[...], NT)
    o_ref[...] = mm(right_ref[2], wd_ref[...], NT).astype(BF16)
    for step in range(parts):
        g_refs[step][...] = gmid[spots[step], :].astype(BF16)


def ffn(me, ms, dys, w2, batch):
    parts = len(ms)
    rows, d = ms[0].shape
    length = parts * rows
    ff = w2.shape[1] // 3
    res = call(
        functools.partial(ffn_body, parts, rows, batch),
        [sds((rows, d), BF16)] * parts + [sds((length, d), BF16)] * 3 + [sds((3, length, ff), BF16)],
        [me, *ms, *dys, w2],
        scratch=[pltpu.VMEM((length, d), F32)]
        + [pltpu.VMEM((d, ff), BF16)] * 3
        + [pltpu.SemaphoreType.DMA((3 + parts,))],
        smem=1,
        far_in=range(1 + parts, 2 + 2 * parts),
        flops=2 * length * d * ff * 6,
        name="ffn",
    )
    return res[:parts], res[parts], res[parts + 1 :]


def turn(left, sources):
    length = sources[0].shape[0]
    for n, source in enumerate(sources):
        left[:, n * length : (n + 1) * length] = source[...].T


def stack(right, sources):
    length = sources[0].shape[0]
    for n, source in enumerate(sources):
        right[n * length : (n + 1) * length, :] = source


def ffn_grads_body(count, *refs):
    mids, dys, rights = refs[:count], refs[count : 2 * count], refs[2 * count : 3 * count]
    out_ref, left, right = refs[3 * count :]
    kind, j = pl.program_id(0), pl.program_id(1)
    pl.when((kind == 0) & (j == 0))(lambda: turn(left, mids))
    pl.when((kind == 2) & (j == 0))(lambda: turn(left, dys))
    stack(right, [ref[0] for ref in rights])
    out_ref[...] = mm(left[...], right[...]).astype(BF16)


def ffn_grads(mids, dys, rights):
    count = len(mids)
    length, d = mids[0].shape
    ff = rights[0].shape[2]
    cols = min(512, ff)
    steps = ff // cols
    whole = pl.BlockSpec((length, d), lambda k, j: (0, 0))
    return pl.pallas_call(
        functools.partial(ffn_grads_body, count),
        grid=(3, steps),
        in_specs=[whole] * (2 * count)
        + [pl.BlockSpec((1, length, cols), lambda k, j: (k, 0, j))] * count,
        out_specs=pl.BlockSpec((d, cols), lambda k, j: (0, k * steps + j)),
        out_shape=sds((d, 3 * ff), BF16),
        scratch_shapes=[
            pltpu.VMEM((d, count * length), BF16),
            pltpu.VMEM((count * length, cols), BF16),
        ],
        compiler_params=pltpu.CompilerParams(vmem_limit_bytes=VMEM_LIMIT),
        cost_estimate=pl.CostEstimate(
            flops=6 * count * length * d * ff, bytes_accessed=6 * d * ff, transcendentals=0
        ),
        name="ffn_grads",
    )(*mids, *dys, *rights)


def attn_grads_body(count, *refs):
    ins, gas = refs[:count], refs[count : 2 * count]
    projs, groups = refs[2 * count : 3 * count], refs[3 * count : 4 * count]
    out_ref, left, right = refs[4 * count :]
    j = pl.program_id(0)
    last = pl.num_programs(0) - 1

    @pl.when(j == 0)
    def _():
        turn(left, ins)

    @pl.when(j < last)
    def _():
        stack(right, [ref[...] for ref in projs])

    @pl.when(j == last)
    def _():
        turn(left, gas)
        stack(right, [ref[...] for ref in groups])

    out_ref[...] = mm(left[...], right[...]).astype(BF16)


def attn_grads(ins, gas, projs, groups):
    count = len(ins)
    length, d = ins[0].shape
    width = groups[0].shape[1]
    whole = pl.BlockSpec((length, d), lambda j: (0, 0))
    return pl.pallas_call(
        functools.partial(attn_grads_body, count),
        grid=(4,),
        in_specs=[whole] * (2 * count)
        + [pl.BlockSpec((length, width), lambda j: (0, jnp.minimum(j, 2)))] * count
        + [pl.BlockSpec((length, width), lambda j: (0, 0))] * count,
        out_specs=pl.BlockSpec((d, width), lambda j: (0, j)),
        out_shape=sds((d, 4 * width), BF16),
        scratch_shapes=[
            pltpu.VMEM((d, count * length), BF16),
            pltpu.VMEM((count * length, width), BF16),
        ],
        compiler_params=pltpu.CompilerParams(vmem_limit_bytes=VMEM_LIMIT),
        cost_estimate=pl.CostEstimate(
            flops=8 * count * length * d * width, bytes_accessed=8 * d * width, transcendentals=0
        ),
        name="attn_grads",
    )(*ins, *gas, *projs, *groups)


def band_sum(values, length):
    lane = lax.broadcasted_iota(jnp.int32, (8, 128), 1)
    lane = jnp.where(lane >= 64, lane - 128, lane)
    acc = jnp.zeros((8, 128), F32)
    tiles = length // 128
    for s in range(length // 8):
        back = (128 - 8 * s % 128) % 128
        low, high = 8 * s - CENTER, 8 * s + 7 + CENTER
        first, last = max(low, 0) // 128, min(high, length - 1) // 128
        for tile in range(first, last + 1):
            piece = values[8 * s : 8 * s + 8, tile * 128 : (tile + 1) * 128]
            if back:
                piece = pltpu.roll(piece, back, 1)
            start, stop = tile * 128 - 8 * s, tile * 128 + 128 - 8 * s
            if low < tile * 128 or high >= tile * 128 + 128:
                piece = jnp.where((lane >= start) & (lane < stop), piece, 0.0)
            acc = acc + piece
    return acc


def attn_bwd_body(cfg, me_ref, mix_ref, *refs):
    parts, rows, heads, size = cfg
    ga_refs = refs[:parts]
    (w_hbm, band_hbm, segc_ref, segr_ref, ggain_ref, gains_ref, normed_hbm, qkv_hbm, z_hbm,
     p_hbm, ho_hbm) = refs[parts : parts + 11]
    outs = refs[parts + 11 :]
    gi_refs = outs[:parts]
    (gaa_ref, gproj_ref, again_ref, ggrad_ref, kern_ref, mixg_ref, gin_scr, diag_scr,
     wo_ref, wq_ref, band_ref, normed_ref, qkv_ref, z_ref, p_ref, ho_ref, sems) = outs[parts:]
    length = parts * rows
    width = heads * size
    me = me_ref[0]
    copies = begin(
        sems,
        (w_hbm.at[:, pl.ds(3 * width, width)], wo_ref),
        (ho_hbm, ho_ref),
        (qkv_hbm, qkv_ref),
        (p_hbm, p_ref),
        (z_hbm, z_ref),
        *[(band_hbm.at[pl.ds(h * CQ, CQ)], band_ref.at[pl.ds(h * CQ, CQ)]) for h in range(heads)],
        (w_hbm.at[:, pl.ds(0, 3 * width)], wq_ref),
        (normed_hbm, normed_ref),
    )
    for step in range(parts):
        gaa_ref[pl.ds(place(me, step, parts, rows), rows), :] = ga_refs[step][...]
    copies[0].wait()
    gin_scr[:, :width] = mm(gaa_ref[...], wo_ref[...])
    for copy in copies[1:5]:
        copy.wait()
    same, allow = masks(segc_ref[...], segr_ref[...], length)
    scale = 1.0 / math.sqrt(size)
    for pair in range(heads // 2):
        gmix = []
        for a in range(2):
            h = 2 * pair + a
            lanes = slice(h * size, (h + 1) * size)
            gg = gin_scr[:, lanes]
            normed, inv_std = head_norm(ho_ref[h])
            ggrad_ref[:, lanes] = jnp.sum(gg * normed, axis=0, keepdims=True)
            u = gg * ggain_ref[:, lanes]
            gh = inv_std * (
                u
                - jnp.mean(u, axis=-1, keepdims=True)
                - normed * jnp.mean(u * normed, axis=-1, keepdims=True)
            )
            gh = gh.astype(BF16)
            v = qkv_ref[:, 2 * width + h * size : 2 * width + (h + 1) * size]
            gmix.append(mm(gh, v, NT))
            mixed = (
                mix_ref[4 * pair + 2 * a] * p_ref[2 * pair]
                + mix_ref[4 * pair + 2 * a + 1] * p_ref[2 * pair + 1]
            ).astype(BF16)
            gproj_ref[:, 2 * width + h * size : 2 * width + (h + 1) * size] = mm(
                mixed, gh, TN
            ).astype(BF16)
        for b in range(2):
            h = 2 * pair + b
            p = p_ref[h]
            for a in range(2):
                mixg_ref[4 * pair + 2 * a + b : 4 * pair + 2 * a + b + 1, :] = jnp.sum(
                    gmix[a] * p, axis=0, keepdims=True
                )
            gp = mix_ref[4 * pair + b] * gmix[0] + mix_ref[4 * pair + 2 + b] * gmix[1]
            gl = p * (gp - jnp.sum(gp * p, axis=-1, keepdims=True))
            glt = gl.T.astype(BF16)
            z = z_ref[h].astype(F32)
            copies[5 + h].wait()
            gz = jnp.zeros((length, length), F32)
            for a in range(CQ):
                gz = gz + mm(shift_rows(gl, -a, same), band_ref[h * CQ + a], NT)
                diag_scr[h * CQ + a] = band_sum(mm(glt, shift_rows(z, a, same)), length)
            gs = jnp.where(allow, gz, 0.0).astype(BF16)
            q = qkv_ref[:, h * size : (h + 1) * size]
            k = qkv_ref[:, width + h * size : width + (h + 1) * size]
            gproj_ref[:, h * size : (h + 1) * size] = (mm(gs, k) * scale).astype(BF16)
            gproj_ref[:, width + h * size : width + (h + 1) * size] = (
                mm(gs, q, TN) * scale
            ).astype(BF16)
    taps = diag_scr[:, 0, :]
    for r in range(1, 8):
        taps = taps + pltpu.roll(diag_scr[:, r, :], 128 - r, 1)
    kern_ref[...] = taps
    copies[-2].wait()
    gin_scr[...] = mm(gproj_ref[...], wq_ref[...], NT)
    copies[-1].wait()
    again_ref[...] = (
        jnp.sum(gin_scr[...] * normed_ref[...].astype(F32), axis=0, keepdims=True) / gains_ref[0:1]
    )
    for step in range(parts):
        gi_refs[step][...] = gin_scr[pl.ds(place(me, step, parts, rows), rows), :].astype(BF16)


def attn_bwd(me, mix, gas, w1, band, segc, segr, ggain, gains, saved, heads, size):
    parts = len(gas)
    rows, d = gas[0].shape
    length, width = parts * rows, heads * size
    outs = (
        [sds((rows, d), BF16)] * parts
        + [
            sds((length, d), BF16),
            sds((length, 3 * width), BF16),
            sds((1, d), F32),
            sds((1, width), F32),
            sds((heads * CQ, 128), F32),
            sds((2 * heads, length), F32),
        ]
    )
    res = call(
        functools.partial(attn_bwd_body, (parts, rows, heads, size)),
        outs,
        [me, mix, *gas, w1, band, segc, segr, ggain, gains, *saved],
        scratch=[
            pltpu.VMEM((length, d), F32),
            pltpu.VMEM((heads * CQ, 8, 128), F32),
            pltpu.VMEM((d, width), BF16),
            pltpu.VMEM((d, 3 * width), BF16),
            pltpu.VMEM((heads * CQ, length, length), BF16),
            pltpu.VMEM((length, d), BF16),
            pltpu.VMEM((length, 3 * width), BF16),
            pltpu.VMEM((heads, length, length), BF16),
            pltpu.VMEM((heads, length, length), F32),
            pltpu.VMEM((heads, length, size), F32),
            pltpu.SemaphoreType.DMA((7 + heads,)),
        ],
        smem=2,
        far_in=[parts + 2, parts + 3, *range(parts + 8, parts + 13)],
        flops=2 * length * d * width * 4 + 2 * heads * (2 * CQ + 4) * length**3,
        name="attn_bwd",
    )
    return res[:parts], res[parts:]


def shift_mp(part, step, size):
    return lax.ppermute(part, "mp", [(i, (i + step) % size) for i in range(size)])


def gather_mp(part, size):
    if size != 4:
        return [part] + [shift_mp(part, step, size) for step in range(1, size)]
    back, ahead = shift_mp(part, 1, size), shift_mp(part, -1, size)
    return [part, back, shift_mp(back, 1, size), ahead]


def scatter_first(pieces, size):
    if size != 4:
        return [pieces[0]] + [shift_mp(pieces[step], -step, size) for step in range(1, size)], None
    far = shift_mp(pieces[2], -1, size)
    ahead = shift_mp(pieces[3], 1, size)
    return [pieces[0], ahead], (pieces[1].astype(F32) + far.astype(F32)).astype(BF16)


def scatter_second(first, size):
    here, near = first
    return here if near is None else here + [shift_mp(near, -1, size)]


def scatter_mp(pieces, size):
    return scatter_second(scatter_first(pieces, size), size)


def take(values, index, axis):
    return lax.dynamic_index_in_dim(values, index, axis, keepdims=False)


def scatter_dp(whole, extra, size):
    rows, cols = whole.shape[0] // size, whole.shape[1]
    if size != 8:
        whole = lax.psum_scatter(whole, "dp", scatter_dimension=0, tiled=True).astype(F32)
        return whole, lax.psum(extra, "dp"), whole
    me = lax.axis_index("dp")
    core, chip = me % 2, me // 2
    pieces = whole.reshape(size // 2, 2, rows, cols)
    keep, give = take(pieces, core, 1), take(pieces, 1 - core, 1)
    pairs = [(i, i ^ 1) for i in range(size)]
    keep = (keep.astype(F32) + lax.ppermute(give, "dp", pairs).astype(F32)).astype(BF16)
    extra = extra + lax.ppermute(extra, "dp", pairs)
    count = extra.shape[0]
    high = extra.astype(BF16)
    low = (extra - high.astype(F32)).astype(BF16)
    tail = jnp.concatenate([high, low])
    tail = jnp.pad(tail, (0, -tail.shape[0] % (16 * cols))).reshape(-1, cols)
    total = take(keep, chip, 0).astype(F32)
    for step in (3, 1, 2):
        send = jnp.concatenate([take(keep, chip ^ step, 0), tail])
        got = lax.ppermute(send, "dp", [(i, i ^ (2 * step)) for i in range(size)]).astype(F32)
        total = total + got[:rows]
        flat = got[rows:].reshape(-1)
        extra = extra + (flat[:count] + flat[count : 2 * count])
    return total, extra, keep


def shards(
    block_input,
    out_grad,
    doc_lengths,
    attn_gain,
    qkv_weight,
    conv_kernel,
    head_mixing,
    group_gain,
    out_weight,
    mlp_gain,
    gate_weight,
    up_weight,
    down_weight,
):
    batches = block_input.shape[0]
    rows = block_input.shape[2]
    mp, dp = lax.axis_size("mp"), lax.axis_size("dp")
    length = rows * mp
    heads = conv_kernel.shape[0]
    width = qkv_weight.shape[2]
    size = width // heads
    local_d = attn_gain.shape[0]
    me = lax.axis_index("mp").astype(jnp.int32).reshape(1)
    mix = head_mixing.reshape(-1)
    ggain = group_gain.astype(F32)[None]

    pack1 = pack_attn(qkv_weight, out_weight, attn_gain, mlp_gain)
    pack2 = jnp.concatenate([gate_weight, up_weight, down_weight.T], axis=1)
    w1 = lax.all_gather(pack1, "dp", axis=0, tiled=True)
    w2 = lax.all_gather(pack2, "dp", axis=0, tiled=True)

    offset = (
        jnp.arange(length, dtype=jnp.int32)[None, :]
        - jnp.arange(length, dtype=jnp.int32)[:, None]
        + CENTER
    )
    band = jnp.zeros((heads * CQ, length, length), F32)
    taps = conv_kernel.reshape(heads * CQ, CK)
    for b in range(CK):
        band = jnp.where(offset[None] == b, taps[:, b][:, None, None], band)
    band = band.astype(BF16)

    barrier = lambda value, *others: lax.optimization_barrier((value, others))[0]
    xs = gather_mp(block_input[:, 0], mp)
    dys = gather_mp(barrier(out_grad[:, 0], xs), mp)
    segs, front = [], []
    for batch in range(batches):
        segment = segment_ids(doc_lengths[batch, 0], length)
        segs.append((segment[:, None], segment[None, :]))
        front.append(attn_fwd(me, mix, xs, w1, band, *segs[batch], ggain, heads, size, batch))
    mids = []
    for batch in range(batches):
        pieces, saved = front[batch]
        x = barrier(block_input[batch, 0], dys)
        mids.append(mid_step(x, saved[-1], scatter_mp(pieces, mp)))
    middle = []
    for batch in range(batches):
        parts = gather_mp(mids[batch][1], mp)
        parts = barrier(parts, mids[-1])
        middle.append((mids[batch][0], *ffn(me, parts, dys, w2, batch)))

    firsts = [scatter_first(m[1], mp) for m in middle]
    rights = barrier([m[3][2] for m in middle], firsts[0])
    grads2 = ffn_grads([m[3][0] for m in middle], [m[3][1] for m in middle], rights)
    share2 = lax.psum_scatter(grads2, "dp", scatter_dimension=0, tiled=True)
    turned = []
    for batch in range(batches):
        got = barrier(scatter_second(firsts[batch], mp), grads2)
        turned.append(mid_back(middle[batch][0], out_grad[batch, 0], front[batch][1][-1], got))
    gass = [gather_mp(turned[n][1], mp) for n in range(batches)]
    back, kept, head_total = [], [], None
    for batch in range(batches):
        normed, qkv, z, probs, ho, grouped, gains = front[batch][1]
        ghid, ga, mlp_part = turned[batch]
        gas = barrier(gass[batch], turned[-1], grads2)
        gi_pieces, (ga_all, gproj, again, ggrad, kern, mixg) = attn_bwd(
            me, mix, gas, w1, band, *segs[batch], ggain, gains, [normed, qkv, z, probs, ho], heads, size
        )
        back.append((ghid, scatter_first(gi_pieces, mp) if batch == 0 else gi_pieces))
        small = (again, mlp_part, ggrad, kern, jnp.sum(mixg, axis=1))
        head_total = small if head_total is None else jax.tree.map(jnp.add, head_total, small)
        kept.append((normed, ga_all, gproj, grouped))

    o_parts = barrier(jnp.stack([m[2] for m in middle]), share2)
    mlp_out = lax.psum_scatter(o_parts, "mp", scatter_dimension=1, tiled=True)
    kept = barrier(kept, back[0][1])
    again, mlp_part, ggrad, kern, mixg = head_total
    d = again.shape[1]
    kern = jnp.roll(kern, CK - 1 - CENTER, axis=1)[:, :CK][:, ::-1]
    gain_grads = jnp.concatenate([again, mlp_part]).reshape(-1, 128)
    gain_grads = functools.reduce(
        jnp.add, [gain_grads] + [shift_mp(gain_grads, step, mp) for step in range(1, mp)]
    )
    extra = jnp.concatenate([gain_grads.reshape(-1), ggrad[0], kern.reshape(-1), mixg])
    grads1 = attn_grads(*(list(group) for group in zip(*kept)))
    share1, extra, keep = scatter_dp(grads1, extra, dp)
    input_grads = []
    for batch in range(batches):
        ghid, first = back[batch]
        if batch:
            first = scatter_first(barrier(first, keep), mp)
        got = barrier(scatter_second(first, mp), keep)
        input_grads.append(last_step(block_input[batch, 0], ghid, front[batch][1][-1], got))
    outputs = (jnp.stack([m[0] for m in middle]) + mlp_out.astype(F32)).astype(BF16)
    share2 = share2.astype(F32)
    gain_grads = extra[: 2 * d].reshape(2, dp, local_d)
    gain_grads = take(gain_grads, lax.axis_index("dp"), 1)
    ggrad, kern, mixg = jnp.split(extra[2 * d :], [width, width + heads * CQ * CK])
    kernel_grad = kern.reshape(heads, CQ, CK)
    mixing_grad = mixg.reshape(heads // 2, 2, 2)
    ff = gate_weight.shape[1]
    return (
        outputs[:, None],
        jnp.stack(input_grads)[:, None],
        gain_grads[0],
        jnp.stack([share1[:, c * width : (c + 1) * width] for c in range(3)]),
        kernel_grad,
        mixing_grad,
        ggrad,
        share1[:, 3 * width :].T,
        gain_grads[1],
        share2[:, :ff],
        share2[:, ff : 2 * ff],
        share2[:, 2 * ff :].T,
    )


def solution(mesh):
    return jax.shard_map(
        shards,
        mesh=mesh,
        in_specs=(
            P(None, "dp", "mp", None),
            P(None, "dp", "mp", None),
            P(None, "dp", None),
            P("dp"),
            P(None, "dp", "mp"),
            P("mp", None, None),
            P("mp", None, None),
            P("mp"),
            P("mp", "dp"),
            P("dp"),
            P("dp", "mp"),
            P("dp", "mp"),
            P("mp", "dp"),
        ),
        out_specs=(
            P(None, "dp", "mp", None),
            P(None, "dp", "mp", None),
            P("dp"),
            P(None, "dp", "mp"),
            P("mp", None, None),
            P("mp", None, None),
            P("mp"),
            P("mp", "dp"),
            P("dp"),
            P("dp", "mp"),
            P("dp", "mp"),
            P("mp", "dp"),
        ),
        check_vma=False,
    )
```

```python
import functools
import math

import jax
import jax.numpy as jnp
from jax import lax
from jax.experimental import pallas as pl
from jax.experimental.pallas import tpu as pltpu
from jax.sharding import PartitionSpec as P

CQ = 6
CK = 11
CENTER = CK // 2
EPS = 1e-05
F32 = jnp.float32
BF16 = jnp.bfloat16
VMEM_LIMIT = 58 * 1024 * 1024

NN = (((1,), (0,)), ((), ()))
NT = (((1,), (1,)), ((), ()))
TN = (((0,), (0,)), ((), ()))


def mm(left, right, dims=NN):
    return lax.dot_general(left, right, dims, preferred_element_type=F32)


def spec_vmem():
    return pl.BlockSpec(memory_space=pltpu.VMEM)


def spec_smem():
    return pl.BlockSpec(memory_space=pltpu.SMEM)


def spec_any():
    return pl.BlockSpec(memory_space=pl.ANY)


def begin(sems, *pairs):
    copies = [pltpu.make_async_copy(src, dst, sems.at[n]) for n, (src, dst) in enumerate(pairs)]
    for copy in copies:
        copy.start()
    return copies


def call(body, outs, ins, scratch=(), smem=0, flops=0, name=None, far_in=(), far_out=()):
    nbytes = sum(math.prod(a.shape) * a.dtype.itemsize for a in list(ins) + list(outs))
    return pl.pallas_call(
        body,
        out_shape=outs,
        in_specs=[
            spec_smem() if n < smem else spec_any() if n in far_in else spec_vmem()
            for n in range(len(ins))
        ],
        out_specs=[spec_any() if n in far_out else spec_vmem() for n in range(len(outs))],
        scratch_shapes=list(scratch),
        compiler_params=pltpu.CompilerParams(vmem_limit_bytes=VMEM_LIMIT),
        cost_estimate=pl.CostEstimate(flops=3 * flops, bytes_accessed=nbytes, transcendentals=0),
        name=name,
    )(*ins)


def sds(shape, dtype):
    return jax.ShapeDtypeStruct(shape, dtype)


def pack_attn_body(qkv_ref, out_ref, gains_ref, pack_ref):
    width = qkv_ref.shape[2]
    for c in range(3):
        pack_ref[:, c * width : (c + 1) * width] = qkv_ref[c]
    pack_ref[:, 3 * width : 4 * width] = out_ref[...]
    rows = qkv_ref.shape[1]
    at = lax.broadcasted_iota(jnp.int32, (128, rows), 0)
    first, second = gains_ref[0:1].astype(F32), gains_ref[1:2].astype(F32)
    gains = jnp.where(at == 0, first, jnp.where(at == 1, second, 0.0))
    pack_ref[:, 4 * width :] = gains.T.astype(BF16)


def pack_attn(qkv, out, first, second):
    _, rows, width = qkv.shape
    if rows % 16:
        gains = jnp.pad(jnp.stack([first, second], axis=1), ((0, 0), (0, 126)))
        return jnp.concatenate([qkv[0], qkv[1], qkv[2], out.T, gains], axis=1)
    return call(
        pack_attn_body,
        [sds((rows, 4 * width + 128), BF16)],
        [qkv, out.T, jnp.stack([first, second])],
        name="pack_attn",
    )[0]


def segment_ids(lengths, length):
    ends = jnp.cumsum(lengths)
    places = jnp.arange(length, dtype=jnp.int32)
    return jnp.sum((places[:, None] >= ends[None, :]).astype(jnp.int32), axis=1)


def place(me, step, parts, rows):
    return pl.multiple_of(lax.rem(me - step + parts, parts) * rows, rows)


def masks(seg_col, seg_row, length):
    same = seg_col == seg_row
    row = lax.broadcasted_iota(jnp.int32, (length, length), 0)
    col = lax.broadcasted_iota(jnp.int32, (length, length), 1)
    return same, same & (col <= row)


def shift_rows(values, shift, same):
    if shift == 0:
        return values.astype(BF16)
    length = values.shape[0]
    return jnp.where(same, pltpu.roll(values, shift % length, 0), 0.0).astype(BF16)


def head_norm(heads_out):
    centered = heads_out - jnp.mean(heads_out, axis=-1, keepdims=True)
    inv_std = lax.rsqrt(jnp.mean(centered * centered, axis=-1, keepdims=True) + EPS)
    return centered * inv_std, inv_std


def attn_fwd_body(cfg, me_ref, mix_ref, *refs):
    parts, rows, heads, size, batch = cfg
    x_refs = refs[:parts]
    w_ref, band_ref, segc_ref, segr_ref, ggain_ref = refs[parts : parts + 5]
    outs = refs[parts + 5 :]
    att_refs = outs[:parts]
    normed_ref, qkv_ref, z_ref, p_ref, ho_ref, grouped_ref, gains_ref, att_scr = outs[parts:]
    length = parts * rows
    width = heads * size
    me = me_ref[0]
    gains = w_ref[:, 4 * width :].astype(F32).T
    gains_ref[...] = gains[:8]
    gain = gains[0:1]
    for step in range(parts):
        x = x_refs[step][batch].astype(F32)
        r1 = lax.rsqrt(jnp.mean(x * x, axis=-1, keepdims=True) + EPS)
        normed_ref[pl.ds(place(me, step, parts, rows), rows), :] = (x * r1 * gain).astype(BF16)
    qkv_ref[...] = mm(normed_ref[...], w_ref[:, : 3 * width]).astype(BF16)
    same, allow = masks(segc_ref[...], segr_ref[...], length)
    scale = 1.0 / math.sqrt(size)
    for pair in range(heads // 2):
        probs = []
        for b in range(2):
            h = 2 * pair + b
            q = qkv_ref[:, h * size : (h + 1) * size]
            k = qkv_ref[:, width + h * size : width + (h + 1) * size]
            z = jnp.where(allow, mm(q, k, NT) * scale, 0.0)
            z_ref[h] = z.astype(BF16)
            acc = jnp.zeros((length, length), F32)
            for a in range(CQ):
                acc = acc + mm(shift_rows(z, a, same), band_ref[h * CQ + a])
            logits = jnp.where(allow, acc, -jnp.inf)
            e = jnp.exp(logits - jnp.max(logits, axis=-1, keepdims=True))
            p = e * (1.0 / jnp.sum(e, axis=-1, keepdims=True))
            p_ref[h] = p
            probs.append(p)
        for a in range(2):
            h = 2 * pair + a
            mixed = (
                mix_ref[4 * pair + 2 * a] * probs[0] + mix_ref[4 * pair + 2 * a + 1] * probs[1]
            ).astype(BF16)
            v = qkv_ref[:, 2 * width + h * size : 2 * width + (h + 1) * size]
            ho = mm(mixed, v)
            ho_ref[h] = ho
            normed, _ = head_norm(ho)
            grouped_ref[:, h * size : (h + 1) * size] = (
                normed * ggain_ref[:, h * size : (h + 1) * size]
            ).astype(BF16)
    att_scr[...] = mm(grouped_ref[...], w_ref[:, 3 * width : 4 * width], NT)
    for step in range(parts):
        att_refs[step][...] = att_scr[pl.ds(place(me, step, parts, rows), rows), :].astype(BF16)


def attn_fwd(me, mix, xs, w1, band, segc, segr, ggain, heads, size, batch):
    parts = len(xs)
    _, rows, d = xs[0].shape
    length, width = parts * rows, heads * size
    outs = (
        [sds((rows, d), BF16)] * parts
        + [
            sds((length, d), BF16),
            sds((length, 3 * width), BF16),
            sds((heads, length, length), BF16),
            sds((heads, length, length), F32),
            sds((heads, length, size), F32),
            sds((length, width), BF16),
            sds((8, d), F32),
        ]
    )
    res = call(
        functools.partial(attn_fwd_body, (parts, rows, heads, size, batch)),
        outs,
        [me, mix, *xs, w1, band, segc, segr, ggain],
        scratch=[pltpu.VMEM((length, d), F32)],
        smem=2,
        flops=2 * length * d * width * 4 + 2 * heads * (CQ + 2) * length**3,
        name="attn_fwd",
    )
    return res[:parts], res[parts:]


def tail_rms(values, gain):
    r = lax.rsqrt(jnp.mean(values * values, axis=-1, keepdims=True) + EPS)
    return values * r, r


def rms_back(grad, normal, r, gain):
    u = grad * gain
    return r * (u - normal * jnp.mean(u * normal, axis=-1, keepdims=True))


def total(refs):
    acc = refs[0][...].astype(F32)
    for ref in refs[1:]:
        acc = acc + ref[...].astype(F32)
    return acc


def mid_body(parts, *refs):
    x_ref, gains_ref = refs[:2]
    hid_ref, mid_ref = refs[2 + parts :]
    hidden_in = x_ref[...].astype(F32) + total(refs[2 : 2 + parts])
    hid_ref[...] = hidden_in
    normal, _ = tail_rms(hidden_in, None)
    mid_ref[...] = (normal * gains_ref[1:2]).astype(BF16)


def mid_step(x, gains, pieces):
    return call(
        functools.partial(mid_body, len(pieces)),
        [sds(x.shape, F32), sds(x.shape, BF16)],
        [x, gains, *pieces],
        name="mid_step",
    )


def mid_back_body(parts, *refs):
    hid_ref, dy_ref, gains_ref = refs[:3]
    ghid_ref, ga_ref, gain_ref = refs[3 + parts :]
    gain = gains_ref[1:2]
    normal, r = tail_rms(hid_ref[...], None)
    grad = total(refs[3 : 3 + parts])
    gain_ref[...] = jnp.sum(grad * normal, axis=0, keepdims=True)
    ghid = dy_ref[...].astype(F32) + rms_back(grad, normal, r, gain)
    ghid_ref[...] = ghid
    ga_ref[...] = ghid.astype(BF16)


def mid_back(hid, dy, gains, pieces):
    return call(
        functools.partial(mid_back_body, len(pieces)),
        [sds(hid.shape, F32), sds(hid.shape, BF16), sds((1, hid.shape[1]), F32)],
        [hid, dy, gains, *pieces],
        name="mid_back",
    )


def last_body(parts, *refs):
    x_ref, ghid_ref, gains_ref = refs[:3]
    out_ref = refs[3 + parts]
    normal, r = tail_rms(x_ref[...].astype(F32), None)
    grad = total(refs[3 : 3 + parts])
    out_ref[...] = ghid_ref[...] + rms_back(grad, normal, r, gains_ref[0:1])


def last_step(x, ghid, gains, pieces):
    return call(
        functools.partial(last_body, len(pieces)),
        [sds(x.shape, F32)],
        [x, ghid, gains, *pieces],
        name="last_step",
    )[0]


def ffn_body(parts, rows, batch, me_ref, *refs):
    m_refs, dy_hbm = refs[:parts], refs[parts : 2 * parts]
    w_hbm = refs[2 * parts]
    rest = refs[2 * parts + 1 :]
    g_refs = rest[:parts]
    o_ref, mid_ref, dy_ref, right_ref, gmid, wg_ref, wu_ref, wd_ref, sems = rest[parts:]
    me = me_ref[0]
    ff = wg_ref.shape[1]
    spots = [pl.ds(place(me, step, parts, rows), rows) for step in range(parts)]
    copies = begin(
        sems,
        (w_hbm.at[:, pl.ds(0, ff)], wg_ref),
        (w_hbm.at[:, pl.ds(ff, ff)], wu_ref),
        *[(dy_hbm[step].at[batch], dy_ref.at[spots[step]]) for step in range(parts)],
        (w_hbm.at[:, pl.ds(2 * ff, ff)], wd_ref),
    )
    for step in range(parts):
        mid_ref[spots[step], :] = m_refs[step][...]
    mid = mid_ref[...]
    cols = min(512, ff)
    copies[0].wait()
    gates = [mm(mid, wg_ref[:, c : c + cols]) for c in range(0, ff, cols)]
    copies[1].wait()
    ups = [mm(mid, wu_ref[:, c : c + cols]) for c in range(0, ff, cols)]
    for copy in copies[2:]:
        copy.wait()
    for n, (gate, up) in enumerate(zip(gates, ups)):
        at = slice(n * cols, (n + 1) * cols)
        gh = mm(dy_ref[...], wd_ref[:, at])
        sig = jax.nn.sigmoid(gate)
        swish = gate * sig
        right_ref[0, :, at] = (gh * up * sig * (1.0 + gate * (1.0 - sig))).astype(BF16)
        right_ref[1, :, at] = (gh * swish).astype(BF16)
        right_ref[2, :, at] = (swish * up).astype(BF16)
    gmid[...] = mm(right_ref[0], wg_ref[...], NT) + mm(right_ref[1], wu_ref[...], NT)
    o_ref[...] = mm(right_ref[2], wd_ref[...], NT).astype(BF16)
    for step in range(parts):
        g_refs[step][...] = gmid[spots[step], :].astype(BF16)


def ffn(me, ms, dys, w2, batch):
    parts = len(ms)
    rows, d = ms[0].shape
    length = parts * rows
    ff = w2.shape[1] // 3
    res = call(
        functools.partial(ffn_body, parts, rows, batch),
        [sds((rows, d), BF16)] * parts + [sds((length, d), BF16)] * 3 + [sds((3, length, ff), BF16)],
        [me, *ms, *dys, w2],
        scratch=[pltpu.VMEM((length, d), F32)]
        + [pltpu.VMEM((d, ff), BF16)] * 3
        + [pltpu.SemaphoreType.DMA((3 + parts,))],
        smem=1,
        far_in=range(1 + parts, 2 + 2 * parts),
        flops=2 * length * d * ff * 6,
        name="ffn",
    )
    return res[:parts], res[parts], res[parts + 1 :]


def turn(left, sources):
    length = sources[0].shape[0]
    for n, source in enumerate(sources):
        left[:, n * length : (n + 1) * length] = source[...].T


def stack(right, sources):
    length = sources[0].shape[0]
    for n, source in enumerate(sources):
        right[n * length : (n + 1) * length, :] = source


def ffn_grads_body(count, *refs):
    mids, dys, rights = refs[:count], refs[count : 2 * count], refs[2 * count : 3 * count]
    out_ref, left, right = refs[3 * count :]
    kind, j = pl.program_id(0), pl.program_id(1)
    pl.when((kind == 0) & (j == 0))(lambda: turn(left, mids))
    pl.when((kind == 2) & (j == 0))(lambda: turn(left, dys))
    stack(right, [ref[0] for ref in rights])
    out_ref[...] = mm(left[...], right[...]).astype(BF16)


def ffn_grads(mids, dys, rights):
    count = len(mids)
    length, d = mids[0].shape
    ff = rights[0].shape[2]
    cols = min(512, ff)
    steps = ff // cols
    whole = pl.BlockSpec((length, d), lambda k, j: (0, 0))
    return pl.pallas_call(
        functools.partial(ffn_grads_body, count),
        grid=(3, steps),
        in_specs=[whole] * (2 * count)
        + [pl.BlockSpec((1, length, cols), lambda k, j: (k, 0, j))] * count,
        out_specs=pl.BlockSpec((d, cols), lambda k, j: (0, k * steps + j)),
        out_shape=sds((d, 3 * ff), BF16),
        scratch_shapes=[
            pltpu.VMEM((d, count * length), BF16),
            pltpu.VMEM((count * length, cols), BF16),
        ],
        compiler_params=pltpu.CompilerParams(vmem_limit_bytes=VMEM_LIMIT),
        cost_estimate=pl.CostEstimate(
            flops=6 * count * length * d * ff, bytes_accessed=6 * d * ff, transcendentals=0
        ),
        name="ffn_grads",
    )(*mids, *dys, *rights)


def attn_grads_body(count, *refs):
    ins, gas = refs[:count], refs[count : 2 * count]
    projs, groups = refs[2 * count : 3 * count], refs[3 * count : 4 * count]
    out_ref, left, right = refs[4 * count :]
    j = pl.program_id(0)
    last = pl.num_programs(0) - 1

    @pl.when(j == 0)
    def _():
        turn(left, ins)

    @pl.when(j < last)
    def _():
        stack(right, [ref[...] for ref in projs])

    @pl.when(j == last)
    def _():
        turn(left, gas)
        stack(right, [ref[...] for ref in groups])

    out_ref[...] = mm(left[...], right[...]).astype(BF16)


def attn_grads(ins, gas, projs, groups):
    count = len(ins)
    length, d = ins[0].shape
    width = groups[0].shape[1]
    whole = pl.BlockSpec((length, d), lambda j: (0, 0))
    return pl.pallas_call(
        functools.partial(attn_grads_body, count),
        grid=(4,),
        in_specs=[whole] * (2 * count)
        + [pl.BlockSpec((length, width), lambda j: (0, jnp.minimum(j, 2)))] * count
        + [pl.BlockSpec((length, width), lambda j: (0, 0))] * count,
        out_specs=pl.BlockSpec((d, width), lambda j: (0, j)),
        out_shape=sds((d, 4 * width), BF16),
        scratch_shapes=[
            pltpu.VMEM((d, count * length), BF16),
            pltpu.VMEM((count * length, width), BF16),
        ],
        compiler_params=pltpu.CompilerParams(vmem_limit_bytes=VMEM_LIMIT),
        cost_estimate=pl.CostEstimate(
            flops=8 * count * length * d * width, bytes_accessed=8 * d * width, transcendentals=0
        ),
        name="attn_grads",
    )(*ins, *gas, *projs, *groups)


def band_sum(values, length):
    lane = lax.broadcasted_iota(jnp.int32, (8, 128), 1)
    lane = jnp.where(lane >= 64, lane - 128, lane)
    acc = jnp.zeros((8, 128), F32)
    tiles = length // 128
    for s in range(length // 8):
        back = (128 - 8 * s % 128) % 128
        low, high = 8 * s - CENTER, 8 * s + 7 + CENTER
        first, last = max(low, 0) // 128, min(high, length - 1) // 128
        for tile in range(first, last + 1):
            piece = values[8 * s : 8 * s + 8, tile * 128 : (tile + 1) * 128]
            if back:
                piece = pltpu.roll(piece, back, 1)
            start, stop = tile * 128 - 8 * s, tile * 128 + 128 - 8 * s
            if low < tile * 128 or high >= tile * 128 + 128:
                piece = jnp.where((lane >= start) & (lane < stop), piece, 0.0)
            acc = acc + piece
    return acc


def attn_bwd_body(cfg, me_ref, mix_ref, *refs):
    parts, rows, heads, size = cfg
    ga_refs = refs[:parts]
    (w_hbm, band_hbm, segc_ref, segr_ref, ggain_ref, gains_ref, normed_hbm, qkv_hbm, z_hbm,
     p_hbm, ho_hbm) = refs[parts : parts + 11]
    outs = refs[parts + 11 :]
    gi_refs = outs[:parts]
    (gaa_ref, gproj_ref, again_ref, ggrad_ref, kern_ref, mixg_ref, gin_scr, diag_scr,
     wo_ref, wq_ref, band_ref, normed_ref, qkv_ref, z_ref, p_ref, ho_ref, sems) = outs[parts:]
    length = parts * rows
    width = heads * size
    me = me_ref[0]
    copies = begin(
        sems,
        (w_hbm.at[:, pl.ds(3 * width, width)], wo_ref),
        (ho_hbm, ho_ref),
        (qkv_hbm, qkv_ref),
        (p_hbm, p_ref),
        (z_hbm, z_ref),
        *[(band_hbm.at[pl.ds(h * CQ, CQ)], band_ref.at[pl.ds(h * CQ, CQ)]) for h in range(heads)],
        (w_hbm.at[:, pl.ds(0, 3 * width)], wq_ref),
        (normed_hbm, normed_ref),
    )
    for step in range(parts):
        gaa_ref[pl.ds(place(me, step, parts, rows), rows), :] = ga_refs[step][...]
    copies[0].wait()
    gin_scr[:, :width] = mm(gaa_ref[...], wo_ref[...])
    for copy in copies[1:5]:
        copy.wait()
    same, allow = masks(segc_ref[...], segr_ref[...], length)
    scale = 1.0 / math.sqrt(size)
    for pair in range(heads // 2):
        gmix = []
        for a in range(2):
            h = 2 * pair + a
            lanes = slice(h * size, (h + 1) * size)
            gg = gin_scr[:, lanes]
            normed, inv_std = head_norm(ho_ref[h])
            ggrad_ref[:, lanes] = jnp.sum(gg * normed, axis=0, keepdims=True)
            u = gg * ggain_ref[:, lanes]
            gh = inv_std * (
                u
                - jnp.mean(u, axis=-1, keepdims=True)
                - normed * jnp.mean(u * normed, axis=-1, keepdims=True)
            )
            gh = gh.astype(BF16)
            v = qkv_ref[:, 2 * width + h * size : 2 * width + (h + 1) * size]
            gmix.append(mm(gh, v, NT))
            mixed = (
                mix_ref[4 * pair + 2 * a] * p_ref[2 * pair]
                + mix_ref[4 * pair + 2 * a + 1] * p_ref[2 * pair + 1]
            ).astype(BF16)
            gproj_ref[:, 2 * width + h * size : 2 * width + (h + 1) * size] = mm(
                mixed, gh, TN
            ).astype(BF16)
        for b in range(2):
            h = 2 * pair + b
            p = p_ref[h]
            for a in range(2):
                mixg_ref[4 * pair + 2 * a + b : 4 * pair + 2 * a + b + 1, :] = jnp.sum(
                    gmix[a] * p, axis=0, keepdims=True
                )
            gp = mix_ref[4 * pair + b] * gmix[0] + mix_ref[4 * pair + 2 + b] * gmix[1]
            gl = p * (gp - jnp.sum(gp * p, axis=-1, keepdims=True))
            glt = gl.T.astype(BF16)
            z = z_ref[h].astype(F32)
            copies[5 + h].wait()
            gz = jnp.zeros((length, length), F32)
            for a in range(CQ):
                gz = gz + mm(shift_rows(gl, -a, same), band_ref[h * CQ + a], NT)
                diag_scr[h * CQ + a] = band_sum(mm(glt, shift_rows(z, a, same)), length)
            gs = jnp.where(allow, gz, 0.0).astype(BF16)
            q = qkv_ref[:, h * size : (h + 1) * size]
            k = qkv_ref[:, width + h * size : width + (h + 1) * size]
            gproj_ref[:, h * size : (h + 1) * size] = (mm(gs, k) * scale).astype(BF16)
            gproj_ref[:, width + h * size : width + (h + 1) * size] = (
                mm(gs, q, TN) * scale
            ).astype(BF16)
    taps = diag_scr[:, 0, :]
    for r in range(1, 8):
        taps = taps + pltpu.roll(diag_scr[:, r, :], 128 - r, 1)
    kern_ref[...] = taps
    copies[-2].wait()
    gin_scr[...] = mm(gproj_ref[...], wq_ref[...], NT)
    copies[-1].wait()
    again_ref[...] = (
        jnp.sum(gin_scr[...] * normed_ref[...].astype(F32), axis=0, keepdims=True) / gains_ref[0:1]
    )
    for step in range(parts):
        gi_refs[step][...] = gin_scr[pl.ds(place(me, step, parts, rows), rows), :].astype(BF16)


def attn_bwd(me, mix, gas, w1, band, segc, segr, ggain, gains, saved, heads, size):
    parts = len(gas)
    rows, d = gas[0].shape
    length, width = parts * rows, heads * size
    outs = (
        [sds((rows, d), BF16)] * parts
        + [
            sds((length, d), BF16),
            sds((length, 3 * width), BF16),
            sds((1, d), F32),
            sds((1, width), F32),
            sds((heads * CQ, 128), F32),
            sds((2 * heads, length), F32),
        ]
    )
    res = call(
        functools.partial(attn_bwd_body, (parts, rows, heads, size)),
        outs,
        [me, mix, *gas, w1, band, segc, segr, ggain, gains, *saved],
        scratch=[
            pltpu.VMEM((length, d), F32),
            pltpu.VMEM((heads * CQ, 8, 128), F32),
            pltpu.VMEM((d, width), BF16),
            pltpu.VMEM((d, 3 * width), BF16),
            pltpu.VMEM((heads * CQ, length, length), BF16),
            pltpu.VMEM((length, d), BF16),
            pltpu.VMEM((length, 3 * width), BF16),
            pltpu.VMEM((heads, length, length), BF16),
            pltpu.VMEM((heads, length, length), F32),
            pltpu.VMEM((heads, length, size), F32),
            pltpu.SemaphoreType.DMA((7 + heads,)),
        ],
        smem=2,
        far_in=[parts + 2, parts + 3, *range(parts + 8, parts + 13)],
        flops=2 * length * d * width * 4 + 2 * heads * (2 * CQ + 4) * length**3,
        name="attn_bwd",
    )
    return res[:parts], res[parts:]


def shift_mp(part, step, size):
    return lax.ppermute(part, "mp", [(i, (i + step) % size) for i in range(size)])


def gather_mp(part, size):
    if size != 4:
        return [part] + [shift_mp(part, step, size) for step in range(1, size)]
    back, ahead = shift_mp(part, 1, size), shift_mp(part, -1, size)
    return [part, back, shift_mp(back, 1, size), ahead]


def scatter_first(pieces, size):
    if size != 4:
        return [pieces[0]] + [shift_mp(pieces[step], -step, size) for step in range(1, size)], None
    far = shift_mp(pieces[2], -1, size)
    ahead = shift_mp(pieces[3], 1, size)
    return [pieces[0], ahead], (pieces[1].astype(F32) + far.astype(F32)).astype(BF16)


def scatter_second(first, size):
    here, near = first
    return here if near is None else here + [shift_mp(near, -1, size)]


def scatter_mp(pieces, size):
    return scatter_second(scatter_first(pieces, size), size)


def take(values, index, axis):
    return lax.dynamic_index_in_dim(values, index, axis, keepdims=False)


def scatter_dp(whole, extra, size):
    rows, cols = whole.shape[0] // size, whole.shape[1]
    if size != 8:
        whole = lax.psum_scatter(whole, "dp", scatter_dimension=0, tiled=True).astype(F32)
        return whole, lax.psum(extra, "dp"), whole
    me = lax.axis_index("dp")
    core, chip = me % 2, me // 2
    pieces = whole.reshape(size // 2, 2, rows, cols)
    keep, give = take(pieces, core, 1), take(pieces, 1 - core, 1)
    pairs = [(i, i ^ 1) for i in range(size)]
    keep = (keep.astype(F32) + lax.ppermute(give, "dp", pairs).astype(F32)).astype(BF16)
    extra = extra + lax.ppermute(extra, "dp", pairs)
    count = extra.shape[0]
    high = extra.astype(BF16)
    low = (extra - high.astype(F32)).astype(BF16)
    tail = jnp.concatenate([high, low])
    tail = jnp.pad(tail, (0, -tail.shape[0] % (16 * cols))).reshape(-1, cols)
    total = take(keep, chip, 0).astype(F32)
    for step in (3, 1, 2):
        send = jnp.concatenate([take(keep, chip ^ step, 0), tail])
        got = lax.ppermute(send, "dp", [(i, i ^ (2 * step)) for i in range(size)]).astype(F32)
        total = total + got[:rows]
        flat = got[rows:].reshape(-1)
        extra = extra + (flat[:count] + flat[count : 2 * count])
    return total, extra, keep


def shards(
    block_input,
    out_grad,
    doc_lengths,
    attn_gain,
    qkv_weight,
    conv_kernel,
    head_mixing,
    group_gain,
    out_weight,
    mlp_gain,
    gate_weight,
    up_weight,
    down_weight,
):
    batches = block_input.shape[0]
    rows = block_input.shape[2]
    mp, dp = lax.axis_size("mp"), lax.axis_size("dp")
    length = rows * mp
    heads = conv_kernel.shape[0]
    width = qkv_weight.shape[2]
    size = width // heads
    local_d = attn_gain.shape[0]
    me = lax.axis_index("mp").astype(jnp.int32).reshape(1)
    mix = head_mixing.reshape(-1)
    ggain = group_gain.astype(F32)[None]

    pack1 = pack_attn(qkv_weight, out_weight, attn_gain, mlp_gain)
    pack2 = jnp.concatenate([gate_weight, up_weight, down_weight.T], axis=1)
    w1 = lax.all_gather(pack1, "dp", axis=0, tiled=True)
    w2 = lax.all_gather(pack2, "dp", axis=0, tiled=True)

    offset = (
        jnp.arange(length, dtype=jnp.int32)[None, :]
        - jnp.arange(length, dtype=jnp.int32)[:, None]
        + CENTER
    )
    band = jnp.zeros((heads * CQ, length, length), F32)
    taps = conv_kernel.reshape(heads * CQ, CK)
    for b in range(CK):
        band = jnp.where(offset[None] == b, taps[:, b][:, None, None], band)
    band = band.astype(BF16)

    barrier = lambda value, *others: lax.optimization_barrier((value, others))[0]
    xs = gather_mp(block_input[:, 0], mp)
    dys = gather_mp(barrier(out_grad[:, 0], xs), mp)
    segs, front = [], []
    for batch in range(batches):
        segment = segment_ids(doc_lengths[batch, 0], length)
        segs.append((segment[:, None], segment[None, :]))
        front.append(attn_fwd(me, mix, xs, w1, band, *segs[batch], ggain, heads, size, batch))
    mids = []
    for batch in range(batches):
        pieces, saved = front[batch]
        x = barrier(block_input[batch, 0], dys)
        mids.append(mid_step(x, saved[-1], scatter_mp(pieces, mp)))
    middle = []
    for batch in range(batches):
        parts = gather_mp(mids[batch][1], mp)
        parts = barrier(parts, mids[-1])
        middle.append((mids[batch][0], *ffn(me, parts, dys, w2, batch)))

    firsts = [scatter_first(m[1], mp) for m in middle]
    rights = barrier([m[3][2] for m in middle], firsts[0])
    grads2 = ffn_grads([m[3][0] for m in middle], [m[3][1] for m in middle], rights)
    share2 = lax.psum_scatter(grads2, "dp", scatter_dimension=0, tiled=True)
    turned = []
    for batch in range(batches):
        got = barrier(scatter_second(firsts[batch], mp), grads2)
        turned.append(mid_back(middle[batch][0], out_grad[batch, 0], front[batch][1][-1], got))
    gass = [gather_mp(turned[n][1], mp) for n in range(batches)]
    back, kept, head_total = [], [], None
    for batch in range(batches):
        normed, qkv, z, probs, ho, grouped, gains = front[batch][1]
        ghid, ga, mlp_part = turned[batch]
        gas = barrier(gass[batch], turned[-1], grads2)
        gi_pieces, (ga_all, gproj, again, ggrad, kern, mixg) = attn_bwd(
            me, mix, gas, w1, band, *segs[batch], ggain, gains, [normed, qkv, z, probs, ho], heads, size
        )
        back.append((ghid, scatter_first(gi_pieces, mp) if batch == 0 else gi_pieces))
        small = (again, mlp_part, ggrad, kern, jnp.sum(mixg, axis=1))
        head_total = small if head_total is None else jax.tree.map(jnp.add, head_total, small)
        kept.append((normed, ga_all, gproj, grouped))

    o_parts = barrier(jnp.stack([m[2] for m in middle]), share2)
    mlp_out = lax.psum_scatter(o_parts, "mp", scatter_dimension=1, tiled=True)
    kept = barrier(kept, back[0][1])
    again, mlp_part, ggrad, kern, mixg = head_total
    d = again.shape[1]
    kern = jnp.roll(kern, CK - 1 - CENTER, axis=1)[:, :CK][:, ::-1]
    gain_grads = jnp.concatenate([again, mlp_part]).reshape(-1, 128)
    gain_grads = functools.reduce(
        jnp.add, [gain_grads] + [shift_mp(gain_grads, step, mp) for step in range(1, mp)]
    )
    extra = jnp.concatenate([gain_grads.reshape(-1), ggrad[0], kern.reshape(-1), mixg])
    grads1 = attn_grads(*(list(group) for group in zip(*kept)))
    share1, extra, keep = scatter_dp(grads1, extra, dp)
    input_grads = []
    for batch in range(batches):
        ghid, first = back[batch]
        if batch:
            first = scatter_first(barrier(first, keep), mp)
        got = barrier(scatter_second(first, mp), keep)
        input_grads.append(last_step(block_input[batch, 0], ghid, front[batch][1][-1], got))
    outputs = (jnp.stack([m[0] for m in middle]) + mlp_out.astype(F32)).astype(BF16)
    share2 = share2.astype(F32)
    gain_grads = extra[: 2 * d].reshape(2, dp, local_d)
    gain_grads = take(gain_grads, lax.axis_index("dp"), 1)
    ggrad, kern, mixg = jnp.split(extra[2 * d :], [width, width + heads * CQ * CK])
    kernel_grad = kern.reshape(heads, CQ, CK)
    mixing_grad = mixg.reshape(heads // 2, 2, 2)
    ff = gate_weight.shape[1]
    return (
        outputs[:, None],
        jnp.stack(input_grads)[:, None],
        gain_grads[0],
        jnp.stack([share1[:, c * width : (c + 1) * width] for c in range(3)]),
        kernel_grad,
        mixing_grad,
        ggrad,
        share1[:, 3 * width :].T,
        gain_grads[1],
        share2[:, :ff],
        share2[:, ff : 2 * ff],
        share2[:, 2 * ff :].T,
    )


def solution(mesh):
    return jax.shard_map(
        shards,
        mesh=mesh,
        in_specs=(
            P(None, "dp", "mp", None),
            P(None, "dp", "mp", None),
            P(None, "dp", None),
            P("dp"),
            P(None, "dp", "mp"),
            P("mp", None, None),
            P("mp", None, None),
            P("mp"),
            P("mp", "dp"),
            P("dp"),
            P("dp", "mp"),
            P("dp", "mp"),
            P("mp", "dp"),
        ),
        out_specs=(
            P(None, "dp", "mp", None),
            P(None, "dp", "mp", None),
            P("dp"),
            P(None, "dp", "mp"),
            P("mp", None, None),
            P("mp", None, None),
            P("mp"),
            P("mp", "dp"),
            P("dp"),
            P("dp", "mp"),
            P("dp", "mp"),
            P("mp", "dp"),
        ),
        check_vma=False,
    )
```
